128 devices in a mesh: dp: 16 (over z, y), seq: 8 (over x, core).
Axes of the slice: x: 4, y: 4, z: 4, core: 2. Of those that a mesh axis runs over, the one named last changes fastest.
Arguments:
- tokens: bfloat16 [16, 1024, 1024], P('dp', 'seq'), may hold values from -6 to 6
- counts: int32 [16, 8], P('dp'), may hold values from 1 to 128, 577 in all within a row
- cotangent: bfloat16 [16, 1024, 1024], P('dp', 'seq'), may hold values from -6 to 6
- w_qkv: bfloat16 [2, 1024, 3072], P(None, 'dp'), may hold values from -0.1875 to 0.1875
- w_out: bfloat16 [2, 1024, 1024], P(None, 'dp'), may hold values from -0.75 to 0.75
- w_up: bfloat16 [2, 1024, 4096], P(None, 'dp'), may hold values from -0.1875 to 0.1875
- w_down: bfloat16 [2, 4096, 1024], P(None, 'dp'), may hold values from -0.09375 to 0.09375
- norm_gain: bfloat16 [2, 2, 1024], P(None, None, 'dp'), may hold values from 0.5 to 1.5
- norm_shift: bfloat16 [2, 2, 1024], P(None, None, 'dp'), may hold values from -1.75 to 1.75
- bias_qv: bfloat16 [2, 2048], P(None, 'dp'), may hold values from -1.25 to 1.25
- bias_up: bfloat16 [2, 4096], P(None, 'dp'), may hold values from -3 to 3
- bias_branch: bfloat16 [2, 2, 1024], P(None, None, 'dp'), may hold values from -1.75 to 1.75
Outputs:
- output: bfloat16 [16, 1024, 1024], P('dp', 'seq')
- grad_tokens: bfloat16 [16, 1024, 1024], P('dp', 'seq')
- grad_qkv: float32 [2, 1024, 3072], P(None, 'dp')
- grad_out: float32 [2, 1024, 1024], P(None, 'dp')
- grad_up: float32 [2, 1024, 4096], P(None, 'dp')
- grad_down: float32 [2, 4096, 1024], P(None, 'dp')
- grad_gain: float32 [2, 2, 1024], P(None, None, 'dp')
- grad_shift: float32 [2, 2, 1024], P(None, None, 'dp')
- grad_bias_qv: float32 [2, 2048], P(None, 'dp')
- grad_bias_up: float32 [2, 4096], P(None, 'dp')
- grad_bias_branch: float32 [2, 2, 1024], P(None, None, 'dp')
The draws below stay inside these ranges and needn't reach their ends.
Inputs may be any that keep to these rules, and one draw needn't show every extreme that they name: counts[i, j] is the number of live tokens of image i in the j-th block of 128 slots, which comes first in that block; each row sums to 577 and its largest entry is 128.
All inputs are finite; a program needn't handle non-finite values.
Results may differ from the reference program's by a relative error of at most 0.018.
Values may be sent and summed in bfloat16 or wider, within the bound.
No kernel may reach another device: no remote copies, remote signals or barrier semaphores. Data moves between devices by JAX's collectives and lax.ppermute only.
A program may use at most 256 MiB of HBM per device.

```python
import math
import jax
import jax.numpy as jnp
import numpy as np
from jax import lax

D = 1024
HEADS = 16
HEAD_DIM = 64
FF = 4096
LEN = 577
LAYERS = 2
SLOT = 128
SPAN = 1024
IMAGES = 16
N_SEQ = 8


def raised(result, stream_key, source, target, shards_of, factor):
    def block_of(position):
        return (jnp.arange(result.shape[position]) // (result.shape[position] // shards_of)).reshape((-1,) + (1,) * (result.ndim - 1 - position))

    one_side = jax.random.permutation(stream_key, shards_of)[block_of(target)]
    other_side = (block_of(target) + shards_of // 2) % shards_of
    return jnp.where((block_of(source) == one_side) | (block_of(source) == other_side), factor * result, result)


def shard_levels(stream_key, shape, shards, smallest, top_value):
    def one(position, parts):
        draws = jax.random.uniform(jax.random.fold_in(jax.random.fold_in(stream_key, 6), position), (parts,), jnp.float32, smallest / len(shards), top_value / len(shards))
        return jnp.repeat(jnp.exp(draws), shape[position] // parts).reshape((-1,) + (1,) * (len(shape) - position - 1))

    gain = one(*shards[0])
    for cut in shards[1:]:
        gain = gain * one(*cut)
    return gain


def profile(amount, total, most, slope):
    loads = [(1 << 20) // math.isqrt(standing ** slope) + 1 for standing in range(2, amount + 1)]
    spare, given = total - most - (amount - 1), [1] * (amount - 1)
    while spare > 0:
        free = [i for i in range(amount - 1) if given[i] < most]
        mass, budget = sum([loads[i] for i in free]), spare
        for i in free:
            extra = min(most - given[i], max(1, budget * loads[i] // mass), spare)
            given[i] = given[i] + extra
            spare = spare - extra
    return np.array([most] + given)


def uneven(key, amount, total, limit, skew):
    if amount == 2:
        one = jax.random.randint(key, (), max(1, total - limit), min(limit, total - 1) + 1)
        return jnp.stack([one, total - one])
    lengths = jnp.asarray(profile(amount, total, limit, skew), jnp.int32)
    twos = (amount - 1) // 2
    giver, receiver = lengths[1:1 + 2 * twos:2], lengths[2:2 + 2 * twos:2]
    slack = jnp.minimum(giver - 1, limit - receiver)
    shifted = jax.random.randint(jax.random.fold_in(key, 1), (twos,), 0, 1 << 20) % (slack + 1)
    lengths = lengths.at[1:1 + 2 * twos:2].set(giver - shifted).at[2:2 + 2 * twos:2].set(receiver + shifted)
    return lengths[jax.random.permutation(jax.random.fold_in(key, 2), amount)]


def bell_draw(stream_key, shape, width, reach, cuts=(), held_as=jnp.bfloat16):
    factor_of = shard_levels(stream_key, shape, cuts, -0.22, 0.18) if cuts else 1.0
    entries = jax.random.normal(stream_key, shape, jnp.float32) * width * factor_of
    return jnp.minimum(jnp.maximum(entries, -reach), reach).astype(held_as)


def bell_draw_with(own_key, shape, width, limit, pieces, heavy, held_as=jnp.bfloat16):
    array = width * jax.random.normal(own_key, shape, jnp.float32)
    if pieces:
        array = array * shard_levels(own_key, shape, pieces, -0.22, 0.18)
    return jnp.clip(raised(array, jax.random.fold_in(own_key, 3), *heavy), -limit, limit).astype(held_as)


def setup_inputs(seed: int = 0) -> dict:
    keys = jax.random.split(jax.random.key(seed), 13)
    tokens = bell_draw(keys[0], (IMAGES, SPAN, D), 1.0, 6.0, ((0, 16), (1, 8)))
    counts = jax.vmap(lambda own: uneven(own, N_SEQ, LEN, SLOT, 2))(jax.random.split(keys[1], IMAGES)).reshape((IMAGES, N_SEQ)).astype(jnp.int32)
    cotangent = bell_draw_with(keys[2], (IMAGES, SPAN, D), 1.0, 6.0, ((0, 16), (1, 8)), (0, 2, 16, 2.0))
    w_qkv = bell_draw(keys[3], (LAYERS, D, 3 * D), D ** -0.5, 0.1875, ((1, 16),))
    w_out = bell_draw(keys[4], (LAYERS, D, D), (D // 16) ** -0.5, 0.75, ((1, 16),))
    w_up = bell_draw(keys[5], (LAYERS, D, FF), D ** -0.5, 0.1875, ((1, 16),))
    w_down = bell_draw(keys[6], (LAYERS, FF, D), FF ** -0.5, 0.09375, ((1, 16),))
    norm_gain = jnp.clip(1.0 + 0.1 * jax.random.normal(keys[7], (LAYERS, 2, D), jnp.float32), 0.5, 1.5).astype(jnp.bfloat16)
    norm_shift = bell_draw(keys[8], (LAYERS, 2, D), 0.3, 1.75, ((2, 16),))
    bias_qv = bell_draw(keys[9], (LAYERS, 2 * D), 0.2, 1.25, ((1, 16),))
    bias_up = bell_draw(keys[10], (LAYERS, FF), 0.5, 3.0, ((1, 16),))
    bias_branch = bell_draw(keys[11], (LAYERS, 2, D), 0.3, 1.75, ((2, 16),))
    return {"tokens": tokens, "counts": counts, "cotangent": cotangent, "w_qkv": w_qkv, "w_out": w_out, "w_up": w_up, "w_down": w_down, "norm_gain": norm_gain, "norm_shift": norm_shift, "bias_qv": bias_qv, "bias_up": bias_up, "bias_branch": bias_branch}


@jax.custom_vjp
def low(v):
    return lax.optimization_barrier(v.astype(jnp.bfloat16)).astype(jnp.float32)

@jax.custom_vjp
def low_back(v):
    return v

def low_keep(v):
    return (low(v), None)

def low_pass(kept, grad):
    return (grad,)

def back_keep(v):
    return (v, None)

def back_low(kept, grad):
    return (low(grad),)
low.defvjp(low_keep, low_pass)
low_back.defvjp(back_keep, back_low)
EPSILON = 1e-06
EXACT = lax.Precision.HIGHEST

def normalize(inputs, gain_row, shift_row):
    row_mean = lax.optimization_barrier(jnp.mean(inputs, axis=-1, keepdims=True))
    centered = inputs - row_mean
    variance = lax.optimization_barrier(jnp.mean(centered * centered, axis=-1, keepdims=True))
    return centered * lax.rsqrt(variance + EPSILON) * gain_row + shift_row

def image_attention(queries, key_rows, value_rows, validity):
    scores = jnp.einsum('qhd,khd->hqk', queries, key_rows, precision=EXACT) * HEAD_DIM ** (-0.5)
    scores = jnp.where(validity[None, None, :], scores, -1000000000.0)
    scores = low_back(scores)
    attention = low(jax.nn.softmax(scores, axis=-1))
    return jnp.einsum('hqk,khd->qhd', attention, value_rows, precision=EXACT)

def encoder_layer(hidden, validity, params):
    qkv_weight, out_weight, up_weight, down_weight, gains, shifts, qv_bias, up_bias, branch_bias = params
    inputs = hidden.reshape(-1, D)
    normed = low(normalize(inputs, gains[0], shifts[0]))
    packed = jnp.dot(normed, qkv_weight, precision=EXACT)
    zeros_mid = jnp.zeros((D,), jnp.float32)
    packed = packed + jnp.concatenate([qv_bias[:D], zeros_mid, qv_bias[D:]])
    packed = low_back(low(packed))
    packed = packed.reshape(IMAGES, SPAN, 3, HEADS, HEAD_DIM)
    attend = jax.checkpoint(image_attention)
    mixed = lax.map(lambda element: attend(element[0][:, 0], element[0][:, 1], element[0][:, 2], element[1]), (packed, validity))
    mixed = low_back(low(mixed)).reshape(-1, D)
    branch_one = low_back(jnp.dot(mixed, out_weight, precision=EXACT) + branch_bias[0])
    middle = inputs + branch_one
    normed_two = low(normalize(middle, gains[1], shifts[1]))
    upward = low_back(jnp.dot(normed_two, up_weight, precision=EXACT) + up_bias)
    activated = low(jax.nn.gelu(upward, approximate=False))
    branch_two = low_back(jnp.dot(activated, down_weight, precision=EXACT) + branch_bias[1])
    return (middle + branch_two).reshape(hidden.shape)

def reference(tokens, counts, cotangent, w_qkv, w_out, w_up, w_down, norm_gain, norm_shift, bias_qv, bias_up, bias_branch):
    positions = jnp.arange(N_SEQ * SLOT, dtype=jnp.int32)
    validity = (positions % SLOT)[None, :] < jnp.repeat(counts, SLOT, axis=1)
    row_mask = validity.astype(jnp.float32)[:, :, None]
    params = tuple((weight.astype(jnp.float32) for weight in (w_qkv, w_out, w_up, w_down, norm_gain, norm_shift, bias_qv, bias_up, bias_branch)))

    def forward(inputs, weights):
        hidden = inputs
        for layer_index in range(LAYERS):
            hidden = encoder_layer(hidden, validity, tuple((weight[layer_index] for weight in weights)))
        return hidden * row_mask
    output, pullback = jax.vjp(forward, tokens.astype(jnp.float32), params)
    grad_inputs, gradients = pullback(cotangent.astype(jnp.float32))
    return (output.astype(jnp.bfloat16), grad_inputs.astype(jnp.bfloat16), gradients[0], gradients[1], gradients[2], gradients[3], gradients[4], gradients[5], gradients[6], gradients[7], gradients[8])
```

```python
import jax
import jax.numpy as jnp
from jax import lax
from jax.sharding import PartitionSpec as P

EPSILON = 1e-06
BF = jnp.bfloat16
F32 = jnp.float32
BLOCK = 80
SHARE = 73
TOTAL = 577

NEXT = [(i, (i + 2) % 8) for i in range(8)]
PREV = [(i, (i - 2) % 8) for i in range(8)]
FAR = [(i, (i + 4) % 8) for i in range(8)]
CORE = [(i, i ^ 1) for i in range(8)]


def x_gather(block):
    return [
        block,
        lax.ppermute(block, "seq", PREV),
        lax.ppermute(block, "seq", FAR),
        lax.ppermute(block, "seq", NEXT),
    ]


def x_scatter(blocks):
    return [
        blocks[0],
        lax.ppermute(blocks[1], "seq", NEXT),
        lax.ppermute(blocks[2], "seq", FAR),
        lax.ppermute(blocks[3], "seq", PREV),
    ]


def core_swap(v):
    return lax.ppermute(v, "seq", CORE)


def dot(a, b):
    return jnp.dot(a, b, preferred_element_type=F32)


def dot_nt(a, b):
    return lax.dot_general(a, b, (((1,), (1,)), ((), ())), preferred_element_type=F32)


def dot_tn(a, b):
    return lax.dot_general(a, b, (((0,), (0,)), ((), ())), preferred_element_type=F32)


def norm_parts(rows):
    mean = jnp.mean(rows, axis=-1, keepdims=True)
    centered = rows - mean
    rstd = lax.rsqrt(jnp.mean(centered * centered, axis=-1, keepdims=True) + EPSILON)
    return centered * rstd, rstd


def layer_norm(rows, gain, shift):
    return (norm_parts(rows)[0] * gain + shift).astype(BF)


def norm_back(rows, gain, err):
    n, rstd = norm_parts(rows)
    eg = err * gain
    back = rstd * (
        eg - jnp.mean(eg, axis=-1, keepdims=True) - n * jnp.mean(eg * n, axis=-1, keepdims=True)
    )
    return back, jnp.sum(err * n, axis=0), jnp.sum(err, axis=0)


def heads(v):
    return v.reshape(v.shape[0], 4, 64)


def attend(q, k, v, keep):
    s = jnp.einsum("qhd,khd->hqk", heads(q), heads(k), preferred_element_type=F32) * 0.125
    s = jnp.where(keep[None], s, -1e9)
    top = jnp.max(s, axis=-1, keepdims=True)
    e = jnp.exp(s - top)
    total = jnp.sum(e, axis=-1, keepdims=True)
    p = (e / total).astype(BF)
    mixed = jnp.einsum("hqk,khd->qhd", p, heads(v), preferred_element_type=F32)
    return mixed.reshape(q.shape).astype(BF), top + jnp.log(total)


def attend_back(q, k, v, keep, lse, dmixed):
    s = jnp.einsum("qhd,khd->hqk", heads(q), heads(k), preferred_element_type=F32) * 0.125
    s = jnp.where(keep[None], s, -1e9)
    p = jnp.exp(s - lse)
    dp = jnp.einsum("qhd,khd->hqk", heads(dmixed), heads(v), preferred_element_type=F32)
    inner = jnp.sum(dp * p, axis=-1, keepdims=True)
    ds = (p * (dp - inner)).astype(BF)
    dq = jnp.einsum("hqk,khd->qhd", ds, heads(k), preferred_element_type=F32) * 0.125
    dk = jnp.einsum("hqk,qhd->khd", ds, heads(q), preferred_element_type=F32) * 0.125
    dv = jnp.einsum("hqk,qhd->khd", p.astype(BF), heads(dmixed), preferred_element_type=F32)
    return dq.reshape(q.shape), dk.reshape(k.shape), dv.reshape(v.shape)


def swap_halves(v):
    n = v.shape[-1] // 2
    return jnp.concatenate([v[..., n:], v[..., :n]], axis=-1)


def shards(tokens, counts, cotangent, w_qkv, w_out, w_up, w_down, norm_gain, norm_shift,
           bias_qv, bias_up, bias_branch):
    s = lax.axis_index("seq")
    x = s // 2
    c = s % 2
    at = lambda v, i, axis: lax.dynamic_index_in_dim(v, i, axis, keepdims=False)

    live = counts[0]
    start = jnp.cumsum(live) - live
    slot = jnp.arange(1024, dtype=jnp.int32)
    in_slot = slot % 128
    slot_rank = jnp.where(in_slot < jnp.repeat(live, 128), jnp.repeat(start, 128) + in_slot, -1)

    def ranks(core):
        r = jnp.arange(4 * BLOCK, dtype=jnp.int32)
        within = r % BLOCK
        rank = (core * 4 + (x + r // BLOCK) % 4) * SHARE + within
        return jnp.where((within < SHARE) & (rank < TOTAL), rank, -2)

    mine_rank, other_rank = ranks(c), ranks(1 - c)
    keep = (jnp.concatenate([mine_rank, other_rank]) >= 0)[None, :]
    order = ((x + jnp.arange(4)) % 4 * 2)[None, :] + jnp.stack([c, 1 - c])[:, None]
    came_rank = slot_rank.reshape(8, 128)[order.reshape(8)].reshape(1024)
    pick = (mine_rank[:, None] == came_rank[None, :]).astype(BF)
    own_rank = at(slot_rank.reshape(8, 128), s, 0)
    place = (own_rank[:, None] == jnp.concatenate([mine_rank, other_rank])[None, :]).astype(BF)

    def compact(rows):
        half = jnp.concatenate(x_gather(rows), axis=0)
        return dot(pick, jnp.concatenate([half, core_swap(half)], axis=0)).astype(BF)

    def spread(block):
        half = jnp.concatenate(x_gather(block), axis=0)
        return dot(place, jnp.concatenate([half, core_swap(half)], axis=0)).astype(BF)

    def offered(l):
        qkv = at(w_qkv[l].reshape(64, 3, 8, 128), 2 * x + c, 2).reshape(64, 384)
        up = at(at(w_up[l].reshape(64, 2, 8, 4, 64), c, 1), x, 2).reshape(64, 512)
        out = at(w_out[l].reshape(64, 2, 512), c, 1)
        down = at(at(w_down[l].reshape(4, 64, 2, 512), x, 0), c, 1)
        return jnp.concatenate([qkv, up, out, down], axis=1)

    small = jnp.concatenate([norm_gain.reshape(-1), norm_shift.reshape(-1), bias_branch.reshape(-1),
                             bias_qv.reshape(-1), bias_up.reshape(-1)])
    small = lax.all_gather(small.reshape(12, 128), "dp", axis=0).reshape(16, 1536).astype(F32)
    per_d = lambda i: small[:, i:i + 256].reshape(16, 2, 2, 64).transpose(1, 2, 0, 3).reshape(2, 2, 1024)
    gains, shifts, branch = per_d(0), per_d(256), per_d(512)
    qv = small[:, 768:1024].reshape(2, 8, 2, 128)
    upb = small[:, 1024:1536].reshape(2, 8, 2, 4, 64)

    weights = []
    for l in range(2):
        mine = lax.all_gather(offered(l), "dp", axis=0, tiled=True)
        other = core_swap(mine)
        w = []
        for v, cc in ((mine, c), (other, 1 - c)):
            qb, vb = at(qv[0, :, l], 2 * x + cc, 0), at(qv[1, :, l], 2 * x + cc, 0)
            w.append(dict(qkv=v[:, :384], up=v[:, 384:896], out=v[:, 896:1408], down=v[:, 1408:],
                          qkv_bias=jnp.concatenate([qb, jnp.zeros((128,), F32), vb]),
                          up_bias=at(at(upb[:, :, l], cc, 0), x, 1).reshape(512)))
        full_out = jnp.where(c == 0, jnp.concatenate([w[0]["out"], w[1]["out"]], 1),
                             jnp.concatenate([w[1]["out"], w[0]["out"]], 1))
        pairs = jnp.stack([2 * ((x + j) % 4) + (c + i) % 2 for j in range(4) for i in range(2)])
        full_out = full_out.reshape(8, 128, 1024)[pairs].reshape(1024, 1024)
        down = [jnp.concatenate([at(v["down"].reshape(2, 512, 512), cc, 0) for cc in (c, 1 - c)], 0) for v in w]
        down = jnp.where(c == 0, jnp.concatenate(down, 1), jnp.concatenate(down[::-1], 1))
        weights.append(dict(
            qkv=jnp.concatenate([w[0]["qkv"], w[1]["qkv"]], 1),
            qkv_bias=jnp.concatenate([w[0]["qkv_bias"], w[1]["qkv_bias"]]),
            up=jnp.concatenate([w[0]["up"], w[1]["up"]], 1),
            up_bias=jnp.concatenate([w[0]["up_bias"], w[1]["up_bias"]]),
            out=full_out, down=down))

    hidden = compact(tokens[0]).astype(F32)
    kept = []
    for l in range(2):
        w = weights[l]
        a = layer_norm(hidden, gains[l, 0], shifts[l, 0])
        packed = (dot(a, w["qkv"]) + w["qkv_bias"]).astype(BF)
        q = jnp.concatenate([packed[:, :128], packed[:, 384:512]], 1)
        k = jnp.concatenate([packed[:, 128:256], packed[:, 512:640]], 1)
        v = jnp.concatenate([packed[:, 256:384], packed[:, 640:]], 1)
        far = core_swap(jnp.concatenate([swap_halves(k), swap_halves(v)], 1))
        k = jnp.concatenate([k, far[:, :256]], 0)
        v = jnp.concatenate([v, far[:, 256:]], 0)
        mixed, lse = attend(q, k, v, keep)
        came = x_gather(mixed)
        came = [jnp.roll(m.reshape(4, BLOCK, 256), j, axis=0).reshape(4 * BLOCK, 256) for j, m in enumerate(came)]
        all_mixed = jnp.concatenate(came, axis=1)
        middle = hidden + dot(all_mixed, w["out"]) + branch[l, 0]
        cc = layer_norm(middle, gains[l, 1], shifts[l, 1])
        u = dot(cc, w["up"]) + w["up_bias"]
        g, gelu_back = jax.vjp(lambda t: jax.nn.gelu(t, approximate=False), u)
        g = g.astype(BF)
        slope = gelu_back(jnp.ones_like(u))[0]
        part = dot(g, w["down"]).astype(BF).reshape(4, BLOCK, 1024)
        mlp = sum(t.astype(F32) for t in x_scatter([part[j] for j in range(4)]))
        kept.append((hidden, a, q, k, v, lse, all_mixed, middle, cc, g, slope))
        if l == 0:
            mlp = jnp.concatenate(x_gather(mlp.astype(BF)), axis=0).astype(F32)
            hidden = middle + mlp + branch[l, 1]
        else:
            last = middle[:BLOCK] + mlp + branch[l, 1]
    output = spread(last.astype(BF))

    dz = compact(cotangent[0])
    dh = dz[:BLOCK].astype(F32)
    big, tiny = [None, None], [None, None]
    for l in (1, 0):
        w = weights[l]
        hidden, a, q, k, v, lse, all_mixed, middle, cc, g, slope = kept[l]
        du = (dot_nt(dz, w["down"]) * slope).astype(BF)
        part = dot_nt(du, w["up"]).astype(BF).reshape(4, BLOCK, 1024)
        err = sum(t.astype(F32) for t in x_scatter([part[j] for j in range(4)]))
        d_down = dot_tn(g, dz)
        d_up = dot_tn(cc, du)
        d_up_bias = jnp.sum(du.astype(F32), axis=0)
        d_branch1 = jnp.sum(dz[:BLOCK].astype(F32), axis=0)
        back, d_gain1, d_shift1 = norm_back(middle[:BLOCK], gains[l, 1], err)
        dm = dh + back
        dmb = dm.astype(BF)
        d_branch0 = jnp.sum(dmb.astype(F32), axis=0)
        dmb = jnp.concatenate(x_gather(dmb), axis=0)
        dmixed = dot_nt(dmb, w["out"][:256]).astype(BF)
        dq, dk, dv = attend_back(q, k, v, keep, lse, dmixed)
        n = 4 * BLOCK
        far = core_swap(jnp.concatenate([swap_halves(dk[n:]), swap_halves(dv[n:])], 1).astype(BF)).astype(F32)
        dq = dq.astype(BF)
        dk = (dk[:n] + far[:, :256]).astype(BF)
        dv = (dv[:n] + far[:, 256:]).astype(BF)
        dpacked = jnp.concatenate([dq[:, :128], dk[:, :128], dv[:, :128], dq[:, 128:], dk[:, 128:], dv[:, 128:]], 1)
        part = dot_nt(dpacked, w["qkv"]).astype(BF).reshape(4, BLOCK, 1024)
        err = sum(t.astype(F32) for t in x_scatter([part[j] for j in range(4)]))
        d_qkv = dot_tn(a, dpacked)
        d_qv = jnp.sum(dpacked.astype(F32), axis=0)
        d_out = dot_tn(all_mixed, lax.dynamic_slice_in_dim(dmb, 256 * x, 256, 1))
        back, d_gain0, d_shift0 = norm_back(hidden[:BLOCK], gains[l, 0], err)
        dh = dm + back
        dz = dh.astype(BF)
        if l == 1:
            dz = jnp.concatenate(x_gather(dz), axis=0)

        pair_at = [((2 * ((p // 2 - x) % 4)) + (p % 2 - c) % 2) for p in range(8)]
        d_out = d_out.reshape(8, 128, 256)[jnp.stack(pair_at)].reshape(1024, 256)
        halves = []
        for i, core in ((0, c), (1, 1 - c)):
            dd = lax.dynamic_slice_in_dim(d_down, core * 512, 512, 1).reshape(2, 512, 512)
            dd = jnp.concatenate([at(dd, c, 0), at(dd, 1 - c, 0)], 0)
            halves.append(jnp.concatenate([
                d_qkv[:, 384 * i:384 * (i + 1)], d_up[:, 512 * i:512 * (i + 1)],
                lax.dynamic_slice_in_dim(d_out, 128 * core, 128, 1), dd], axis=1).astype(BF))
        grads = (halves[0].astype(F32) + core_swap(halves[1]).astype(F32)).astype(BF)
        got = lax.all_to_all(grads.reshape(16, 64, 1536), "dp", split_axis=0, concat_axis=0, tiled=True)
        got = jnp.sum(got.astype(F32), axis=0).astype(BF)
        half = jnp.stack(x_gather(got))
        both = jnp.stack([half, core_swap(half)])
        both = jnp.stack([at(both, c, 0), at(both, 1 - c, 0)], 1)
        both = jnp.stack([at(both, (j - x) % 4, 0) for j in range(4)])
        big[l] = (
            both[..., :384].reshape(4, 2, 64, 3, 128).transpose(2, 3, 0, 1, 4).reshape(64, 3072),
            both[..., 896:1024].transpose(2, 0, 1, 3).reshape(64, 1024),
            both[..., 384:896].reshape(4, 2, 64, 8, 64).transpose(2, 1, 3, 0, 4).reshape(64, 4096),
            both[..., 1024:].transpose(0, 2, 1, 3).reshape(256, 1024),
        )
        tiny[l] = (jnp.stack([d_gain0, d_gain1]), jnp.stack([d_shift0, d_shift1]),
                   jnp.stack([d_branch0, d_branch1]), d_qv, d_up_bias)
    grad_tokens = spread(dz)

    pieces = []
    by_d = lambda member: jnp.stack([tiny[0][member], tiny[1][member]]).reshape(4, 16, 64).transpose(1, 0, 2).reshape(16, 256)
    pair = jnp.arange(8)
    qv_all = jnp.zeros((2, 2, 8, 128), F32)
    up_all = jnp.zeros((2, 2, 8, 4, 64), F32)
    for l in range(2):
        d_qv, d_up_bias = tiny[l][3], tiny[l][4]
        for i, core in ((0, c), (1, 1 - c)):
            here = (pair == 2 * x + core)[:, None]
            qv_all = qv_all.at[l, 0].add(jnp.where(here, d_qv[384 * i:384 * i + 128], 0.0))
            qv_all = qv_all.at[l, 1].add(jnp.where(here, d_qv[384 * i + 256:384 * i + 384], 0.0))
            here = (jnp.arange(2) == core)[:, None, None, None] & (jnp.arange(4) == x)[None, None, :, None]
            up_all = up_all.at[l].add(jnp.where(here, d_up_bias[512 * i:512 * (i + 1)].reshape(1, 8, 1, 64), 0.0))
    pieces = [by_d(0), by_d(1), by_d(2),
              qv_all.reshape(2, 16, 128).transpose(1, 0, 2).reshape(16, 256),
              up_all.reshape(2, 16, 256).transpose(1, 0, 2).reshape(16, 512)]
    tiny_all = jnp.concatenate(pieces, 1).reshape(16, 12, 128)
    got = lax.all_to_all(tiny_all, "dp", split_axis=0, concat_axis=0, tiled=True)
    got = jnp.sum(got, axis=0)
    got = sum(x_gather(got))
    got = (got + core_swap(got)).reshape(-1)
    lead = lambda i: jnp.stack([big[0][i], big[1][i]]).astype(F32)
    return (
        output[None], spread_shape(grad_tokens),
        lead(0), lead(1), lead(2), lead(3),
        got[:256].reshape(2, 2, 64), got[256:512].reshape(2, 2, 64),
        got[768:1024].reshape(2, 128), got[1024:].reshape(2, 256),
        got[512:768].reshape(2, 2, 64),
    )


def spread_shape(v):
    return v[None]


def solution(mesh):
    rows = P("dp", "seq", None)
    mid = P(None, "dp", None)
    end = P(None, None, "dp")
    two = P(None, "dp")
    return jax.shard_map(
        shards,
        mesh=mesh,
        in_specs=(rows, P("dp", None), rows, mid, mid, mid, mid, end, end, two, two, end),
        out_specs=(rows, rows, mid, mid, mid, mid, end, end, two, two, end),
        check_vma=False,
    )
```

```python
import functools

import jax
import jax.numpy as jnp
from jax import lax
from jax.experimental import pallas as pl
from jax.experimental.pallas import tpu as pltpu
from jax.sharding import PartitionSpec as P

EPSILON = 1e-06
BF = jnp.bfloat16
F32 = jnp.float32
BLOCK = 80
SHARE = 73
TOTAL = 577
ROWS = 4 * BLOCK
D = 1024
LOOSE = ((8, 128), jnp.float32)
MARK = ((8, 128), jnp.float32, "saved")
LIMIT = 24

NEXT = [(i, (i + 2) % 8) for i in range(8)]
PREV = [(i, (i - 2) % 8) for i in range(8)]
FAR = [(i, (i + 4) % 8) for i in range(8)]
CORE = [(i, i ^ 1) for i in range(8)]


def x_gather(block):
    return [
        block,
        lax.ppermute(block, "seq", PREV),
        lax.ppermute(block, "seq", FAR),
        lax.ppermute(block, "seq", NEXT),
    ]


def x_scatter(blocks):
    return [
        blocks[0],
        lax.ppermute(blocks[1], "seq", NEXT),
        lax.ppermute(blocks[2], "seq", FAR),
        lax.ppermute(blocks[3], "seq", PREV),
    ]


def core_swap(v):
    return lax.ppermute(v, "seq", CORE)


def dp_pairs(step, k):
    if step == 1:
        return [(i, i // 4 * 4 + (i + k) % 4) for i in range(16)]
    return [(i, (i + 4 * k) % 16) for i in range(16)]


def dp_scatter(blocks, step):
    return [blocks[0]] + [lax.ppermute(blocks[k], "dp", dp_pairs(step, k)) for k in (1, 2, 3)]


def dp_gather(block, step):
    return [block] + [lax.ppermute(block, "dp", dp_pairs(step, -k)) for k in (1, 2, 3)]


def dot(a, b):
    return jnp.dot(a, b, preferred_element_type=F32)


def dot_nt(a, b):
    return lax.dot_general(a, b, (((1,), (1,)), ((), ())), preferred_element_type=F32)


def dot_tn(a, b):
    return lax.dot_general(a, b, (((0,), (0,)), ((), ())), preferred_element_type=F32)


def cols(ref, at, width):
    return ref.at[:, pl.ds(pl.multiple_of(at, 128), width)]


def norm_parts(rows):
    mean = jnp.mean(rows, axis=-1, keepdims=True)
    centered = rows - mean
    rstd = lax.rsqrt(jnp.mean(centered * centered, axis=-1, keepdims=True) + EPSILON)
    return centered * rstd, rstd


def away(v):
    return ("away", v)


def saved(v):
    return ("saved", v)


def in_hbm(outs):
    return [o + ("saved",) for o in outs]


def run(kernel, outs, *ins, scratch=(), after=(), us=1.0):
    once = pl.Buffered(1)
    small = lambda v: v.size < 100000
    hbm = lambda v: pltpu.with_memory_space_constraint(v, pltpu.HBM)
    whole = lambda s: pl.BlockSpec(s, functools.partial(lambda n, _: (0,) * n, len(s)), pipeline_mode=once)
    specs, arrays = [], []
    for v in ins:
        if isinstance(v, tuple) and len(v) == 2:
            kind, v = v
            specs.append(whole(v.shape) if kind == "saved" else pl.BlockSpec(memory_space=pl.ANY if kind == "any" else pltpu.HBM))
            v = v if kind == "any" else hbm(v)
        elif isinstance(v, tuple):
            v, block, index = v
            specs.append(pl.BlockSpec(block, functools.partial(lambda at, _: at, index), pipeline_mode=once))
            if isinstance(v, tuple):
                v = hbm(v[1])
        elif v.dtype == jnp.int32:
            specs.append(pl.BlockSpec(memory_space=pltpu.SMEM))
        else:
            specs.append(whole(v.shape))
        arrays.append(v)
    specs += [pl.BlockSpec(memory_space=pl.ANY if small(v) else pltpu.HBM) for v in after]
    n = len(arrays)
    body = lambda *refs: kernel(*refs[:n], *refs[n + len(after):])
    kinds = [o[2] if len(o) > 2 else "" for o in outs]
    return pl.pallas_call(
        body,
        grid=(1,),
        in_specs=specs,
        out_specs=[pl.BlockSpec(memory_space=pltpu.HBM) if k == "away" else whole(o[0]) for k, o in zip(kinds, outs)],
        out_shape=[pltpu.HBM(o[0], o[1]) if k else jax.ShapeDtypeStruct(o[0], o[1]) for k, o in zip(kinds, outs)],
        scratch_shapes=list(scratch),
        compiler_params=pltpu.CompilerParams(vmem_limit_bytes=LIMIT << 20),
        cost_estimate=pl.CostEstimate(flops=int(us * 1.0 * 1.15e9), bytes_accessed=1, transcendentals=0),
    )(*arrays, *[v if small(v) else hbm(v) for v in after])


def fetch(parts, buf, sem):
    copies = [pltpu.make_async_copy(v, buf.at[i], sem.at[i]) for i, v in enumerate(parts)]
    for copy in copies:
        copy.start()
    return copies


def send(pairs, sem):
    copies = [pltpu.make_async_copy(v, out, sem.at[i]) for i, (v, out) in enumerate(pairs)]
    for copy in copies:
        copy.start()
    return copies


def held(count, rows, width):
    return [pltpu.VMEM((count, rows, width), BF), pltpu.SemaphoreType.DMA((count,))]


def half_ranks(shape, axis, x, core):
    at = lax.broadcasted_iota(jnp.int32, shape, axis)
    block = sum((at >= BLOCK * i).astype(jnp.int32) for i in (1, 2, 3))
    within = at - BLOCK * block
    chip = x + block
    chip = jnp.where(chip >= 4, chip - 4, chip)
    rank = (4 * core + chip) * SHARE + within
    return jnp.where((within < SHARE) & (rank < TOTAL), rank, -2)


def slot_ranks(shape, axis, counts, s):
    at = lax.broadcasted_iota(jnp.int32, shape, axis)
    start = sum(jnp.where(i < s, counts[0, i], 0) for i in range(8))
    return jnp.where(at < counts[0, s], start + at, -1)


def kept_keys(x, c):
    at = lax.broadcasted_iota(jnp.int32, (1, 2 * ROWS), 1)
    second = (at >= ROWS).astype(jnp.int32)
    at = at - ROWS * second
    block = sum((at >= BLOCK * i).astype(jnp.int32) for i in (1, 2, 3))
    chip = x + block
    chip = jnp.where(chip >= 4, chip - 4, chip)
    core = jnp.where(second > 0, 1 - c, c)
    within = at - BLOCK * block
    return (within < SHARE) & ((4 * core + chip) * SHARE + within < TOTAL)


def pick_kernel(ids, counts, t0, t1, t2, t3, own_ref, far_ref):
    x, c = ids[0], ids[1]
    rows = jnp.concatenate([t[...] for t in (t0, t1, t2, t3)], axis=0)
    slots = [slot_ranks((1, 128), 1, counts, 2 * lax.rem(x + j, 4) + c) for j in range(4)]
    for core, out in ((c, own_ref), (1 - c, far_ref)):
        rank = half_ranks((ROWS, 1), 0, x, core)
        pick = jnp.concatenate([jnp.where(rank == s, 1.0, 0.0) for s in slots], axis=1)
        out[...] = dot(pick.astype(BF), rows).astype(BF)


def join_kernel(own, far, dz_ref, dh_ref, mark):
    mark[...] = jnp.zeros_like(mark)
    dz = own[...] + far[...]
    dz_ref[...] = dz
    dh_ref[...] = dz[:BLOCK, :].astype(F32)


def place_kernel(ids, counts, b0, b1, b2, b3, own_ref, far_ref):
    x, c = ids[0], ids[1]
    rows = jnp.concatenate([t[...] for t in (b0, b1, b2, b3)], axis=0)
    rank = half_ranks((1, ROWS), 1, x, c)
    for core, out in ((c, own_ref), (1 - c, far_ref)):
        put = jnp.where(slot_ranks((128, 1), 0, counts, 2 * x + core) == rank, 1.0, 0.0).astype(BF)
        out[...] = dot(put, rows).astype(BF)


def pack_kernel(ids, w_qkv, w_out, w_up, w_down, gain, shift, branch, qv, up,
                first_ref, rest0_ref, rest1_ref, qkv_buf, up_buf, norm_buf, qv_buf, wide_buf, sem):
    x, c = ids[0], ids[1]
    lanes = lambda at, width: pl.ds(pl.multiple_of(at, 128), width)
    copies = []

    def copy(source, target):
        copies.append(pltpu.make_async_copy(source, target, sem.at[len(copies)]))
        copies[-1].start()

    rests = (rest0_ref, rest1_ref)
    for l in range(2):
        for m in range(3):
            target = qkv_buf.at[:, pl.ds(128 * m, 128)] if l == 0 else rest0_ref.at[:, pl.ds(1536 + 128 * m, 128)]
            copy(w_qkv.at[l, :, lanes(D * m + 256 * x + 128 * c, 128)], target)
        for d in range(8):
            copy(w_up.at[l, :, lanes(2048 * c + 256 * d + 128 * (x // 2), 128)], up_buf.at[l, d])
        copy(w_out.at[l, :, lanes(512 * c, 512)], rests[l].at[:, pl.ds(512, 512)])
        copy(w_down.at[l, pl.ds(pl.multiple_of(64 * x, 64), 64), lanes(512 * c, 512)], rests[l].at[:, pl.ds(1024, 512)])
    for i, v in enumerate((gain, shift, branch)):
        copy(v, norm_buf.at[i])
    copy(qv, qv_buf)
    copy(up, wide_buf)
    for each in copies:
        each.wait()
    pairs = lambda i: jnp.concatenate([norm_buf[i, 0], norm_buf[i, 1]], axis=0).astype(F32)
    wide = wide_buf[...].astype(F32)
    small = jnp.concatenate([
        jnp.concatenate([pairs(0), pairs(1)], axis=1),
        jnp.concatenate([pairs(2), jnp.zeros((4, 64), F32)], axis=1),
        qv_buf[...].astype(F32),
        wide[0:1, :128], wide[0:1, 128:], wide[1:2, :128], wide[1:2, 128:],
        jnp.zeros((50, 128), F32)], axis=0).astype(BF)
    block = jnp.concatenate([qkv_buf[...], small], axis=1)
    first_ref[...] = block
    odd = lax.rem(x, 2) == 1
    for l in range(2):
        got = []
        for d in range(8):
            piece = up_buf[l, d].astype(F32)
            got.append(jnp.where(odd, piece[:, 64:], piece[:, :64]))
        rests[l][:, :512] = jnp.concatenate(got, axis=1).astype(BF)


def order_kernel(ids, a, b, c, d, out):
    for i, v in enumerate((a, b, c, d)):
        out[lax.rem(ids[2] + i, 4)] = v[...]


def unpack_kernel(ids, a, b, c, d, first_ref, vec_ref, qkv_ref, up_ref, first):
    for i, v in enumerate((a, b, c, d)):
        for y in range(4):
            first[4 * lax.rem(ids[3] + i, 4) + y] = v[y]
    for i in range(16):
        first_ref[64 * i:64 * (i + 1), :] = first[i]
    x, c = ids[0], ids[1]
    rows = [first[d, 0:16, 384:].astype(F32) for d in range(16)]
    line = lambda at, lanes: jnp.concatenate([r[at:at + 4, lanes:lanes + 64] for r in rows], axis=1)
    vec_ref[...] = jnp.concatenate([line(0, 0), line(0, 64), line(4, 0), jnp.zeros((4, D), F32)], axis=0)
    qkv, up = [], []
    for l in range(2):
        for core in (c, 1 - c):
            q = first[2 * x + core, 0:16, 384:].astype(F32)[8 + l:9 + l]
            v = first[8 + 2 * x + core, 0:16, 384:].astype(F32)[8 + l:9 + l]
            qkv.append(jnp.concatenate([q, jnp.zeros((1, 128), F32), v], axis=1))
            got = []
            for d in range(8):
                r = first[8 * core + d, 0:16, 384:].astype(F32)
                r = jnp.where(x >= 2, r[11 + 2 * l:12 + 2 * l], r[10 + 2 * l:11 + 2 * l])
                got.append(jnp.where(lax.rem(x, 2) == 1, r[:, 64:], r[:, :64]))
            up.append(jnp.concatenate(got, axis=1))
    qkv_ref[...] = jnp.concatenate(qkv + [jnp.zeros((4, 384), F32)], axis=0)
    up_ref[...] = jnp.concatenate(up + [jnp.zeros((4, 512), F32)], axis=0)


def qkv_kernel(l, ids, vec, bias, *refs):
    gain, shift = vec[2 * l:2 * l + 1, :], vec[4 + 2 * l:5 + 2 * l, :]
    first = l == 0
    keeps = []
    if first:
        own, far, wm, wo, h_ref, a_ref, q_ref, kv_ref = refs
        weight = lambda i: (wm, wo)[i][:, :384]
    else:
        (m, d0, d1, d2, d3, g, slope, wm, wo, h_ref, a_ref, q_ref, kv_ref,
         m_out, g_out, slope_out, buf, sem, out_sem) = refs
        branch = vec[9:10, :]
        copies = fetch([w.at[:, pl.ds(1536, 384)] for w in (wm, wo)], buf, sem)
        keeps = send([(m.at[pl.ds(0, BLOCK), :], m_out), (g, g_out), (slope, slope_out)], out_sem)

        def weight(i):
            copies[i].wait()
            return buf[i]

    c = ids[1]
    for r in range(0, ROWS, 16):
        rows = slice(r, r + 16)
        if first:
            h = own[rows, :].astype(F32) + far[rows, :].astype(F32)
        else:
            b, o = divmod(r, BLOCK)
            h = m[rows, :] + (d0, d1, d2, d3)[b][o:o + 16, :].astype(F32) + branch
        h_ref[rows, :] = h
        a_ref[rows, :] = (norm_parts(h)[0] * gain + shift).astype(BF)
    a = a_ref[...]
    for i in range(2):
        core = c if i == 0 else 1 - c
        packed = (dot(a, weight(i)) + bias[2 * l + i:2 * l + i + 1, :]).astype(BF)
        cols(q_ref, 128 * core, 128)[...] = packed[:, :128]
        cols(kv_ref, 128 * core, 128)[...] = packed[:, 128:256]
        cols(kv_ref, 256 + 128 * core, 128)[...] = packed[:, 256:]
    for keep in keeps:
        keep.wait()


def head_mask(rows, sub):
    lane = lax.broadcasted_iota(jnp.int32, (rows, 128), 1)
    return (lane < 64) if sub == 0 else (lane >= 64)


def attend_kernel(ids, q_ref, kv_ref, far_ref, *refs):
    keeps = []
    if len(refs) == 2:
        mixed_ref, lse_ref = refs
    else:
        n = (len(refs) - 5) // 2
        mixed_ref, lse_ref = refs[n:n + 2]
        outs, sem = refs[n + 2:-1], refs[-1]
        keeps = send([(q_ref, outs[0]), (kv_ref, outs[1].at[pl.ds(0, ROWS), :]),
                      (far_ref, outs[1].at[pl.ds(ROWS, ROWS), :])], sem)
        keeps += send(list(zip(refs[:n], outs[2:])), sem.at[pl.ds(3, n)])
    low = head_mask(ROWS, 0)
    keep = kept_keys(ids[0], ids[1])
    lane = lax.broadcasted_iota(jnp.int32, (ROWS, 128), 1)
    lses = jnp.zeros((ROWS, 128), F32)
    for pair in range(2):
        at = 128 * pair
        k = jnp.concatenate([kv_ref[:, at:at + 128], far_ref[:, at:at + 128]], axis=0)
        v = jnp.concatenate([kv_ref[:, 256 + at:384 + at], far_ref[:, 256 + at:384 + at]], axis=0)
        q = q_ref[:, at:at + 128]
        got = []
        for sub in range(2):
            qm = jnp.where(low if sub == 0 else ~low, q, jnp.zeros_like(q))
            s = dot_nt(qm, k) * 0.125
            s = jnp.where(keep, s, -1e9)
            top = jnp.max(s, axis=-1, keepdims=True)
            e = jnp.exp(s - top)
            total = jnp.sum(e, axis=-1, keepdims=True)
            got.append(dot((e * (1.0 / total)).astype(BF), v))
            lses = jnp.where(lane == 2 * pair + sub, top + jnp.log(total), lses)
        mixed_ref[:, at:at + 128] = jnp.where(low, got[0], got[1]).astype(BF)
    lse_ref[...] = lses
    for keep in keeps:
        keep.wait()


def mlp_kernel(l, ids, vec, up_bias, mx0, mx1, mx2, mx3, h, wm, wo, *refs):
    x, c = ids[0], ids[1]
    keeps = []
    if l == 0:
        (all_out, c_out, m_ref, g_ref, slope_ref, p0, p1, p2, p3,
         u_ref, buf, sem, all_ref, c_ref, out_sem) = refs
    else:
        all_ref, c_ref, m_ref, g_ref, slope_ref, p0, p1, p2, p3, u_ref, buf, sem = refs
    copies = fetch([w.at[:, pl.ds(at, 512)] for at in (512, 0, 1024) for w in (wm, wo)], buf, sem)
    gain, shift, branch = (vec[i + 2 * l:i + 1 + 2 * l, :] for i in (1, 5, 8))
    for j, mx in enumerate((mx0, mx1, mx2, mx3)):
        at = 256 * lax.rem(x + j, 4)
        for b in range(4):
            to = BLOCK * ((j + b) % 4)
            all_ref[to:to + BLOCK, pl.ds(pl.multiple_of(at, 128), 256)] = mx[BLOCK * b:BLOCK * (b + 1), :]
    if l == 0:
        keeps += send([(all_ref, all_out)], out_sem)
    mixed = all_ref[...]
    for i in range(2):
        core = c if i == 0 else 1 - c
        copies[i].wait()
        cols(m_ref, 512 * core, 512)[...] = dot(mixed, buf[i])
    for r in range(0, ROWS, 16):
        rows = slice(r, r + 16)
        m = h[rows, :] + m_ref[rows, :] + branch
        m_ref[rows, :] = m
        c_ref[rows, :] = (norm_parts(m)[0] * gain + shift).astype(BF)
    if l == 0:
        keeps += send([(c_ref, c_out)], out_sem.at[pl.ds(1, 1)])
    normed = c_ref[...]
    for i in range(2):
        core = c if i == 0 else 1 - c
        slope_part = cols(slope_ref, 512 * core, 512)
        g_part = cols(g_ref, 512 * core, 512)
        copies[2 + i].wait()
        u_ref[...] = dot(normed, buf[2 + i]) + up_bias[2 * l + i:2 * l + i + 1, :]
        for r in range(0, ROWS, 32):
            rows = pl.ds(r, 32)
            u = u_ref[rows, :]
            half = 0.5 + 0.5 * lax.erf(u * 0.7071067811865476)
            g_part[rows, :] = (u * half).astype(BF)
            slope_part[rows, :] = (half + u * (0.3989422804014327 * jnp.exp(-0.5 * u * u))).astype(BF)
    g = g_ref[...]
    for i in range(2):
        core = c if i == 0 else 1 - c
        copies[4 + i].wait()
        part = dot(g, buf[4 + i]).astype(BF)
        for j, out in enumerate((p0, p1, p2, p3)):
            cols(out, 512 * core, 512)[...] = part[BLOCK * j:BLOCK * (j + 1), :]
    for keep in keeps:
        keep.wait()


def sum_kernel(a, b, c, d, out, mark):
    mark[...] = jnp.zeros_like(mark)
    out[...] = (a[...].astype(F32) + b[...].astype(F32) + c[...].astype(F32) + d[...].astype(F32)).astype(BF)


def last_kernel(vec, m, a, b, c, d, out):
    got = sum(v[...].astype(F32) for v in (a, b, c, d))
    out[...] = (m[...] + got + vec[11:12, :]).astype(BF)


def mlp_back_kernel(ids, z0, z1, z2, z3, slope, wm, wo, dz_ref, du_ref, sum_ref, p0, p1, p2, p3, buf, sem):
    copies = fetch([w.at[:, pl.ds(at, 512)] for at in (1024, 0) for w in (wm, wo)], buf, sem)
    c = ids[1]
    for j, z in enumerate((z0, z1, z2, z3)):
        dz_ref[BLOCK * j:BLOCK * (j + 1), :] = z[...]
    copies[0].wait()
    copies[1].wait()
    dact = (dot_nt(cols(dz_ref, 512 * c, 512)[...], buf[0])
            + dot_nt(cols(dz_ref, 512 * (1 - c), 512)[...], buf[1]))
    du_ref[...] = (dact * slope[...].astype(F32)).astype(BF)
    copies[2].wait()
    copies[3].wait()
    part = (dot_nt(cols(du_ref, 512 * c, 512)[...], buf[2])
            + dot_nt(cols(du_ref, 512 * (1 - c), 512)[...], buf[3]))
    part = part.astype(BF)
    for j, out in enumerate((p0, p1, p2, p3)):
        out[...] = part[BLOCK * j:BLOCK * (j + 1), :]
    sums = jnp.sum(du_ref[...].astype(F32), axis=0, keepdims=True)
    sum_ref[...] = jnp.broadcast_to(sums, (8, D))


def norm_back_kernel(row, vec, base, above, e0, e1, e2, e3, d_ref, db_ref, sum_ref=None):
    gain = vec[row:row + 1, :]
    totals = [jnp.zeros((16, D), F32) for _ in range(4)]
    for r in range(0, BLOCK, 16):
        rows = slice(r, r + 16)
        e = e0[rows, :].astype(F32) + e1[rows, :].astype(F32) + e2[rows, :].astype(F32) + e3[rows, :].astype(F32)
        n, rstd = norm_parts(base[rows, :])
        eg = e * gain
        back = rstd * (eg - jnp.mean(eg, axis=-1, keepdims=True) - n * jnp.mean(eg * n, axis=-1, keepdims=True))
        up = above[rows, :]
        d = up + back
        db = d.astype(BF)
        d_ref[rows, :] = d
        db_ref[rows, :] = db
        if sum_ref is not None:
            for i, t in enumerate((e * n, e, db.astype(F32), up.astype(BF).astype(F32))):
                totals[i] = totals[i] + t
    if sum_ref is not None:
        out = [jnp.sum(t, axis=0, keepdims=True) for t in totals]
        sum_ref[...] = jnp.concatenate(out + out, axis=0)


def attend_back_kernel(ids, z0, z1, z2, z3, wm, wo, q_ref, lse_ref, *refs):
    kvs, (dmb_ref, dq_ref, dkv_ref, give_ref, buf, sem) = refs[:-6], refs[-6:]
    x, c = ids[0], ids[1]
    copies = fetch([w.at[pl.ds(pl.multiple_of(256 * x, 256), 256), pl.ds(512, 512)] for w in (wm, wo)], buf, sem)
    for j, z in enumerate((z0, z1, z2, z3)):
        dmb_ref[BLOCK * j:BLOCK * (j + 1), :] = z[:BLOCK, :]
    copies[0].wait()
    copies[1].wait()
    dmixed = (dot_nt(cols(dmb_ref, 512 * c, 512)[...], buf[0])
              + dot_nt(cols(dmb_ref, 512 * (1 - c), 512)[...], buf[1])).astype(BF)
    low = head_mask(ROWS, 0)
    keep = kept_keys(ids[0], ids[1])
    lane = lax.broadcasted_iota(jnp.int32, (ROWS, 128), 1)
    for pair in range(2):
        at = 128 * pair
        k, v = (jnp.concatenate([ref[:, i + at:i + at + 128] for ref in kvs], axis=0) for i in (0, 256))
        q = q_ref[:, at:at + 128]
        dmp = dmixed[:, at:at + 128]
        dqs = []
        dk = jnp.zeros((2 * ROWS, 128), F32)
        dv = jnp.zeros((2 * ROWS, 128), F32)
        for sub in range(2):
            mask = low if sub == 0 else ~low
            qm = jnp.where(mask, q, jnp.zeros_like(q))
            dmm = jnp.where(mask, dmp, jnp.zeros_like(dmp))
            lse = jnp.sum(jnp.where(lane == 2 * pair + sub, lse_ref[...], 0.0), axis=-1, keepdims=True)
            s = dot_nt(qm, k) * 0.125
            p = jnp.exp(jnp.where(keep, s, -1e9) - lse)
            dp = dot_nt(dmm, v)
            inner = jnp.sum(dp * p, axis=-1, keepdims=True)
            ds = (p * (dp - inner)).astype(BF)
            dqs.append(dot(ds, k))
            dk = dk + dot_tn(ds, qm)
            dv = dv + dot_tn(p.astype(BF), dmm)
        dq_ref[:, at:at + 128] = (jnp.where(low, dqs[0], dqs[1]) * 0.125).astype(BF)
        dk = dk * 0.125
        dkv_ref[:, at:at + 128] = dk[:ROWS]
        dkv_ref[:, 256 + at:384 + at] = dv[:ROWS]
        give_ref[:, at:at + 128] = dk[ROWS:].astype(BF)
        give_ref[:, 256 + at:384 + at] = dv[ROWS:].astype(BF)


def qkv_back_kernel(at, ids, dq, dkv, far, wm, wo, gm_ref, go_ref, sum_ref, p0, p1, p2, p3, buf, sem):
    c = ids[1]
    copies = fetch([w.at[:, pl.ds(at, 384)] for w in (wm, wo)], buf, sem)
    part = None
    sum_ref[...] = jnp.zeros((8, 512), F32)
    for i, g in enumerate((gm_ref, go_ref)):
        core = c if i == 0 else 1 - c
        g[:, :128] = cols(dq, 128 * core, 128)[...]
        g[:, 128:256] = (cols(dkv, 128 * core, 128)[...] + cols(far, 128 * core, 128)[...].astype(F32)).astype(BF)
        g[:, 256:] = (cols(dkv, 256 + 128 * core, 128)[...]
                      + cols(far, 256 + 128 * core, 128)[...].astype(F32)).astype(BF)
        copies[i].wait()
        got = dot_nt(g[...], buf[i])
        part = got if part is None else part + got
        total = jnp.sum(g[...].astype(F32), axis=0, keepdims=True)
        cols(sum_ref, 128 * core, 128)[0:1, :] = total[:, :128]
        cols(sum_ref, 256 + 128 * core, 128)[0:1, :] = total[:, 256:]
    part = part.astype(BF)
    for j, out in enumerate((p0, p1, p2, p3)):
        out[...] = part[BLOCK * j:BLOCK * (j + 1), :]


def mlp_grad_kernel(ids, normed, du, g, dz, mine_ref, other_ref):
    c = ids[1]
    for at, left, right in ((0, normed, du), (512, g, dz)):
        turned = left[...].T
        for i, out in enumerate((mine_ref, other_ref)):
            core = c if i == 0 else 1 - c
            out[:, at:at + 512] = dot(turned, cols(right, 512 * core, 512)[...]).astype(BF)


def out_grad_kernel(ids, mixed, z0, z1, z2, z3, mine_ref, other_ref):
    x, c = ids[0], ids[1]
    turned = mixed[...].T
    for i, out in enumerate((mine_ref, other_ref)):
        core = c if i == 0 else 1 - c
        dmb = jnp.concatenate([cols(z, 256 * x + 128 * core, 128)[:BLOCK, :] for z in (z0, z1, z2, z3)], axis=0)
        out[...] = dot(turned, dmb).astype(BF)


def qkv_grad_kernel(a, gm, go, h, p0, p1, p2, p3, mine_ref, other_ref, sum_ref):
    turned = a[...].T
    mine_ref[...] = dot(turned, gm[...]).astype(BF)
    other_ref[...] = dot(turned, go[...]).astype(BF)
    gain = jnp.zeros((16, D), F32)
    shift = jnp.zeros((16, D), F32)
    for j, p in enumerate((p0, p1, p2, p3)):
        for r in range(0, BLOCK, 16):
            e = p[r:r + 16, :].astype(F32)
            gain = gain + e * norm_parts(h[BLOCK * j + r:BLOCK * j + r + 16, :])[0]
            shift = shift + e
    out = [jnp.sum(t, axis=0, keepdims=True) for t in (gain, shift)]
    sum_ref[...] = jnp.concatenate(out * 4, axis=0)


def add_kernel(ids, *refs):
    pairs, outs, mark = refs[:-5], refs[-5:-1], refs[-1]
    mark[...] = jnp.zeros_like(mark)
    for k, out in enumerate(outs):
        y = lax.rem(ids[2] + k, 4)
        for z in range(4):
            rows = pl.ds(pl.multiple_of(64 * (4 * z + y), 64), 64)
            at = 0
            for mine, came in zip(pairs[::2], pairs[1::2]):
                width = mine.shape[1]
                out[z, :, at:at + width] = (mine[rows, :].astype(F32) + came[rows, :].astype(F32)).astype(BF)
                at += width


def middle_kernel(ids, a, b, c, d, *outs):
    outs, mark = outs[:-1], outs[-1]
    mark[...] = jnp.zeros_like(mark)
    for k, out in enumerate(outs):
        z = lax.rem(ids[3] + k, 4)
        out[...] = sum(v[z].astype(F32) for v in (a, b, c, d)).astype(BF)


def side_kernel(a, b, c, d, *refs):
    before, out, mark = refs[:-2], refs[-2], refs[-1]
    mark[...] = jnp.zeros_like(mark)
    at = 0
    for v in before:
        out[:, :v.shape[1]] = v[...]
        at = v.shape[1]
    out[:, at:] = sum(v[...].astype(F32) for v in (a, b, c, d)).astype(BF)


def total_kernel(*refs):
    out, mark, at = refs[-2], refs[-1], 0
    mark[...] = jnp.zeros_like(mark)
    for got in refs[:-2]:
        width = got.shape[2]
        total = got[0].astype(F32)
        for d in range(1, got.shape[0]):
            total = total + got[d].astype(F32)
        out[:, at:at + width] = total.astype(out.dtype)
        at += width


def write_gradient(name, layer, ref, all_ref, at):
    for core in range(2):
        if name == "up":
            for d in range(8):
                to = 256 * (8 * core + d)
                ref[layer, :, to:to + 256] = jnp.concatenate(
                    [all_ref[chip, core, :, at + 64 * d:at + 64 * (d + 1)] for chip in range(4)], axis=1).astype(F32)
        for chip in range(4):
            to = 256 * chip + 128 * core
            block = lambda i, width: all_ref[chip, core, :, at + i:at + i + width].astype(F32)
            if name == "down":
                ref[layer, 64 * chip:64 * (chip + 1), 512 * core:512 * (core + 1)] = block(0, 512)
            if name == "out":
                ref[layer, :, to:to + 128] = block(0, 128)
            if name == "qkv":
                for m in range(3):
                    ref[layer, :, D * m + to:D * m + to + 128] = block(128 * m, 128)


def arrange(ids, blocks, all_ref):
    x, c = ids[0], ids[1]
    for i in range(2):
        for j in range(4):
            all_ref[lax.rem(x + j, 4), c if i == 0 else 1 - c] = blocks[4 * i + j][...]


def early_kernel(ids, *refs):
    blocks, (up, down, out, qkv), all_ref = refs[:8], refs[8:12], refs[12]
    arrange(ids, blocks, all_ref)
    for name, layer, ref, at in (("up", 1, up, 0), ("down", 1, down, 512), ("out", 0, out, 1024), ("qkv", 0, qkv, 1152),
                                 ("up", 0, up, 1536), ("down", 0, down, 2048)):
        write_gradient(name, layer, ref, all_ref, at)


def late_kernel(ids, *refs):
    blocks, (out, qkv, gain_ref, shift_ref, branch_ref, qv_ref, up_ref), all_ref = refs[:8], refs[10:17], refs[17]
    arrange(ids, blocks, all_ref)
    write_gradient("out", 0, out, all_ref, 0)
    write_gradient("qkv", 0, qkv, all_ref, 128)
    part = [sum(all_ref[chip, core, 0:16, 512:].astype(F32) for core in range(2)) for chip in range(4)]
    total = part[0] + part[1] + part[2] + part[3]
    for l in range(2):
        for i, small in enumerate((gain_ref, shift_ref, branch_ref)):
            row = total[5 * l + i:5 * l + i + 1]
            small[l] = jnp.concatenate([row[:, :64], row[:, 64:]], axis=0)
        qv_ref[l:l + 1, :] = total[5 * l + 4:5 * l + 5]
        up_ref[l:l + 1, :] = jnp.concatenate([p[5 * l + 3:5 * l + 4, :64] for p in part], axis=1)


def finish(kernel, ids, blocks, outs, before=()):
    once = pl.Buffered(1)
    whole = lambda s: pl.BlockSpec(s, functools.partial(lambda n, _: (0,) * n, len(s)), pipeline_mode=once)
    out_specs = [whole(s) if n is None else pl.BlockSpec((n,) + s[1:], functools.partial(lambda at, _: (at, 0, 0), at),
                                                         pipeline_mode=once) for s, n, at in outs]
    return pl.pallas_call(
        kernel,
        grid=(1,),
        in_specs=[pl.BlockSpec(memory_space=pltpu.SMEM)] + [whole(b.shape) for b in blocks]
        + [pl.BlockSpec(memory_space=pl.ANY)] * len(before),
        out_specs=out_specs,
        out_shape=[pltpu.HBM(s, F32) for s, _, _ in outs],
        scratch_shapes=[pltpu.VMEM((4, 2) + blocks[0].shape, BF)],
        input_output_aliases={9 + i: i for i in range(len(before))},
        compiler_params=pltpu.CompilerParams(vmem_limit_bytes=LIMIT << 20),
        cost_estimate=pl.CostEstimate(flops=int(1.0 * 4e9), bytes_accessed=1, transcendentals=0),
    )(ids, *blocks, *before)


def rest_kernel(ids, out_mine, out_came, qkv_mine, qkv_came, *refs):
    x, out = ids[0], refs[-1]
    for d in range(16):
        at = slice(64 * d, 64 * (d + 1))
        out[d, :, :128] = (out_mine[at, :].astype(F32) + out_came[at, :].astype(F32)).astype(BF)
        out[d, :, 128:512] = (qkv_mine[at, :].astype(F32) + qkv_came[at, :].astype(F32)).astype(BF)
        rows = []
        for l in range(2):
            one, zero, up, qv = refs[4 * l:4 * l + 4]
            pair = lambda u, v: jnp.concatenate([u, v], axis=1)
            rows += [pair(zero[0:1, at], one[0:1, at]), pair(zero[1:2, at], one[1:2, at]),
                     pair(one[2:3, at], one[3:4, at]), pair(up[0:1, at], jnp.zeros((1, 64), F32))]
            lanes = 256 * (d // 8) + 128 * (d % 2)
            rows.append(jnp.where(x == d % 8 // 2, qv[0:1, lanes:lanes + 128], 0.0))
        out[d, :, 512:] = jnp.concatenate(rows + [jnp.zeros((54, 128), F32)], axis=0).astype(BF)


def later(v, *others):
    return lax.optimization_barrier((v, *others))


def over_dp(v):
    return lax.all_to_all(v, "dp", split_axis=0, concat_axis=0, tiled=True)


def shards(tokens, counts, cotangent, w_qkv, w_out, w_up, w_down, norm_gain, norm_shift,
           bias_qv, bias_up, bias_branch):
    s, dp = lax.axis_index("seq"), lax.axis_index("dp")
    ids = jnp.stack([s // 2, s % 2, dp % 4, dp // 4]).astype(jnp.int32)

    def compact(blocks):
        own, give = run(pick_kernel, [((ROWS, D), BF)] * 2, ids, counts, *blocks)
        return own, core_swap(give)

    def spread(blocks):
        own, give = run(place_kernel, [((128, D), BF)] * 2, ids, counts, *blocks)
        return (own + core_swap(give))[None]

    token_blocks = x_gather(tokens[0])
    first, rest0, rest1 = run(
        pack_kernel, [((64, 512), BF), ((64, 1920), BF), ((64, 1536), BF)], ids,
        away(w_qkv), away(w_out), away(w_up), away(w_down), away(norm_gain), away(norm_shift), away(bias_branch),
        away(bias_qv), away(bias_up),
        scratch=[pltpu.VMEM((64, 384), BF), pltpu.VMEM((2, 8, 64, 128), BF), pltpu.VMEM((3, 2, 2, 64), BF),
                 pltpu.VMEM((2, 128), BF), pltpu.VMEM((2, 256), BF), pltpu.SemaphoreType.DMA((31,))])
    rest0 = lax.all_gather(rest0, "dp", axis=0, tiled=True)
    rest1 = lax.all_gather(rest1, "dp", axis=0, tiled=True)
    source = list(compact(token_blocks))
    first, = run(order_kernel, [((4, 64, 512), BF)], ids, *dp_gather(first, 1), after=[source[0]])
    first, vec, qkv_bias, up_bias = run(
        unpack_kernel, [((D, 512), BF), ((16, D), F32), ((8, 384), F32), ((8, 512), F32)], ids, *dp_gather(first, 4),
        scratch=[pltpu.VMEM((16, 64, 512), BF)])
    first_far = core_swap(first)

    own, far = compact(x_gather(cotangent[0]))
    dz, dh, mark = run(join_kernel, in_hbm([((ROWS, D), BF), ((BLOCK, D), F32)]) + [MARK], own, far)
    dh = saved(dh)

    full = lambda *dtypes: [((ROWS, D), t) for t in dtypes]
    sent = [((BLOCK, D), BF)] * 4
    kept = []
    for l in range(2):
        outs = full(F32, BF) + [((ROWS, 256), BF), ((ROWS, 512), BF)]
        if l == 0:
            hidden, a, q, kv = run(functools.partial(qkv_kernel, l), outs, ids, vec, qkv_bias, *source, first, first_far,
                                   after=[mark], us=2)
        else:
            hidden, a, q, kv, middle0, g0, slope0 = run(
                functools.partial(qkv_kernel, l), outs + [((BLOCK, D), F32, "away")] + [((ROWS, D), BF, "away")] * 2,
                ids, vec, qkv_bias, *source, g, slope, *rests[0], scratch=held(2, D, 384) + [pltpu.SemaphoreType.DMA((3,))], us=3)
            kept[0][-3:] = [saved(v) for v in (middle0, g0, slope0)]
        kv_far = core_swap(kv)
        outs = [((ROWS, 256), BF), ((ROWS, 128), F32)]
        if l == 0:
            mixed, lse, q, kv, hidden, a, first, first_far = run(
                attend_kernel, outs + [(s, t, "away") for s, t in (
                    ((ROWS, 256), BF), ((2 * ROWS, 512), BF), ((ROWS, D), F32), ((ROWS, D), BF), ((D, 512), BF), ((D, 512), BF))],
                ids, q, kv, kv_far, hidden, a, first, first_far, scratch=[pltpu.SemaphoreType.DMA((7,))], us=4)
            rest0, lse = later(rest0, lse)
            rests = [[away(rest0), ("any", core_swap(rest0))]]
            hidden, a, q, kvs, lse = saved(hidden), saved(a), saved(q), [saved(kv)], saved(lse)
        else:
            mixed, lse = run(attend_kernel, outs, ids, q, kv, kv_far, us=3)
            kvs = [kv, kv_far]
            rest1, lse = later(rest1, lse)
            rests.append([away(rest1), ("any", core_swap(rest1))])
        mixes = x_gather(mixed)
        outs = [((ROWS, D), BF, "away")] * 2 if l == 0 else full(BF, BF)
        extra = [pltpu.VMEM((ROWS, D), BF)] * 2 + [pltpu.SemaphoreType.DMA((2,))] if l == 0 else []
        all_mixed, normed, middle, g, slope, *parts = run(
            functools.partial(mlp_kernel, l), outs + full(F32, BF, BF) + sent, ids, vec, up_bias, *mixes, hidden, *rests[l],
            scratch=[pltpu.VMEM((ROWS, 512), F32)] + held(6, D, 512) + extra, us=6)
        if l == 0:
            all_mixed, normed = saved(all_mixed), saved(normed)
            mlp, mark = run(sum_kernel, [((BLOCK, D), BF), LOOSE], *x_scatter(parts))
            source = [middle, *x_gather(mlp)]
        kept.append([hidden, a, q, kvs, lse, all_mixed, normed, middle, g, slope])

    dz = [(saved(dz), (BLOCK, D), (j, 0)) for j in range(4)]
    swapped = lambda v: v + [core_swap(b) for b in v]
    last_parts, last_rows = parts, (middle, (BLOCK, D), (0, 0))
    rests[0][1] = away(rests[0][1][1])
    tiny = []
    for l in (1, 0):
        hidden, a, q, kvs, lse, all_mixed, normed, middle, g, slope = kept[l]
        keep = lambda v: v if isinstance(v, tuple) else saved(v)
        qkv = rests[0] if l else [away(first), away(first_far)]
        top = lambda v: (v, (BLOCK, D), (0, 0))
        dz_all, du, up_sum, *parts = run(
            mlp_back_kernel, full(BF, BF) + [((8, D), F32)] + sent, ids, *dz, slope, *rests[l], scratch=held(4, D, 512),
            after=[mark5] if l == 0 else (), us=4)
        errs = x_scatter(parts)
        mlp_mine, mlp_other = run(mlp_grad_kernel, [((D, D), BF, "saved"), ((D, D), BF)], ids, normed, du, g, dz_all, us=4)
        dm, dmb, sums1 = run(functools.partial(norm_back_kernel, 2 * l + 1),
                             [((BLOCK, D), F32), ((BLOCK, D), BF), ((8, D), F32)], vec, top(middle), dh, *errs,
                             after=[mlp_mine])
        mlp_came = core_swap(mlp_other)
        dmbs = x_gather(dmb)
        before = []
        if l == 0:
            shares1 = dp_scatter(shares1, 4)
            *shares, mark = run(add_kernel, [((4, 64, D), BF)] * 4 + [LOOSE], ids, saved(mlp_mine), mlp_came, us=3)
            came = dp_scatter(shares, 1)
            before = [mark, mark7]
        dmb_all, dq, dkv, give = run(
            attend_back_kernel, full(BF) + [((ROWS, 256), BF), ((ROWS, 512), F32), ((ROWS, 512), BF)],
            ids, *dmbs, *rests[l], q, lse, *kvs, scratch=held(2, 256, 512), after=before, us=5)
        give = core_swap(give)
        out_mine, out_other = run(out_grad_kernel, [((D, 128), BF, "saved"), ((D, 128), BF)], ids, all_mixed, *dmbs, us=2)
        out_came = core_swap(out_other)
        before = []
        if l == 1:
            last, = run(last_kernel, [((BLOCK, D), BF)], vec, last_rows, *x_scatter(last_parts))
        gm, go, qv_sum, *parts = run(
            functools.partial(qkv_back_kernel, 1536 * l), [((ROWS, 384), BF)] * 2 + [((8, 512), F32)] + sent,
            ids, dq, dkv, give, *qkv, scratch=held(2, D, 384), us=3)
        errs = x_scatter(parts)
        qkv_mine, qkv_other, sums0 = run(qkv_grad_kernel, [((D, 384), BF, "saved"), ((D, 384), BF), ((8, D), F32)],
                                         keep(a), gm, go, keep(hidden), *parts, us=4)
        tiny = [sums1, sums0, up_sum, qv_sum] + tiny
        before = [out_mine, qkv_mine]
        qkv_came = core_swap(qkv_other)
        rest_pairs = [saved(out_mine), out_came, saved(qkv_mine), qkv_came]
        if l == 1:
            *shares, mark5 = run(add_kernel, [((4, 64, 1536), BF)] * 4 + [LOOSE], ids, saved(mlp_mine), mlp_came, *rest_pairs, us=4)
            came = dp_scatter(shares, 1)
        else:
            *shares, _ = run(middle_kernel, [((64, D), BF)] * 4 + [LOOSE], ids, *came, us=1)
            came = dp_scatter(shares, 4)
            total1, mark = run(side_kernel, [((64, 1536), BF), LOOSE], *shares1)
            rest, = run(rest_kernel, in_hbm([((16, 64, 640), BF)]), ids, *rest_pairs, *tiny, us=3)
            got_rest = over_dp(rest)
            before = [rest, mark]
        dh, dz = run(functools.partial(norm_back_kernel, 2 * l),
                     [((BLOCK, D), F32), ((BLOCK, D), BF)], vec, top(hidden), dm, *errs, after=before)
        dz = x_gather(dz)
        if l == 1:
            *shares1, mark7 = run(middle_kernel, [((64, 1536), BF)] * 4 + [LOOSE], ids, *came, us=2)
            lasts = x_gather(last)
        else:
            total, _ = run(side_kernel, [((64, 2560), BF), LOOSE], *came, total1)
    output = spread(lasts)
    g_up, g_down, g_out, g_qkv = finish(
        early_kernel, ids, swapped(x_gather(total)),
        [((2, 64, 4096), 2, 0), ((2, 256, 1024), 2, 0), ((2, 64, 1024), 1, 1), ((2, 64, 3072), 1, 1)])
    total_rest, _ = run(total_kernel, [((64, 640), BF), LOOSE], got_rest)
    grad_tokens = spread(dz)
    g_out, g_qkv, g_gain, g_shift, g_branch, g_qv, g_upb = finish(
        late_kernel, ids, swapped(x_gather(total_rest)),
        [((2, 64, 1024), 1, 0), ((2, 64, 3072), 1, 0)] + [((2, 2, 64), None, 0)] * 3 + [((2, 128), None, 0), ((2, 256), None, 0)],
        (g_out, g_qkv))
    return (output, grad_tokens, g_qkv, g_out, g_up, g_down, g_gain, g_shift, g_qv, g_upb, g_branch)


def solution(mesh):
    rows = P("dp", "seq", None)
    mid = P(None, "dp", None)
    end = P(None, None, "dp")
    two = P(None, "dp")
    return jax.shard_map(
        shards,
        mesh=mesh,
        in_specs=(rows, P("dp", None), rows, mid, mid, mid, mid, end, end, two, two, end),
        out_specs=(rows, rows, mid, mid, mid, mid, end, end, two, two, end),
        check_vma=False,
    )
```

```python
import functools

import jax
import jax.numpy as jnp
from jax import lax
from jax.experimental import pallas as pl
from jax.experimental.pallas import tpu as pltpu
from jax.sharding import PartitionSpec as P

EPSILON = 1e-06
BF = jnp.bfloat16
F32 = jnp.float32
BLOCK = 80
SHARE = 73
TOTAL = 577
ROWS = 4 * BLOCK
D = 1024
LOOSE = ((8, 128), jnp.float32)
MARK = ((8, 128), jnp.float32, "saved")
LIMIT = 24

NEXT = [(i, (i + 2) % 8) for i in range(8)]
PREV = [(i, (i - 2) % 8) for i in range(8)]
FAR = [(i, (i + 4) % 8) for i in range(8)]
CORE = [(i, i ^ 1) for i in range(8)]


def x_gather(block):
    return [
        block,
        lax.ppermute(block, "seq", PREV),
        lax.ppermute(block, "seq", FAR),
        lax.ppermute(block, "seq", NEXT),
    ]


def x_scatter(blocks):
    return [
        blocks[0],
        lax.ppermute(blocks[1], "seq", NEXT),
        lax.ppermute(blocks[2], "seq", FAR),
        lax.ppermute(blocks[3], "seq", PREV),
    ]


def core_swap(v):
    return lax.ppermute(v, "seq", CORE)


def dp_pairs(step, k):
    if step == 1:
        return [(i, i // 4 * 4 + (i + k) % 4) for i in range(16)]
    return [(i, (i + 4 * k) % 16) for i in range(16)]


def dp_scatter(blocks, step):
    return [blocks[0]] + [lax.ppermute(blocks[k], "dp", dp_pairs(step, k)) for k in (1, 2, 3)]


def dp_gather(block, step):
    return [block] + [lax.ppermute(block, "dp", dp_pairs(step, -k)) for k in (1, 2, 3)]


def dot(a, b):
    return jnp.dot(a, b, preferred_element_type=F32)


def dot_nt(a, b):
    return lax.dot_general(a, b, (((1,), (1,)), ((), ())), preferred_element_type=F32)


def dot_tn(a, b):
    return lax.dot_general(a, b, (((0,), (0,)), ((), ())), preferred_element_type=F32)


def cols(ref, at, width):
    return ref.at[:, pl.ds(pl.multiple_of(at, 128), width)]


def norm_parts(rows):
    mean = jnp.mean(rows, axis=-1, keepdims=True)
    centered = rows - mean
    rstd = lax.rsqrt(jnp.mean(centered * centered, axis=-1, keepdims=True) + EPSILON)
    return centered * rstd, rstd


def away(v):
    return ("away", v)


def saved(v):
    return ("saved", v)


def in_hbm(outs):
    return [o + ("saved",) for o in outs]


def run(kernel, outs, *ins, scratch=(), after=(), us=1.0):
    once = pl.Buffered(1)
    small = lambda v: v.size < 100000
    hbm = lambda v: pltpu.with_memory_space_constraint(v, pltpu.HBM)
    whole = lambda s: pl.BlockSpec(s, functools.partial(lambda n, _: (0,) * n, len(s)), pipeline_mode=once)
    specs, arrays = [], []
    for v in ins:
        if isinstance(v, tuple) and len(v) == 2:
            kind, v = v
            specs.append(whole(v.shape) if kind == "saved" else pl.BlockSpec(memory_space=pl.ANY if kind == "any" else pltpu.HBM))
            v = v if kind == "any" else hbm(v)
        elif isinstance(v, tuple):
            v, block, index = v
            specs.append(pl.BlockSpec(block, functools.partial(lambda at, _: at, index), pipeline_mode=once))
            if isinstance(v, tuple):
                v = hbm(v[1])
        elif v.dtype == jnp.int32:
            specs.append(pl.BlockSpec(memory_space=pltpu.SMEM))
        else:
            specs.append(whole(v.shape))
        arrays.append(v)
    specs += [pl.BlockSpec(memory_space=pl.ANY if small(v) else pltpu.HBM) for v in after]
    n = len(arrays)
    body = lambda *refs: kernel(*refs[:n], *refs[n + len(after):])
    kinds = [o[2] if len(o) > 2 else "" for o in outs]
    return pl.pallas_call(
        body,
        grid=(1,),
        in_specs=specs,
        out_specs=[pl.BlockSpec(memory_space=pltpu.HBM) if k == "away" else whole(o[0]) for k, o in zip(kinds, outs)],
        out_shape=[pltpu.HBM(o[0], o[1]) if k else jax.ShapeDtypeStruct(o[0], o[1]) for k, o in zip(kinds, outs)],
        scratch_shapes=list(scratch),
        compiler_params=pltpu.CompilerParams(vmem_limit_bytes=LIMIT << 20),
        cost_estimate=pl.CostEstimate(flops=int(us * 1.0 * 1.15e9), bytes_accessed=1, transcendentals=0),
    )(*arrays, *[v if small(v) else hbm(v) for v in after])


def fetch(parts, buf, sem):
    copies = [pltpu.make_async_copy(v, buf.at[i], sem.at[i]) for i, v in enumerate(parts)]
    for copy in copies:
        copy.start()
    return copies


def send(pairs, sem):
    copies = [pltpu.make_async_copy(v, out, sem.at[i]) for i, (v, out) in enumerate(pairs)]
    for copy in copies:
        copy.start()
    return copies


def held(count, rows, width):
    return [pltpu.VMEM((count, rows, width), BF), pltpu.SemaphoreType.DMA((count,))]


def half_ranks(shape, axis, x, core):
    at = lax.broadcasted_iota(jnp.int32, shape, axis)
    block = sum((at >= BLOCK * i).astype(jnp.int32) for i in (1, 2, 3))
    within = at - BLOCK * block
    chip = x + block
    chip = jnp.where(chip >= 4, chip - 4, chip)
    rank = (4 * core + chip) * SHARE + within
    return jnp.where((within < SHARE) & (rank < TOTAL), rank, -2)


def slot_ranks(shape, axis, counts, s):
    at = lax.broadcasted_iota(jnp.int32, shape, axis)
    start = sum(jnp.where(i < s, counts[0, i], 0) for i in range(8))
    return jnp.where(at < counts[0, s], start + at, -1)


def kept_keys(x, c):
    at = lax.broadcasted_iota(jnp.int32, (1, 2 * ROWS), 1)
    second = (at >= ROWS).astype(jnp.int32)
    at = at - ROWS * second
    block = sum((at >= BLOCK * i).astype(jnp.int32) for i in (1, 2, 3))
    chip = x + block
    chip = jnp.where(chip >= 4, chip - 4, chip)
    core = jnp.where(second > 0, 1 - c, c)
    within = at - BLOCK * block
    return (within < SHARE) & ((4 * core + chip) * SHARE + within < TOTAL)


def pick_kernel(ids, counts, t0, t1, t2, t3, own_ref, far_ref):
    x, c = ids[0], ids[1]
    rows = jnp.concatenate([t[...] for t in (t0, t1, t2, t3)], axis=0)
    slots = [slot_ranks((1, 128), 1, counts, 2 * lax.rem(x + j, 4) + c) for j in range(4)]
    for core, out in ((c, own_ref), (1 - c, far_ref)):
        rank = half_ranks((ROWS, 1), 0, x, core)
        pick = jnp.concatenate([jnp.where(rank == s, 1.0, 0.0) for s in slots], axis=1)
        out[...] = dot(pick.astype(BF), rows).astype(BF)


def join_kernel(own, far, dz_ref, dh_ref, mark):
    mark[...] = jnp.zeros_like(mark)
    dz = own[...] + far[...]
    dz_ref[...] = dz
    dh_ref[...] = dz[:BLOCK, :].astype(F32)


def pack_kernel(ids, w_qkv, w_out, w_up, w_down, gain, shift, branch, qv, up,
                first_ref, rest0_ref, rest1_ref, qkv_buf, up_buf, norm_buf, qv_buf, wide_buf, sem):
    x, c = ids[0], ids[1]
    lanes = lambda at, width: pl.ds(pl.multiple_of(at, 128), width)
    copies = []

    def copy(source, target):
        copies.append(pltpu.make_async_copy(source, target, sem.at[len(copies)]))
        copies[-1].start()

    rests = (rest0_ref, rest1_ref)
    for l in range(2):
        for m in range(3):
            target = qkv_buf.at[:, pl.ds(128 * m, 128)] if l == 0 else rest0_ref.at[:, pl.ds(1536 + 128 * m, 128)]
            copy(w_qkv.at[l, :, lanes(D * m + 256 * x + 128 * c, 128)], target)
        for d in range(8):
            copy(w_up.at[l, :, lanes(2048 * c + 256 * d + 128 * (x // 2), 128)], up_buf.at[l, d])
        copy(w_out.at[l, :, lanes(512 * c, 512)], rests[l].at[:, pl.ds(512, 512)])
        copy(w_down.at[l, pl.ds(pl.multiple_of(64 * x, 64), 64), lanes(512 * c, 512)], rests[l].at[:, pl.ds(1024, 512)])
    for i, v in enumerate((gain, shift, branch)):
        copy(v, norm_buf.at[i])
    copy(qv, qv_buf)
    copy(up, wide_buf)
    for each in copies:
        each.wait()
    pairs = lambda i: jnp.concatenate([norm_buf[i, 0], norm_buf[i, 1]], axis=0).astype(F32)
    wide = wide_buf[...].astype(F32)
    small = jnp.concatenate([
        jnp.concatenate([pairs(0), pairs(1)], axis=1),
        jnp.concatenate([pairs(2), jnp.zeros((4, 64), F32)], axis=1),
        qv_buf[...].astype(F32),
        wide[0:1, :128], wide[0:1, 128:], wide[1:2, :128], wide[1:2, 128:],
        jnp.zeros((50, 128), F32)], axis=0).astype(BF)
    block = jnp.concatenate([qkv_buf[...], small], axis=1)
    first_ref[...] = block
    odd = lax.rem(x, 2) == 1
    for l in range(2):
        got = []
        for d in range(8):
            piece = up_buf[l, d].astype(F32)
            got.append(jnp.where(odd, piece[:, 64:], piece[:, :64]))
        rests[l][:, :512] = jnp.concatenate(got, axis=1).astype(BF)


def order_kernel(ids, a, b, c, d, out):
    for i, v in enumerate((a, b, c, d)):
        out[lax.rem(ids[2] + i, 4)] = v[...]


def unpack_kernel(ids, a, b, c, d, first_ref, vec_ref, qkv_ref, up_ref, first):
    for i, v in enumerate((a, b, c, d)):
        for y in range(4):
            first[4 * lax.rem(ids[3] + i, 4) + y] = v[y]
    for i in range(16):
        first_ref[64 * i:64 * (i + 1), :] = first[i]
    x, c = ids[0], ids[1]
    rows = [first[d, 0:16, 384:].astype(F32) for d in range(16)]
    line = lambda at, lanes: jnp.concatenate([r[at:at + 4, lanes:lanes + 64] for r in rows], axis=1)
    vec_ref[...] = jnp.concatenate([line(0, 0), line(0, 64), line(4, 0), jnp.zeros((4, D), F32)], axis=0)
    qkv, up = [], []
    for l in range(2):
        for core in (c, 1 - c):
            q = first[2 * x + core, 0:16, 384:].astype(F32)[8 + l:9 + l]
            v = first[8 + 2 * x + core, 0:16, 384:].astype(F32)[8 + l:9 + l]
            qkv.append(jnp.concatenate([q, jnp.zeros((1, 128), F32), v], axis=1))
            got = []
            for d in range(8):
                r = first[8 * core + d, 0:16, 384:].astype(F32)
                r = jnp.where(x >= 2, r[11 + 2 * l:12 + 2 * l], r[10 + 2 * l:11 + 2 * l])
                got.append(jnp.where(lax.rem(x, 2) == 1, r[:, 64:], r[:, :64]))
            up.append(jnp.concatenate(got, axis=1))
    qkv_ref[...] = jnp.concatenate(qkv + [jnp.zeros((4, 384), F32)], axis=0)
    up_ref[...] = jnp.concatenate(up + [jnp.zeros((4, 512), F32)], axis=0)


def qkv_kernel(l, ids, vec, bias, *refs):
    gain, shift = vec[2 * l:2 * l + 1, :], vec[4 + 2 * l:5 + 2 * l, :]
    first = l == 0
    keeps = []
    if first:
        own, far, wm, wo, h_ref, a_ref, q_ref, kv_ref = refs
        weight = lambda i: (wm, wo)[i][:, :384]
    else:
        (m, d0, d1, d2, d3, g, slope, wm, wo, h_ref, a_ref, q_ref, kv_ref,
         m_out, g_out, slope_out, buf, sem, out_sem) = refs
        branch = vec[9:10, :]
        copies = fetch([w.at[:, pl.ds(1536, 384)] for w in (wm, wo)], buf, sem)
        keeps = send([(m.at[pl.ds(0, BLOCK), :], m_out), (g, g_out), (slope, slope_out)], out_sem)

        def weight(i):
            copies[i].wait()
            return buf[i]

    c = ids[1]
    for r in range(0, ROWS, 16):
        rows = slice(r, r + 16)
        if first:
            h = own[rows, :].astype(F32) + far[rows, :].astype(F32)
        else:
            b, o = divmod(r, BLOCK)
            h = m[rows, :] + (d0, d1, d2, d3)[b][o:o + 16, :].astype(F32) + branch
        h_ref[rows, :] = h
        a_ref[rows, :] = (norm_parts(h)[0] * gain + shift).astype(BF)
    a = a_ref[...]
    for i in range(2):
        core = c if i == 0 else 1 - c
        packed = (dot(a, weight(i)) + bias[2 * l + i:2 * l + i + 1, :]).astype(BF)
        cols(q_ref, 128 * core, 128)[...] = packed[:, :128]
        cols(kv_ref, 128 * core, 128)[...] = packed[:, 128:256]
        cols(kv_ref, 256 + 128 * core, 128)[...] = packed[:, 256:]
    for keep in keeps:
        keep.wait()


def head_mask(rows, sub):
    lane = lax.broadcasted_iota(jnp.int32, (rows, 128), 1)
    return (lane < 64) if sub == 0 else (lane >= 64)


def attend_kernel(ids, q_ref, kv_ref, far_ref, *refs):
    keeps = []
    if len(refs) == 2:
        mixed_ref, lse_ref = refs
    else:
        n = (len(refs) - 5) // 2
        mixed_ref, lse_ref = refs[n:n + 2]
        outs, sem = refs[n + 2:-1], refs[-1]
        keeps = send([(q_ref, outs[0]), (kv_ref, outs[1].at[pl.ds(0, ROWS), :]),
                      (far_ref, outs[1].at[pl.ds(ROWS, ROWS), :])], sem)
        keeps += send(list(zip(refs[:n], outs[2:])), sem.at[pl.ds(3, n)])
    low = head_mask(ROWS, 0)
    keep = kept_keys(ids[0], ids[1])
    lane = lax.broadcasted_iota(jnp.int32, (ROWS, 128), 1)
    lses = jnp.zeros((ROWS, 128), F32)
    for pair in range(2):
        at = 128 * pair
        k = jnp.concatenate([kv_ref[:, at:at + 128], far_ref[:, at:at + 128]], axis=0)
        v = jnp.concatenate([kv_ref[:, 256 + at:384 + at], far_ref[:, 256 + at:384 + at]], axis=0)
        q = q_ref[:, at:at + 128]
        got = []
        for sub in range(2):
            qm = jnp.where(low if sub == 0 else ~low, q, jnp.zeros_like(q))
            s = dot_nt(qm, k) * 0.125
            s = jnp.where(keep, s, -1e9)
            top = jnp.max(s, axis=-1, keepdims=True)
            e = jnp.exp(s - top)
            total = jnp.sum(e, axis=-1, keepdims=True)
            got.append(dot((e * (1.0 / total)).astype(BF), v))
            lses = jnp.where(lane == 2 * pair + sub, top + jnp.log(total), lses)
        mixed_ref[:, at:at + 128] = jnp.where(low, got[0], got[1]).astype(BF)
    lse_ref[...] = lses
    for keep in keeps:
        keep.wait()


def mlp_kernel(l, ids, vec, up_bias, mx0, mx1, mx2, mx3, h, wm, wo, *refs):
    x, c = ids[0], ids[1]
    keeps = []
    if l == 0:
        (all_out, c_out, m_ref, g_ref, slope_ref, p0, p1, p2, p3,
         u_ref, buf, sem, all_ref, c_ref, out_sem) = refs
    else:
        all_ref, c_ref, m_ref, g_ref, slope_ref, p0, p1, p2, p3, u_ref, buf, sem = refs
    copies = fetch([w.at[:, pl.ds(at, 512)] for at in (512, 0, 1024) for w in (wm, wo)], buf, sem)
    gain, shift, branch = (vec[i + 2 * l:i + 1 + 2 * l, :] for i in (1, 5, 8))
    for j, mx in enumerate((mx0, mx1, mx2, mx3)):
        at = 256 * lax.rem(x + j, 4)
        for b in range(4):
            to = BLOCK * ((j + b) % 4)
            all_ref[to:to + BLOCK, pl.ds(pl.multiple_of(at, 128), 256)] = mx[BLOCK * b:BLOCK * (b + 1), :]
    if l == 0:
        keeps += send([(all_ref, all_out)], out_sem)
    mixed = all_ref[...]
    for i in range(2):
        core = c if i == 0 else 1 - c
        copies[i].wait()
        cols(m_ref, 512 * core, 512)[...] = dot(mixed, buf[i])
    for r in range(0, ROWS, 16):
        rows = slice(r, r + 16)
        m = h[rows, :] + m_ref[rows, :] + branch
        m_ref[rows, :] = m
        c_ref[rows, :] = (norm_parts(m)[0] * gain + shift).astype(BF)
    if l == 0:
        keeps += send([(c_ref, c_out)], out_sem.at[pl.ds(1, 1)])
    normed = c_ref[...]
    for i in range(2):
        core = c if i == 0 else 1 - c
        slope_part = cols(slope_ref, 512 * core, 512)
        g_part = cols(g_ref, 512 * core, 512)
        copies[2 + i].wait()
        u_ref[...] = dot(normed, buf[2 + i]) + up_bias[2 * l + i:2 * l + i + 1, :]
        for r in range(0, ROWS, 32):
            rows = pl.ds(r, 32)
            u = u_ref[rows, :]
            half = 0.5 + 0.5 * lax.erf(u * 0.7071067811865476)
            g_part[rows, :] = (u * half).astype(BF)
            slope_part[rows, :] = (half + u * (0.3989422804014327 * jnp.exp(-0.5 * u * u))).astype(BF)
    g = g_ref[...]
    for i in range(2):
        core = c if i == 0 else 1 - c
        copies[4 + i].wait()
        part = dot(g, buf[4 + i]).astype(BF)
        for j, out in enumerate((p0, p1, p2, p3)):
            cols(out, 512 * core, 512)[...] = part[BLOCK * j:BLOCK * (j + 1), :]
    for keep in keeps:
        keep.wait()


def sum_kernel(a, b, c, d, out, mark):
    mark[...] = jnp.zeros_like(mark)
    out[...] = (a[...].astype(F32) + b[...].astype(F32) + c[...].astype(F32) + d[...].astype(F32)).astype(BF)


def mlp_back_kernel(ids, z0, z1, z2, z3, slope, wm, wo, dz_ref, du_ref, sum_ref, p0, p1, p2, p3, buf, sem):
    copies = fetch([w.at[:, pl.ds(at, 512)] for at in (1024, 0) for w in (wm, wo)], buf, sem)
    c = ids[1]
    for j, z in enumerate((z0, z1, z2, z3)):
        dz_ref[BLOCK * j:BLOCK * (j + 1), :] = z[...]
    copies[0].wait()
    copies[1].wait()
    dact = (dot_nt(cols(dz_ref, 512 * c, 512)[...], buf[0])
            + dot_nt(cols(dz_ref, 512 * (1 - c), 512)[...], buf[1]))
    du_ref[...] = (dact * slope[...].astype(F32)).astype(BF)
    copies[2].wait()
    copies[3].wait()
    part = (dot_nt(cols(du_ref, 512 * c, 512)[...], buf[2])
            + dot_nt(cols(du_ref, 512 * (1 - c), 512)[...], buf[3]))
    part = part.astype(BF)
    for j, out in enumerate((p0, p1, p2, p3)):
        out[...] = part[BLOCK * j:BLOCK * (j + 1), :]
    sums = jnp.sum(du_ref[...].astype(F32), axis=0, keepdims=True)
    sum_ref[...] = jnp.broadcast_to(sums, (8, D))


def norm_back_kernel(row, vec, base, above, e0, e1, e2, e3, *refs):
    final = len(refs) == 3 and refs[2].shape[0] > BLOCK
    if final:
        last, got, db_ref = refs
    else:
        d_ref, db_ref, sum_ref = refs if len(refs) == 3 else (*refs, None)
    gain = vec[row:row + 1, :]
    totals = [jnp.zeros((16, D), F32) for _ in range(4)]
    for r in range(0, BLOCK, 16):
        rows = slice(r, r + 16)
        e = e0[rows, :].astype(F32) + e1[rows, :].astype(F32) + e2[rows, :].astype(F32) + e3[rows, :].astype(F32)
        n, rstd = norm_parts(base[rows, :])
        eg = e * gain
        back = rstd * (eg - jnp.mean(eg, axis=-1, keepdims=True) - n * jnp.mean(eg * n, axis=-1, keepdims=True))
        up = above[rows, :]
        d = up + back
        db = d.astype(BF)
        db_ref[rows, :] = db
        if final:
            late = slice(BLOCK + r, BLOCK + r + 16)
            sums = sum(v[late, :].astype(F32) for v in (e0, e1, e2, e3))
            db_ref[late, :] = (last[rows, :] + sums + vec[11:12, :]).astype(BF)
            continue
        d_ref[rows, :] = d
        if sum_ref is not None:
            for i, t in enumerate((e * n, e, db.astype(F32), up.astype(BF).astype(F32))):
                totals[i] = totals[i] + t
    if final:
        total = got[0].astype(F32)
        for d in range(1, 16):
            total = total + got[d].astype(F32)
        db_ref[2 * BLOCK:, :] = total.astype(BF)
    elif sum_ref is not None:
        out = [jnp.sum(t, axis=0, keepdims=True) for t in totals]
        sum_ref[...] = jnp.concatenate(out + out, axis=0)


def attend_back_kernel(ids, z0, z1, z2, z3, wm, wo, q_ref, lse_ref, *refs):
    kvs, (dmb_ref, dq_ref, dkv_ref, give_ref, buf, sem) = refs[:-6], refs[-6:]
    x, c = ids[0], ids[1]
    copies = fetch([w.at[pl.ds(pl.multiple_of(256 * x, 256), 256), pl.ds(512, 512)] for w in (wm, wo)], buf, sem)
    for j, z in enumerate((z0, z1, z2, z3)):
        dmb_ref[BLOCK * j:BLOCK * (j + 1), :] = z[:BLOCK, :]
    copies[0].wait()
    copies[1].wait()
    dmixed = (dot_nt(cols(dmb_ref, 512 * c, 512)[...], buf[0])
              + dot_nt(cols(dmb_ref, 512 * (1 - c), 512)[...], buf[1])).astype(BF)
    low = head_mask(ROWS, 0)
    keep = kept_keys(ids[0], ids[1])
    lane = lax.broadcasted_iota(jnp.int32, (ROWS, 128), 1)
    for pair in range(2):
        at = 128 * pair
        k, v = (jnp.concatenate([ref[:, i + at:i + at + 128] for ref in kvs], axis=0) for i in (0, 256))
        q = q_ref[:, at:at + 128]
        dmp = dmixed[:, at:at + 128]
        dqs = []
        dk = jnp.zeros((2 * ROWS, 128), F32)
        dv = jnp.zeros((2 * ROWS, 128), F32)
        for sub in range(2):
            mask = low if sub == 0 else ~low
            qm = jnp.where(mask, q, jnp.zeros_like(q))
            dmm = jnp.where(mask, dmp, jnp.zeros_like(dmp))
            lse = jnp.sum(jnp.where(lane == 2 * pair + sub, lse_ref[...], 0.0), axis=-1, keepdims=True)
            s = dot_nt(qm, k) * 0.125
            p = jnp.exp(jnp.where(keep, s, -1e9) - lse)
            dp = dot_nt(dmm, v)
            inner = jnp.sum(dp * p, axis=-1, keepdims=True)
            ds = (p * (dp - inner)).astype(BF)
            dqs.append(dot(ds, k))
            dk = dk + dot_tn(ds, qm)
            dv = dv + dot_tn(p.astype(BF), dmm)
        dq_ref[:, at:at + 128] = (jnp.where(low, dqs[0], dqs[1]) * 0.125).astype(BF)
        dk = dk * 0.125
        dkv_ref[:, at:at + 128] = dk[:ROWS]
        dkv_ref[:, 256 + at:384 + at] = dv[:ROWS]
        give_ref[:, at:at + 128] = dk[ROWS:].astype(BF)
        give_ref[:, 256 + at:384 + at] = dv[ROWS:].astype(BF)


def qkv_back_kernel(at, ids, dq, dkv, far, wm, wo, *refs):
    lasts, (gm_ref, go_ref, sum_ref, p0, p1, p2, p3, buf, sem) = refs[:-9], refs[-9:]
    c = ids[1]
    copies = fetch([w.at[:, pl.ds(at, 384)] for w in (wm, wo)], buf, sem)
    part = None
    sum_ref[...] = jnp.zeros((8, 512), F32)
    for i, g in enumerate((gm_ref, go_ref)):
        core = c if i == 0 else 1 - c
        g[:, :128] = cols(dq, 128 * core, 128)[...]
        g[:, 128:256] = (cols(dkv, 128 * core, 128)[...] + cols(far, 128 * core, 128)[...].astype(F32)).astype(BF)
        g[:, 256:] = (cols(dkv, 256 + 128 * core, 128)[...]
                      + cols(far, 256 + 128 * core, 128)[...].astype(F32)).astype(BF)
        copies[i].wait()
        got = dot_nt(g[...], buf[i])
        part = got if part is None else part + got
        total = jnp.sum(g[...].astype(F32), axis=0, keepdims=True)
        cols(sum_ref, 128 * core, 128)[0:1, :] = total[:, :128]
        cols(sum_ref, 256 + 128 * core, 128)[0:1, :] = total[:, 256:]
    part = part.astype(BF)
    for j, out in enumerate((p0, p1, p2, p3)):
        out[:BLOCK, :] = part[BLOCK * j:BLOCK * (j + 1), :]
        if lasts:
            out[BLOCK:, :] = lasts[j][...]


def mlp_grad_kernel(ids, normed, du, g, dz, mine_ref, other_ref):
    c = ids[1]
    for at, left, right in ((0, normed, du), (512, g, dz)):
        turned = left[...].T
        for i, out in enumerate((mine_ref, other_ref)):
            core = c if i == 0 else 1 - c
            out[:, at:at + 512] = dot(turned, cols(right, 512 * core, 512)[...]).astype(BF)


def out_grad_kernel(ids, mixed, z0, z1, z2, z3, mine_ref, other_ref):
    x, c = ids[0], ids[1]
    turned = mixed[...].T
    for i, out in enumerate((mine_ref, other_ref)):
        core = c if i == 0 else 1 - c
        dmb = jnp.concatenate([cols(z, 256 * x + 128 * core, 128)[:BLOCK, :] for z in (z0, z1, z2, z3)], axis=0)
        out[...] = dot(turned, dmb).astype(BF)


def qkv_grad_kernel(a, gm, go, h, p0, p1, p2, p3, mine_ref, other_ref, sum_ref):
    turned = a[...].T
    mine_ref[...] = dot(turned, gm[...]).astype(BF)
    other_ref[...] = dot(turned, go[...]).astype(BF)
    gain = jnp.zeros((16, D), F32)
    shift = jnp.zeros((16, D), F32)
    for j, p in enumerate((p0, p1, p2, p3)):
        for r in range(0, BLOCK, 16):
            e = p[r:r + 16, :].astype(F32)
            gain = gain + e * norm_parts(h[BLOCK * j + r:BLOCK * j + r + 16, :])[0]
            shift = shift + e
    out = [jnp.sum(t, axis=0, keepdims=True) for t in (gain, shift)]
    sum_ref[...] = jnp.concatenate(out * 4, axis=0)


def add_kernel(*refs):
    out, mark, at = refs[-2], refs[-1], 0
    mark[...] = jnp.zeros_like(mark)
    for mine, came in zip(refs[:-2:2], refs[1:-2:2]):
        width = mine.shape[1]
        out[:, at:at + width] = (mine[...].astype(F32) + came[...].astype(F32)).astype(BF)
        at += width


def total_kernel(got, more, out):
    total = got[0].astype(F32)
    for d in range(1, 16):
        total = total + got[d].astype(F32)
    width = got.shape[2]
    out[:, :width] = total.astype(BF)
    out[:, width:] = more[...]


def write_gradient(name, layer, ref, all_ref, at):
    for core in range(2):
        if name == "up":
            for d in range(8):
                to = 256 * (8 * core + d)
                ref[layer, :, to:to + 256] = jnp.concatenate(
                    [all_ref[chip, core, :, at + 64 * d:at + 64 * (d + 1)] for chip in range(4)], axis=1).astype(F32)
        for chip in range(4):
            to = 256 * chip + 128 * core
            block = lambda i, width: all_ref[chip, core, :, at + i:at + i + width].astype(F32)
            if name == "down":
                ref[layer, 64 * chip:64 * (chip + 1), 512 * core:512 * (core + 1)] = block(0, 512)
            if name == "out":
                ref[layer, :, to:to + 128] = block(0, 128)
            if name == "qkv":
                for m in range(3):
                    ref[layer, :, D * m + to:D * m + to + 128] = block(128 * m, 128)


def arrange(ids, blocks, all_ref, at):
    x, c = ids[0], ids[1]
    for i in range(2):
        for j in range(4):
            all_ref[lax.rem(x + j, 4), c if i == 0 else 1 - c] = blocks[4 * i + j][at:, :]


def early_kernel(ids, counts, *refs):
    blocks, (tokens_ref, output_ref, up, down), all_ref = refs[:8], refs[8:12], refs[12]
    x, c = ids[0], ids[1]
    ranks = jnp.concatenate([half_ranks((1, ROWS), 1, x, core) for core in (c, 1 - c)], axis=1)
    put = jnp.where(slot_ranks((128, 1), 0, counts, 2 * x + c) == ranks, 1.0, 0.0).astype(BF)
    for i, ref in enumerate((tokens_ref, output_ref)):
        rows = jnp.concatenate([t[BLOCK * i:BLOCK * (i + 1), :] for t in blocks], axis=0)
        ref[0] = dot(put, rows).astype(BF)
    arrange(ids, blocks, all_ref, 2 * BLOCK)
    write_gradient("up", 0, up, all_ref, 0)
    write_gradient("down", 0, down, all_ref, 512)


def late_kernel(ids, *refs):
    blocks = refs[:8]
    (out, qkv, gain_ref, shift_ref, branch_ref, qv_ref, up_ref, up, down), all_ref = refs[-10:-1], refs[-1]
    arrange(ids, blocks, all_ref, 0)
    for name, layer, ref, at in (("out", 0, out, 0), ("qkv", 0, qkv, 128), ("up", 0, up, 640), ("down", 0, down, 1152),
                                 ("out", 1, out, 1664), ("qkv", 1, qkv, 1792)):
        write_gradient(name, layer, ref, all_ref, at)
    part = [sum(all_ref[chip, core, 0:16, 512:640].astype(F32) for core in range(2)) for chip in range(4)]
    total = part[0] + part[1] + part[2] + part[3]
    for l in range(2):
        for i, small in enumerate((gain_ref, shift_ref, branch_ref)):
            row = total[5 * l + i:5 * l + i + 1]
            small[l] = jnp.concatenate([row[:, :64], row[:, 64:]], axis=0)
        qv_ref[l:l + 1, :] = total[5 * l + 4:5 * l + 5]
        up_ref[l:l + 1, :] = jnp.concatenate([p[5 * l + 3:5 * l + 4, :64] for p in part], axis=1)


def finish(kernel, ids, blocks, outs, width, before=(), at=0, first=()):
    once = pl.Buffered(1)
    whole = lambda s: pl.BlockSpec(s, functools.partial(lambda n, _: (0,) * n, len(s)), pipeline_mode=once)
    out_specs = [whole(s) if n is None else pl.BlockSpec((n,) + s[1:], functools.partial(lambda at, _: (at, 0, 0), at),
                                                         pipeline_mode=once) for s, _, n, at in outs]
    n = 1 + len(first) + len(blocks)
    return pl.pallas_call(
        kernel,
        grid=(1,),
        in_specs=[pl.BlockSpec(memory_space=pltpu.SMEM)] * (1 + len(first)) + [whole(b.shape) for b in blocks]
        + [pl.BlockSpec(memory_space=pl.ANY)] * len(before),
        out_specs=out_specs,
        out_shape=[pltpu.HBM(s, t) for s, t, _, _ in outs],
        scratch_shapes=[pltpu.VMEM((4, 2, 64, width), BF)],
        input_output_aliases={n + i: at + i for i in range(len(before))},
        compiler_params=pltpu.CompilerParams(vmem_limit_bytes=LIMIT << 20),
        cost_estimate=pl.CostEstimate(flops=int(4e9), bytes_accessed=1, transcendentals=0),
    )(ids, *first, *blocks, *before)


def rest_kernel(ids, out_mine, out_came, qkv_mine, qkv_came, *refs):
    x, out = ids[0], refs[-1]
    for d in range(16):
        at = slice(64 * d, 64 * (d + 1))
        out[d, :, :128] = (out_mine[at, :].astype(F32) + out_came[at, :].astype(F32)).astype(BF)
        out[d, :, 128:512] = (qkv_mine[at, :].astype(F32) + qkv_came[at, :].astype(F32)).astype(BF)
        rows = []
        for l in range(2):
            one, zero, up, qv = refs[4 * l:4 * l + 4]
            pair = lambda u, v: jnp.concatenate([u, v], axis=1)
            rows += [pair(zero[0:1, at], one[0:1, at]), pair(zero[1:2, at], one[1:2, at]),
                     pair(one[2:3, at], one[3:4, at]), pair(up[0:1, at], jnp.zeros((1, 64), F32))]
            lanes = 256 * (d // 8) + 128 * (d % 2)
            rows.append(jnp.where(x == d % 8 // 2, qv[0:1, lanes:lanes + 128], 0.0))
        out[d, :, 512:] = jnp.concatenate(rows + [jnp.zeros((54, 128), F32)], axis=0).astype(BF)


def later(v, *others):
    return lax.optimization_barrier((v, *others))


def over_dp(v):
    return lax.all_to_all(v, "dp", split_axis=0, concat_axis=0, tiled=True)


def shards(tokens, counts, cotangent, w_qkv, w_out, w_up, w_down, norm_gain, norm_shift,
           bias_qv, bias_up, bias_branch):
    s, dp = lax.axis_index("seq"), lax.axis_index("dp")
    ids = jnp.stack([s // 2, s % 2, dp % 4, dp // 4]).astype(jnp.int32)

    def compact(blocks):
        own, give = run(pick_kernel, [((ROWS, D), BF)] * 2, ids, counts, *blocks)
        return own, core_swap(give)

    token_blocks = x_gather(tokens[0])
    first, rest0, rest1 = run(
        pack_kernel, [((64, 512), BF), ((64, 1920), BF), ((64, 1536), BF)], ids,
        away(w_qkv), away(w_out), away(w_up), away(w_down), away(norm_gain), away(norm_shift), away(bias_branch),
        away(bias_qv), away(bias_up),
        scratch=[pltpu.VMEM((64, 384), BF), pltpu.VMEM((2, 8, 64, 128), BF), pltpu.VMEM((3, 2, 2, 64), BF),
                 pltpu.VMEM((2, 128), BF), pltpu.VMEM((2, 256), BF), pltpu.SemaphoreType.DMA((31,))])
    rest0 = lax.all_gather(rest0, "dp", axis=0, tiled=True)
    rest1 = lax.all_gather(rest1, "dp", axis=0, tiled=True)
    source = list(compact(token_blocks))
    first, = run(order_kernel, [((4, 64, 512), BF)], ids, *dp_gather(first, 1), after=[source[0]])
    first, vec, qkv_bias, up_bias = run(
        unpack_kernel, [((D, 512), BF), ((16, D), F32), ((8, 384), F32), ((8, 512), F32)], ids, *dp_gather(first, 4),
        scratch=[pltpu.VMEM((16, 64, 512), BF)])
    first_far = core_swap(first)

    own, far = compact(x_gather(cotangent[0]))
    dz, dh, mark = run(join_kernel, in_hbm([((ROWS, D), BF), ((BLOCK, D), F32)]) + [MARK], own, far)
    dh = saved(dh)

    full = lambda *dtypes: [((ROWS, D), t) for t in dtypes]
    sent = [((BLOCK, D), BF)] * 4
    kept = []
    for l in range(2):
        outs = full(F32, BF) + [((ROWS, 256), BF), ((ROWS, 512), BF)]
        if l == 0:
            hidden, a, q, kv = run(functools.partial(qkv_kernel, l), outs, ids, vec, qkv_bias, *source, first, first_far,
                                   after=[mark], us=2)
        else:
            hidden, a, q, kv, middle0, g0, slope0 = run(
                functools.partial(qkv_kernel, l), outs + [((BLOCK, D), F32, "away")] + [((ROWS, D), BF, "away")] * 2,
                ids, vec, qkv_bias, *source, g, slope, *rests[0], scratch=held(2, D, 384) + [pltpu.SemaphoreType.DMA((3,))], us=3)
            kept[0][-3:] = [saved(v) for v in (middle0, g0, slope0)]
        kv_far = core_swap(kv)
        outs = [((ROWS, 256), BF), ((ROWS, 128), F32)]
        if l == 0:
            mixed, lse, q, kv, hidden, a, first, first_far = run(
                attend_kernel, outs + [(s, t, "away") for s, t in (
                    ((ROWS, 256), BF), ((2 * ROWS, 512), BF), ((ROWS, D), F32), ((ROWS, D), BF), ((D, 512), BF), ((D, 512), BF))],
                ids, q, kv, kv_far, hidden, a, first, first_far, scratch=[pltpu.SemaphoreType.DMA((7,))], us=4)
            rest0, lse = later(rest0, lse)
            rests = [[away(rest0), ("any", core_swap(rest0))]]
            hidden, a, q, kvs, lse = saved(hidden), saved(a), saved(q), [saved(kv)], saved(lse)
        else:
            mixed, lse = run(attend_kernel, outs, ids, q, kv, kv_far, us=3)
            kvs = [kv, kv_far]
            rest1, lse = later(rest1, lse)
            rests.append([away(rest1), ("any", core_swap(rest1))])
        mixes = x_gather(mixed)
        outs = [((ROWS, D), BF, "away")] * 2 if l == 0 else full(BF, BF)
        extra = [pltpu.VMEM((ROWS, D), BF)] * 2 + [pltpu.SemaphoreType.DMA((2,))] if l == 0 else []
        all_mixed, normed, middle, g, slope, *parts = run(
            functools.partial(mlp_kernel, l), outs + full(F32, BF, BF) + sent, ids, vec, up_bias, *mixes, hidden, *rests[l],
            scratch=[pltpu.VMEM((ROWS, 512), F32)] + held(6, D, 512) + extra, us=6)
        if l == 0:
            all_mixed, normed = saved(all_mixed), saved(normed)
            mlp, mark = run(sum_kernel, [((BLOCK, D), BF), LOOSE], *x_scatter(parts))
            source = [middle, *x_gather(mlp)]
        kept.append([hidden, a, q, kvs, lse, all_mixed, normed, middle, g, slope])

    dz = [(saved(dz), (BLOCK, D), (j, 0)) for j in range(4)]
    swapped = lambda v: v + [core_swap(b) for b in v]
    last_parts, last_rows = parts, (middle, (BLOCK, D), (0, 0))
    rests[0][1] = away(rests[0][1][1])
    keep = lambda v: v if isinstance(v, tuple) else saved(v)
    tiny = []
    for l in (1, 0):
        hidden, a, q, kvs, lse, all_mixed, normed, middle, g, slope = kept[l]
        qkv = rests[0] if l else [away(first), away(first_far)]
        top = lambda v: (v, (BLOCK, D), (0, 0))
        dz_all, du, up_sum, *parts = run(
            mlp_back_kernel, full(BF, BF) + [((8, D), F32)] + sent, ids, *dz, slope, *rests[l], scratch=held(4, D, 512),
            after=[mark_add] if l == 0 else (), us=4)
        errs = x_scatter(parts)
        mlp_mine, mlp_other = run(mlp_grad_kernel, [((D, D), BF, "saved"), ((D, D), BF)], ids, normed, du, g, dz_all, us=4)
        dm, dmb, sums1 = run(functools.partial(norm_back_kernel, 2 * l + 1),
                             [((BLOCK, D), F32), ((BLOCK, D), BF), ((8, D), F32)], vec, top(middle), dh, *errs,
                             after=[mlp_mine], us=1 if l else 8)
        mlp_came = core_swap(mlp_other)
        dmbs = x_gather(dmb)
        before = []
        if l == 0:
            shares, mark = run(add_kernel, [((D, D), BF, "saved"), LOOSE], saved(mlp_mine), mlp_came, us=3)
            got_mlp = over_dp(shares.reshape(16, 64, D))
            before = [mark]
        dmb_all, dq, dkv, give = run(
            attend_back_kernel, full(BF) + [((ROWS, 256), BF), ((ROWS, 512), F32), ((ROWS, 512), BF)],
            ids, *dmbs, *rests[l], q, lse, *kvs, scratch=held(2, 256, 512), after=before, us=5 if l else 0.1)
        give = core_swap(give)
        out_mine, out_other = run(out_grad_kernel, [((D, 128), BF, "saved"), ((D, 128), BF)], ids, all_mixed, *dmbs, us=2 if l else 0.1)
        out_came = core_swap(out_other)
        high = BLOCK * (2 - l)
        gm, go, qv_sum, *parts = run(
            functools.partial(qkv_back_kernel, 1536 * l),
            [((ROWS, 384), BF)] * 2 + [((8, 512), F32)] + [((high, D), BF)] * 4,
            ids, dq, dkv, give, *qkv, *([] if l else map(keep, last_parts)), scratch=held(2, D, 384), after=[out_mine], us=3 if l else 0.1)
        errs = x_scatter(parts)
        qkv_mine, qkv_other, sums0 = run(qkv_grad_kernel, [((D, 384), BF, "saved"), ((D, 384), BF), ((8, D), F32)],
                                         keep(a), gm, go, keep(hidden), *parts, us=4 if l else 0.1)
        tiny = [sums1, sums0, up_sum, qv_sum] + tiny
        qkv_came = core_swap(qkv_other)
        qkv_pair = [saved(qkv_mine), qkv_came]
        if l == 1:
            shares, mark_add = run(add_kernel, [((D, 1536), BF, "saved"), LOOSE], saved(mlp_mine), mlp_came,
                                   saved(out_mine), out_came, *qkv_pair, us=4)
            got1 = lax.psum_scatter(shares, "dp", scatter_dimension=0, tiled=True)
        else:
            rest, = run(rest_kernel, in_hbm([((16, 64, 640), BF)]), ids, saved(out_mine), out_came, *qkv_pair, *tiny, us=0.1)
            got_rest = over_dp(rest)
        if l == 1:
            dh, dz = run(functools.partial(norm_back_kernel, 2), [((BLOCK, D), F32), ((BLOCK, D), BF)],
                         vec, top(hidden), dm, *errs)
            dz = x_gather(dz)
        else:
            dz, = run(functools.partial(norm_back_kernel, 0), [((2 * BLOCK + 64, D), BF)],
                      vec, top(hidden), dm, *errs, last_rows, got_mlp, after=[rest], us=2)
    grad_tokens, output, g_up, g_down = finish(
        early_kernel, ids, swapped(x_gather(dz)),
        [((1, 128, D), BF, None, 0)] * 2 + [((2, 64, 4096), F32, 1, 0), ((2, 256, 1024), F32, 1, 0)], D, first=[counts])
    total_rest, = run(total_kernel, [((64, 2176), BF)], got_rest, got1)
    g_out, g_qkv, g_gain, g_shift, g_branch, g_qv, g_upb, g_up, g_down = finish(
        late_kernel, ids, swapped(x_gather(total_rest)),
        [((2, 64, 1024), F32, 2, 0), ((2, 64, 3072), F32, 2, 0)] + [((2, 2, 64), F32, None, 0)] * 3
        + [((2, 128), F32, None, 0), ((2, 256), F32, None, 0), ((2, 64, 4096), F32, 1, 1), ((2, 256, 1024), F32, 1, 1)],
        2176, before=(g_up, g_down), at=7)
    return (output, grad_tokens, g_qkv, g_out, g_up, g_down, g_gain, g_shift, g_qv, g_upb, g_branch)


def solution(mesh):
    rows = P("dp", "seq", None)
    mid = P(None, "dp", None)
    end = P(None, None, "dp")
    two = P(None, "dp")
    return jax.shard_map(
        shards,
        mesh=mesh,
        in_specs=(rows, P("dp", None), rows, mid, mid, mid, mid, end, end, two, two, end),
        out_specs=(rows, rows, mid, mid, mid, mid, end, end, two, two, end),
        check_vma=False,
    )
```

```python
import functools

import jax
import jax.numpy as jnp
from jax import lax
from jax.experimental import pallas as pl
from jax.experimental.pallas import tpu as pltpu
from jax.sharding import PartitionSpec as P

EPSILON = 1e-06
BF = jnp.bfloat16
F32 = jnp.float32
BLOCK = 80
SHARE = 73
TOTAL = 577
ROWS = 4 * BLOCK
D = 1024
LOOSE = ((8, 128), jnp.float32)
MARK = ((8, 128), jnp.float32, "saved")
LIMIT = 24

NEXT = [(i, (i + 2) % 8) for i in range(8)]
PREV = [(i, (i - 2) % 8) for i in range(8)]
FAR = [(i, (i + 4) % 8) for i in range(8)]
CORE = [(i, i ^ 1) for i in range(8)]


def x_gather(block):
    two = lax.ppermute(block, "seq", PREV)
    four = lax.ppermute(block, "seq", NEXT)
    return [block, two, lax.ppermute(block, "seq", FAR), four]


def x_scatter(blocks):
    three = lax.ppermute(blocks[2], "seq", FAR)
    return [blocks[0], lax.ppermute(blocks[1], "seq", NEXT), three, lax.ppermute(blocks[3], "seq", PREV)]


def core_swap(v):
    return lax.ppermute(v, "seq", CORE)


def dp_pairs(step, k):
    if step == 1:
        return [(i, i // 4 * 4 + (i + k) % 4) for i in range(16)]
    return [(i, (i + 4 * k) % 16) for i in range(16)]


def dp_scatter(blocks, step):
    return [blocks[0]] + [lax.ppermute(blocks[k], "dp", dp_pairs(step, k)) for k in (1, 2, 3)]


def dp_gather(block, step):
    return [block] + [lax.ppermute(block, "dp", dp_pairs(step, -k)) for k in (1, 2, 3)]


def dot(a, b):
    return jnp.dot(a, b, preferred_element_type=F32)


def dot_nt(a, b):
    return lax.dot_general(a, b, (((1,), (1,)), ((), ())), preferred_element_type=F32)


def dot_tn(a, b):
    return lax.dot_general(a, b, (((0,), (0,)), ((), ())), preferred_element_type=F32)


def cols(ref, at, width):
    return ref.at[:, pl.ds(pl.multiple_of(at, 128), width)]


def norm_parts(rows):
    mean = jnp.mean(rows, axis=-1, keepdims=True)
    centered = rows - mean
    rstd = lax.rsqrt(jnp.mean(centered * centered, axis=-1, keepdims=True) + EPSILON)
    return centered * rstd, rstd


def away(v):
    return ("away", v)


def saved(v):
    return ("saved", v)


def in_hbm(outs):
    return [o + ("saved",) for o in outs]


def run(kernel, outs, *ins, scratch=(), after=(), us=1.0):
    once = pl.Buffered(1)
    small = lambda v: v.size < 200000
    hbm = lambda v: pltpu.with_memory_space_constraint(v, pltpu.HBM)
    whole = lambda s: pl.BlockSpec(s, functools.partial(lambda n, _: (0,) * n, len(s)), pipeline_mode=once)
    specs, arrays = [], []
    for v in ins:
        if isinstance(v, tuple) and len(v) == 2:
            kind, v = v
            specs.append(whole(v.shape) if kind == "saved" else pl.BlockSpec(memory_space=pl.ANY if kind == "any" else pltpu.HBM))
            v = v if kind == "any" else hbm(v)
        elif isinstance(v, tuple):
            v, block, index = v
            specs.append(pl.BlockSpec(block, functools.partial(lambda at, _: at, index), pipeline_mode=once))
            if isinstance(v, tuple):
                v = hbm(v[1])
        elif v.dtype == jnp.int32:
            specs.append(pl.BlockSpec(memory_space=pltpu.SMEM))
        else:
            specs.append(whole(v.shape))
        arrays.append(v)
    specs += [pl.BlockSpec(memory_space=pl.ANY if small(v) else pltpu.HBM) for v in after]
    n = len(arrays)
    body = lambda *refs: kernel(*refs[:n], *refs[n + len(after):])
    kinds = [o[2] if len(o) > 2 else "" for o in outs]
    return pl.pallas_call(
        body,
        grid=(1,),
        in_specs=specs,
        out_specs=[pl.BlockSpec(memory_space=pltpu.HBM) if k == "away" else whole(o[0]) for k, o in zip(kinds, outs)],
        out_shape=[pltpu.HBM(o[0], o[1]) if k else jax.ShapeDtypeStruct(o[0], o[1]) for k, o in zip(kinds, outs)],
        scratch_shapes=list(scratch),
        compiler_params=pltpu.CompilerParams(vmem_limit_bytes=LIMIT << 20),
        cost_estimate=pl.CostEstimate(flops=int(us * 1.0 * 1.15e9), bytes_accessed=1, transcendentals=0),
    )(*arrays, *[v if small(v) else hbm(v) for v in after])


def fetch(parts, buf, sem):
    copies = [pltpu.make_async_copy(v, buf.at[i], sem.at[i]) for i, v in enumerate(parts)]
    for copy in copies:
        copy.start()
    return copies


def send(pairs, sem):
    copies = [pltpu.make_async_copy(v, out, sem.at[i]) for i, (v, out) in enumerate(pairs)]
    for copy in copies:
        copy.start()
    return copies


def held(count, rows, width):
    return [pltpu.VMEM((count, rows, width), BF), pltpu.SemaphoreType.DMA((count,))]


def load_kernel(slices, ids, *refs):
    n = len(slices)
    sources, outs, sem = refs[:n], refs[n:-1], refs[-1]
    copies = []
    for part, source, out in zip(slices, sources, outs):
        for i, at in enumerate(part(ids) if part else [None]):
            copies.append(pltpu.make_async_copy(source if at is None else source.at[at], out if at is None else out.at[i],
                                                sem.at[len(copies)]))
            copies[-1].start()
    for copy in copies:
        copy.wait()


def load(ids, parts, after=()):
    count = sum(s[0] if p else 1 for _, s, p in parts)
    return run(functools.partial(load_kernel, [p for _, _, p in parts]), [(s, BF if v.dtype == BF else F32) for v, s, _ in parts],
               ids, *[away(v) for v, _, _ in parts], scratch=[pltpu.SemaphoreType.DMA((count,))], after=after, us=2)


def lanes_of(*at, width=512):
    return lambda ids: [(slice(None), pl.ds(i, width)) for i in at]


def half_ranks(shape, axis, x, core):
    at = lax.broadcasted_iota(jnp.int32, shape, axis)
    block = sum((at >= BLOCK * i).astype(jnp.int32) for i in (1, 2, 3))
    within = at - BLOCK * block
    chip = x + block
    chip = jnp.where(chip >= 4, chip - 4, chip)
    rank = (4 * core + chip) * SHARE + within
    return jnp.where((within < SHARE) & (rank < TOTAL), rank, -2)


def slot_ranks(shape, axis, counts, s):
    at = lax.broadcasted_iota(jnp.int32, shape, axis)
    start = sum(jnp.where(i < s, counts[0, i], 0) for i in range(8))
    return jnp.where(at < counts[0, s], start + at, -1)


def kept_keys(x, c):
    at = lax.broadcasted_iota(jnp.int32, (1, 2 * ROWS), 1)
    second = (at >= ROWS).astype(jnp.int32)
    at = at - ROWS * second
    block = sum((at >= BLOCK * i).astype(jnp.int32) for i in (1, 2, 3))
    chip = x + block
    chip = jnp.where(chip >= 4, chip - 4, chip)
    core = jnp.where(second > 0, 1 - c, c)
    within = at - BLOCK * block
    return (within < SHARE) & ((4 * core + chip) * SHARE + within < TOTAL)


def pick_kernel(ids, counts, t0, t1, t2, t3, own_ref, far_ref):
    x, c = ids[0], ids[1]
    rows = jnp.concatenate([t[...] for t in (t0, t1, t2, t3)], axis=0)
    slots = [slot_ranks((1, 128), 1, counts, 2 * lax.rem(x + j, 4) + c) for j in range(4)]
    for core, out in ((c, own_ref), (1 - c, far_ref)):
        rank = half_ranks((ROWS, 1), 0, x, core)
        pick = jnp.concatenate([jnp.where(rank == s, 1.0, 0.0) for s in slots], axis=1)
        out[...] = dot(pick.astype(BF), rows).astype(BF)


def join_kernel(own, far, dz_ref, dh_ref, mark):
    mark[...] = jnp.zeros_like(mark)
    dz = own[...] + far[...]
    dz_ref[...] = dz
    dh_ref[...] = dz[:BLOCK, :].astype(F32)


def pack_kernel(ids, w_qkv, w_out, w_up, w_down, gain, shift, branch, qv, up,
                first_ref, rest0_ref, rest1_ref, qkv_buf, up_buf, norm_buf, qv_buf, wide_buf, sem):
    x, c = ids[0], ids[1]
    lanes = lambda at, width: pl.ds(pl.multiple_of(at, 128), width)
    copies = []

    def copy(source, target):
        copies.append(pltpu.make_async_copy(source, target, sem.at[len(copies)]))
        copies[-1].start()

    rests = (rest0_ref, rest1_ref)
    for l in range(2):
        for m in range(3):
            target = qkv_buf.at[:, pl.ds(128 * m, 128)] if l == 0 else rest0_ref.at[:, pl.ds(1536 + 128 * m, 128)]
            copy(w_qkv.at[l, :, lanes(D * m + 256 * x + 128 * c, 128)], target)
        for d in range(8):
            copy(w_up.at[l, :, lanes(2048 * c + 256 * d + 128 * (x // 2), 128)], up_buf.at[l, d])
        copy(w_out.at[l, :, lanes(512 * c, 512)], rests[l].at[:, pl.ds(512, 512)])
        copy(w_down.at[l, pl.ds(pl.multiple_of(64 * x, 64), 64), lanes(512 * c, 512)], rests[l].at[:, pl.ds(1024, 512)])
    for i, v in enumerate((gain, shift, branch)):
        copy(v, norm_buf.at[i])
    copy(qv, qv_buf)
    copy(up, wide_buf)
    for each in copies:
        each.wait()
    pairs = lambda i: jnp.concatenate([norm_buf[i, 0], norm_buf[i, 1]], axis=0).astype(F32)
    wide = wide_buf[...].astype(F32)
    small = jnp.concatenate([
        jnp.concatenate([pairs(0), pairs(1)], axis=1),
        jnp.concatenate([pairs(2), jnp.zeros((4, 64), F32)], axis=1),
        qv_buf[...].astype(F32),
        wide[0:1, :128], wide[0:1, 128:], wide[1:2, :128], wide[1:2, 128:],
        jnp.zeros((50, 128), F32)], axis=0).astype(BF)
    block = jnp.concatenate([qkv_buf[...], small], axis=1)
    first_ref[...] = block
    odd = lax.rem(x, 2) == 1
    for l in range(2):
        got = []
        for d in range(8):
            piece = up_buf[l, d].astype(F32)
            got.append(jnp.where(odd, piece[:, 64:], piece[:, :64]))
        rests[l][:, :512] = jnp.concatenate(got, axis=1).astype(BF)


def order_kernel(ids, a, b, c, d, out):
    for i, v in enumerate((a, b, c, d)):
        out[lax.rem(ids[2] + i, 4)] = v[...]


def unpack_kernel(ids, a, b, c, d, first_ref, vec_ref, qkv_ref, up_ref, first):
    for i, v in enumerate((a, b, c, d)):
        for y in range(4):
            first[4 * lax.rem(ids[3] + i, 4) + y] = v[y]
    for i in range(16):
        first_ref[64 * i:64 * (i + 1), :] = first[i]
    x, c = ids[0], ids[1]
    rows = [first[d, 0:16, 384:].astype(F32) for d in range(16)]
    line = lambda at, lanes: jnp.concatenate([r[at:at + 4, lanes:lanes + 64] for r in rows], axis=1)
    vec_ref[...] = jnp.concatenate([line(0, 0), line(0, 64), line(4, 0), jnp.zeros((4, D), F32)], axis=0)
    qkv, up = [], []
    for l in range(2):
        for core in (c, 1 - c):
            q = first[2 * x + core, 0:16, 384:].astype(F32)[8 + l:9 + l]
            v = first[8 + 2 * x + core, 0:16, 384:].astype(F32)[8 + l:9 + l]
            qkv.append(jnp.concatenate([q, jnp.zeros((1, 128), F32), v], axis=1))
            got = []
            for d in range(8):
                r = first[8 * core + d, 0:16, 384:].astype(F32)
                r = jnp.where(x >= 2, r[11 + 2 * l:12 + 2 * l], r[10 + 2 * l:11 + 2 * l])
                got.append(jnp.where(lax.rem(x, 2) == 1, r[:, 64:], r[:, :64]))
            up.append(jnp.concatenate(got, axis=1))
    qkv_ref[...] = jnp.concatenate(qkv + [jnp.zeros((4, 384), F32)], axis=0)
    up_ref[...] = jnp.concatenate(up + [jnp.zeros((4, 512), F32)], axis=0)


def qkv_kernel(l, ids, vec, bias, *refs):
    gain, shift = vec[2 * l:2 * l + 1, :], vec[4 + 2 * l:5 + 2 * l, :]
    first = l == 0
    keeps = []
    if first:
        own, far, wm, wo, h_ref, a_ref, q_ref, kv_ref = refs
        weight = lambda i: (wm, wo)[i][:, :384]
    else:
        (m, d0, d1, d2, d3, g, slope, wm, wo, h_ref, a_ref, q_ref, kv_ref,
         m_out, g_out, slope_out, buf, sem, out_sem) = refs
        branch = vec[9:10, :]
        copies = fetch([w.at[:, pl.ds(1536, 384)] for w in (wm, wo)], buf, sem)
        keeps = send([(m.at[pl.ds(0, BLOCK), :], m_out), (g, g_out), (slope, slope_out)], out_sem)

        def weight(i):
            copies[i].wait()
            return buf[i]

    c = ids[1]
    for r in range(0, ROWS, 16):
        rows = slice(r, r + 16)
        if first:
            h = own[rows, :].astype(F32) + far[rows, :].astype(F32)
        else:
            b, o = divmod(r, BLOCK)
            h = m[rows, :] + (d0, d1, d2, d3)[b][o:o + 16, :].astype(F32) + branch
        h_ref[rows, :] = h
        a_ref[rows, :] = (norm_parts(h)[0] * gain + shift).astype(BF)
    a = a_ref[...]
    for i in range(2):
        core = c if i == 0 else 1 - c
        packed = (dot(a, weight(i)) + bias[2 * l + i:2 * l + i + 1, :]).astype(BF)
        cols(q_ref, 128 * core, 128)[...] = packed[:, :128]
        cols(kv_ref, 128 * core, 128)[...] = packed[:, 128:256]
        cols(kv_ref, 256 + 128 * core, 128)[...] = packed[:, 256:]
    for keep in keeps:
        keep.wait()


def head_mask(rows, sub):
    lane = lax.broadcasted_iota(jnp.int32, (rows, 128), 1)
    return (lane < 64) if sub == 0 else (lane >= 64)


def attend_kernel(ids, q_ref, kv_ref, far_ref, *refs):
    keeps = []
    if len(refs) == 2:
        mixed_ref, lse_ref = refs
    else:
        n = (len(refs) - 5) // 2
        mixed_ref, lse_ref = refs[n:n + 2]
        outs, sem = refs[n + 2:-1], refs[-1]
        keeps = send([(q_ref, outs[0]), (kv_ref, outs[1].at[pl.ds(0, ROWS), :]),
                      (far_ref, outs[1].at[pl.ds(ROWS, ROWS), :])], sem)
        keeps += send(list(zip(refs[:n], outs[2:])), sem.at[pl.ds(3, n)])
    low = head_mask(ROWS, 0)
    keep = kept_keys(ids[0], ids[1])
    lane = lax.broadcasted_iota(jnp.int32, (ROWS, 128), 1)
    lses = jnp.zeros((ROWS, 128), F32)
    for pair in range(2):
        at = 128 * pair
        k = jnp.concatenate([kv_ref[:, at:at + 128], far_ref[:, at:at + 128]], axis=0)
        v = jnp.concatenate([kv_ref[:, 256 + at:384 + at], far_ref[:, 256 + at:384 + at]], axis=0)
        q = q_ref[:, at:at + 128]
        got = []
        for sub in range(2):
            qm = jnp.where(low if sub == 0 else ~low, q, jnp.zeros_like(q))
            s = dot_nt(qm, k) * 0.125
            s = jnp.where(keep, s, -1e9)
            top = jnp.max(s, axis=-1, keepdims=True)
            e = jnp.exp(s - top)
            total = jnp.sum(e, axis=-1, keepdims=True)
            got.append(dot((e * (1.0 / total)).astype(BF), v))
            lses = jnp.where(lane == 2 * pair + sub, top + jnp.log(total), lses)
        mixed_ref[:, at:at + 128] = jnp.where(low, got[0], got[1]).astype(BF)
    lse_ref[...] = lses
    for keep in keeps:
        keep.wait()


def mlp_kernel(l, ids, vec, up_bias, mx0, mx1, mx2, mx3, h, near, wo, *refs):
    x, c = ids[0], ids[1]
    keeps = []
    if l == 0:
        (all_out, c_out, m_ref, g_ref, slope_ref, p0, p1, p2, p3,
         u_ref, buf, sem, all_ref, c_ref, out_sem) = refs
    else:
        all_ref, c_ref, m_ref, g_ref, slope_ref, p0, p1, p2, p3, buf, u_ref, sem = refs
    copies = fetch([wo.at[:, pl.ds(at, 512)] for at in (512, 0, 1024)], buf, sem)

    def weight(i):
        if i % 2 == 0:
            return near[i // 2]
        copies[i // 2].wait()
        return buf[i // 2]

    gain, shift, branch = (vec[i + 2 * l:i + 1 + 2 * l, :] for i in (1, 5, 8))
    for j, mx in enumerate((mx0, mx1, mx2, mx3)):
        at = 256 * lax.rem(x + j, 4)
        for b in range(4):
            to = BLOCK * ((j + b) % 4)
            all_ref[to:to + BLOCK, pl.ds(pl.multiple_of(at, 128), 256)] = mx[BLOCK * b:BLOCK * (b + 1), :]
    if l == 0:
        keeps += send([(all_ref, all_out)], out_sem)
    mixed = all_ref[...]
    for i in range(2):
        core = c if i == 0 else 1 - c
        cols(m_ref, 512 * core, 512)[...] = dot(mixed, weight(i))
    for r in range(0, ROWS, 16):
        rows = slice(r, r + 16)
        m = h[rows, :] + m_ref[rows, :] + branch
        m_ref[rows, :] = m
        c_ref[rows, :] = (norm_parts(m)[0] * gain + shift).astype(BF)
    if l == 0:
        keeps += send([(c_ref, c_out)], out_sem.at[pl.ds(1, 1)])
    normed = c_ref[...]
    for i in range(2):
        core = c if i == 0 else 1 - c
        slope_part = cols(slope_ref, 512 * core, 512)
        g_part = cols(g_ref, 512 * core, 512)
        u_ref[...] = dot(normed, weight(2 + i)) + up_bias[2 * l + i:2 * l + i + 1, :]
        for r in range(0, ROWS, 32):
            rows = pl.ds(r, 32)
            u = u_ref[rows, :]
            half = 0.5 + 0.5 * lax.erf(u * 0.7071067811865476)
            g_part[rows, :] = (u * half).astype(BF)
            slope_part[rows, :] = (half + u * (0.3989422804014327 * jnp.exp(-0.5 * u * u))).astype(BF)
    g = g_ref[...]
    for i in range(2):
        core = c if i == 0 else 1 - c
        part = dot(g, weight(4 + i)).astype(BF)
        for j, out in enumerate((p0, p1, p2, p3)):
            cols(out, 512 * core, 512)[...] = part[BLOCK * j:BLOCK * (j + 1), :]
    for keep in keeps:
        keep.wait()


def sum_kernel(a, b, c, d, out, mark):
    mark[...] = jnp.zeros_like(mark)
    out[...] = (a[...].astype(F32) + b[...].astype(F32) + c[...].astype(F32) + d[...].astype(F32)).astype(BF)


def mlp_back_kernel(ids, z0, z1, z2, z3, slope, *refs):
    near, near_far, dz_ref, du_ref, sum_ref, p0, p1, p2, p3 = refs
    weight = lambda i: (near, near_far)[i % 2][near.shape[0] - 1 - i // 2]
    c = ids[1]
    for j, z in enumerate((z0, z1, z2, z3)):
        dz_ref[BLOCK * j:BLOCK * (j + 1), :] = z[...]
    dact = (dot_nt(cols(dz_ref, 512 * c, 512)[...], weight(0))
            + dot_nt(cols(dz_ref, 512 * (1 - c), 512)[...], weight(1)))
    du_ref[...] = (dact * slope[...].astype(F32)).astype(BF)
    part = (dot_nt(cols(du_ref, 512 * c, 512)[...], weight(2))
            + dot_nt(cols(du_ref, 512 * (1 - c), 512)[...], weight(3)))
    part = part.astype(BF)
    for j, out in enumerate((p0, p1, p2, p3)):
        out[...] = part[BLOCK * j:BLOCK * (j + 1), :]
    sums = jnp.sum(du_ref[...].astype(F32), axis=0, keepdims=True)
    sum_ref[...] = jnp.broadcast_to(sums, (8, D))


def norm_back_kernel(row, vec, base, above, e0, e1, e2, e3, *refs):
    final = len(refs) == 3 and refs[2].shape[0] > BLOCK
    if final:
        last, got, db_ref = refs
    else:
        d_ref, db_ref, sum_ref = refs if len(refs) == 3 else (*refs, None)
    gain = vec[row:row + 1, :]
    totals = [jnp.zeros((16, D), F32) for _ in range(4)]
    for r in range(0, BLOCK, 16):
        rows = slice(r, r + 16)
        e = e0[rows, :].astype(F32) + e1[rows, :].astype(F32) + e2[rows, :].astype(F32) + e3[rows, :].astype(F32)
        n, rstd = norm_parts(base[rows, :])
        eg = e * gain
        back = rstd * (eg - jnp.mean(eg, axis=-1, keepdims=True) - n * jnp.mean(eg * n, axis=-1, keepdims=True))
        up = above[rows, :]
        d = up + back
        db = d.astype(BF)
        db_ref[rows, :] = db
        if final:
            late = slice(BLOCK + r, BLOCK + r + 16)
            sums = sum(v[late, :].astype(F32) for v in (e0, e1, e2, e3))
            db_ref[late, :] = (last[rows, :] + sums + vec[11:12, :]).astype(BF)
            continue
        d_ref[rows, :] = d
        if sum_ref is not None:
            for i, t in enumerate((e * n, e, db.astype(F32), up.astype(BF).astype(F32))):
                totals[i] = totals[i] + t
    if final:
        total = got[0].astype(F32)
        for d in range(1, 16):
            total = total + got[d].astype(F32)
        db_ref[2 * BLOCK:, :] = total.astype(BF)
    elif sum_ref is not None:
        out = [jnp.sum(t, axis=0, keepdims=True) for t in totals]
        sum_ref[...] = jnp.concatenate(out + out, axis=0)


def attend_back_kernel(ids, z0, z1, z2, z3, *refs):
    near, near_far, q_ref, lse_ref, *kvs, dmb_ref, dq_ref, dkv_ref, give_ref = refs
    x, c = ids[0], ids[1]
    part = pl.ds(pl.multiple_of(256 * x, 256), 256)
    for j, z in enumerate((z0, z1, z2, z3)):
        dmb_ref[BLOCK * j:BLOCK * (j + 1), :] = z[:BLOCK, :]
    weight = lambda i: (near, near_far)[i][0] if near.shape[1] == 256 else (near, near_far)[i][0, part, :]
    dmixed = (dot_nt(cols(dmb_ref, 512 * c, 512)[...], weight(0))
              + dot_nt(cols(dmb_ref, 512 * (1 - c), 512)[...], weight(1))).astype(BF)
    low = head_mask(ROWS, 0)
    keep = kept_keys(ids[0], ids[1])
    lane = lax.broadcasted_iota(jnp.int32, (ROWS, 128), 1)
    for pair in range(2):
        at = 128 * pair
        k, v = (jnp.concatenate([ref[:, i + at:i + at + 128] for ref in kvs], axis=0) for i in (0, 256))
        q = q_ref[:, at:at + 128]
        dmp = dmixed[:, at:at + 128]
        dqs = []
        dk = jnp.zeros((2 * ROWS, 128), F32)
        dv = jnp.zeros((2 * ROWS, 128), F32)
        for sub in range(2):
            mask = low if sub == 0 else ~low
            qm = jnp.where(mask, q, jnp.zeros_like(q))
            dmm = jnp.where(mask, dmp, jnp.zeros_like(dmp))
            lse = jnp.sum(jnp.where(lane == 2 * pair + sub, lse_ref[...], 0.0), axis=-1, keepdims=True)
            s = dot_nt(qm, k) * 0.125
            p = jnp.exp(jnp.where(keep, s, -1e9) - lse)
            dp = dot_nt(dmm, v)
            inner = jnp.sum(dp * p, axis=-1, keepdims=True)
            ds = (p * (dp - inner)).astype(BF)
            dqs.append(dot(ds, k))
            dk = dk + dot_tn(ds, qm)
            dv = dv + dot_tn(p.astype(BF), dmm)
        dq_ref[:, at:at + 128] = (jnp.where(low, dqs[0], dqs[1]) * 0.125).astype(BF)
        dk = dk * 0.125
        dkv_ref[:, at:at + 128] = dk[:ROWS]
        dkv_ref[:, 256 + at:384 + at] = dv[:ROWS]
        give_ref[:, at:at + 128] = dk[ROWS:].astype(BF)
        give_ref[:, 256 + at:384 + at] = dv[ROWS:].astype(BF)


def qkv_back_kernel(at, ids, dq, dkv, far, wm, wo, *refs):
    if at is None:
        lasts, (gm_ref, go_ref, sum_ref, p0, p1, p2, p3) = refs[:-7], refs[-7:]
        weight = lambda i: (wm, wo)[i][0]
    else:
        lasts, (gm_ref, go_ref, sum_ref, p0, p1, p2, p3, buf, sem) = refs[:-9], refs[-9:]
        copies = fetch([w.at[:, pl.ds(at, 384)] for w in (wm, wo)], buf, sem)

        def weight(i):
            copies[i].wait()
            return buf[i]

    c = ids[1]
    part = None
    sum_ref[...] = jnp.zeros((8, 512), F32)
    for i, g in enumerate((gm_ref, go_ref)):
        core = c if i == 0 else 1 - c
        g[:, :128] = cols(dq, 128 * core, 128)[...]
        g[:, 128:256] = (cols(dkv, 128 * core, 128)[...] + cols(far, 128 * core, 128)[...].astype(F32)).astype(BF)
        g[:, 256:] = (cols(dkv, 256 + 128 * core, 128)[...]
                      + cols(far, 256 + 128 * core, 128)[...].astype(F32)).astype(BF)
        got = dot_nt(g[...], weight(i))
        part = got if part is None else part + got
        total = jnp.sum(g[...].astype(F32), axis=0, keepdims=True)
        cols(sum_ref, 128 * core, 128)[0:1, :] = total[:, :128]
        cols(sum_ref, 256 + 128 * core, 128)[0:1, :] = total[:, 256:]
    part = part.astype(BF)
    for j, out in enumerate((p0, p1, p2, p3)):
        out[:BLOCK, :] = part[BLOCK * j:BLOCK * (j + 1), :]
        if lasts:
            out[BLOCK:, :] = lasts[j][...]


def mlp_grad_kernel(ids, normed, du, g, dz, mine_ref, other_ref, mark):
    mark[...] = jnp.zeros_like(mark)
    c = ids[1]
    for at, left, right in ((0, normed, du), (512, g, dz)):
        turned = left[...].T
        for i, out in enumerate((mine_ref, other_ref)):
            core = c if i == 0 else 1 - c
            out[:, at:at + 512] = dot(turned, cols(right, 512 * core, 512)[...]).astype(BF)


def out_grad_kernel(ids, mixed, z0, z1, z2, z3, mine_ref, other_ref, mark):
    mark[...] = jnp.zeros_like(mark)
    x, c = ids[0], ids[1]
    turned = mixed[...].T
    for i, out in enumerate((mine_ref, other_ref)):
        core = c if i == 0 else 1 - c
        dmb = jnp.concatenate([cols(z, 256 * x + 128 * core, 128)[:BLOCK, :] for z in (z0, z1, z2, z3)], axis=0)
        out[...] = dot(turned, dmb).astype(BF)


def qkv_grad_kernel(a, gm, go, h, p0, p1, p2, p3, mine_ref, other_ref, sum_ref):
    turned = a[...].T
    mine_ref[...] = dot(turned, gm[...]).astype(BF)
    other_ref[...] = dot(turned, go[...]).astype(BF)
    gain = jnp.zeros((16, D), F32)
    shift = jnp.zeros((16, D), F32)
    for j, p in enumerate((p0, p1, p2, p3)):
        for r in range(0, BLOCK, 16):
            e = p[r:r + 16, :].astype(F32)
            gain = gain + e * norm_parts(h[BLOCK * j + r:BLOCK * j + r + 16, :])[0]
            shift = shift + e
    out = [jnp.sum(t, axis=0, keepdims=True) for t in (gain, shift)]
    sum_ref[...] = jnp.concatenate(out * 4, axis=0)


def add_kernel(*refs):
    out, mark, at = refs[-2], refs[-1], 0
    mark[...] = jnp.zeros_like(mark)
    for mine, came in zip(refs[:-2:2], refs[1:-2:2]):
        width = mine.shape[1]
        out[:, at:at + width] = (mine[...].astype(F32) + came[...].astype(F32)).astype(BF)
        at += width


def total_kernel(got, more, out):
    total = got[0].astype(F32)
    for d in range(1, 16):
        total = total + got[d].astype(F32)
    width = got.shape[2]
    out[:, :width] = total.astype(BF)
    out[:, width:] = more[...]


def write_gradient(name, layer, ref, all_ref, at):
    for core in range(2):
        if name == "up":
            for d in range(8):
                to = 256 * (8 * core + d)
                ref[layer, :, to:to + 256] = jnp.concatenate(
                    [all_ref[chip, core, :, at + 64 * d:at + 64 * (d + 1)] for chip in range(4)], axis=1).astype(F32)
        for chip in range(4):
            to = 256 * chip + 128 * core
            block = lambda i, width: all_ref[chip, core, :, at + i:at + i + width].astype(F32)
            if name == "down":
                ref[layer, 64 * chip:64 * (chip + 1), 512 * core:512 * (core + 1)] = block(0, 512)
            if name == "out":
                ref[layer, :, to:to + 128] = block(0, 128)
            if name == "qkv":
                for m in range(3):
                    ref[layer, :, D * m + to:D * m + to + 128] = block(128 * m, 128)


def arrange(ids, blocks, all_ref, at):
    x, c = ids[0], ids[1]
    for i in range(2):
        for j in range(4):
            all_ref[lax.rem(x + j, 4), c if i == 0 else 1 - c] = blocks[4 * i + j][at:, :]


def early_kernel(ids, counts, *refs):
    blocks, (tokens_ref, output_ref, up, down), all_ref = refs[:8], refs[8:12], refs[12]
    x, c = ids[0], ids[1]
    ranks = jnp.concatenate([half_ranks((1, ROWS), 1, x, core) for core in (c, 1 - c)], axis=1)
    put = jnp.where(slot_ranks((128, 1), 0, counts, 2 * x + c) == ranks, 1.0, 0.0).astype(BF)
    for i, ref in enumerate((tokens_ref, output_ref)):
        rows = jnp.concatenate([t[BLOCK * i:BLOCK * (i + 1), :] for t in blocks], axis=0)
        ref[0] = dot(put, rows).astype(BF)
    arrange(ids, blocks, all_ref, 2 * BLOCK)
    write_gradient("up", 0, up, all_ref, 0)
    write_gradient("down", 0, down, all_ref, 512)


def late_kernel(ids, *refs):
    blocks = refs[:8]
    (out, qkv, gain_ref, shift_ref, branch_ref, qv_ref, up_ref, up, down), all_ref = refs[-10:-1], refs[-1]
    arrange(ids, blocks, all_ref, 0)
    for name, layer, ref, at in (("out", 0, out, 0), ("qkv", 0, qkv, 128), ("up", 0, up, 640), ("down", 0, down, 1152),
                                 ("out", 1, out, 1664), ("qkv", 1, qkv, 1792)):
        write_gradient(name, layer, ref, all_ref, at)
    part = [sum(all_ref[chip, core, 0:16, 512:640].astype(F32) for core in range(2)) for chip in range(4)]
    total = part[0] + part[1] + part[2] + part[3]
    for l in range(2):
        for i, small in enumerate((gain_ref, shift_ref, branch_ref)):
            row = total[5 * l + i:5 * l + i + 1]
            small[l] = jnp.concatenate([row[:, :64], row[:, 64:]], axis=0)
        qv_ref[l:l + 1, :] = total[5 * l + 4:5 * l + 5]
        up_ref[l:l + 1, :] = jnp.concatenate([p[5 * l + 3:5 * l + 4, :64] for p in part], axis=1)


def finish(kernel, ids, blocks, outs, width, before=(), at=0, first=()):
    once = pl.Buffered(1)
    whole = lambda s: pl.BlockSpec(s, functools.partial(lambda n, _: (0,) * n, len(s)), pipeline_mode=once)
    out_specs = [whole(s) if n is None else pl.BlockSpec((n,) + s[1:], functools.partial(lambda at, _: (at, 0, 0), at),
                                                         pipeline_mode=once) for s, _, n, at in outs]
    n = 1 + len(first) + len(blocks)
    return pl.pallas_call(
        kernel,
        grid=(1,),
        in_specs=[pl.BlockSpec(memory_space=pltpu.SMEM)] * (1 + len(first)) + [whole(b.shape) for b in blocks]
        + [pl.BlockSpec(memory_space=pl.ANY)] * len(before),
        out_specs=out_specs,
        out_shape=[pltpu.HBM(s, t) for s, t, _, _ in outs],
        scratch_shapes=[pltpu.VMEM((4, 2, 64, width), BF)],
        input_output_aliases={n + i: at + i for i in range(len(before))},
        compiler_params=pltpu.CompilerParams(vmem_limit_bytes=LIMIT << 20),
        cost_estimate=pl.CostEstimate(flops=int(4e9), bytes_accessed=1, transcendentals=0),
    )(ids, *first, *blocks, *before)


def rest_kernel(ids, out_mine, out_came, qkv_mine, qkv_came, *refs):
    x, out = ids[0], refs[-1]
    for d in range(16):
        at = slice(64 * d, 64 * (d + 1))
        out[d, :, :128] = (out_mine[at, :].astype(F32) + out_came[at, :].astype(F32)).astype(BF)
        out[d, :, 128:512] = (qkv_mine[at, :].astype(F32) + qkv_came[at, :].astype(F32)).astype(BF)
        rows = []
        for l in range(2):
            one, zero, up, qv = refs[4 * l:4 * l + 4]
            pair = lambda u, v: jnp.concatenate([u, v], axis=1)
            rows += [pair(zero[0:1, at], one[0:1, at]), pair(zero[1:2, at], one[1:2, at]),
                     pair(one[2:3, at], one[3:4, at]), pair(up[0:1, at], jnp.zeros((1, 64), F32))]
            lanes = 256 * (d // 8) + 128 * (d % 2)
            rows.append(jnp.where(x == d % 8 // 2, qv[0:1, lanes:lanes + 128], 0.0))
        out[d, :, 512:] = jnp.concatenate(rows + [jnp.zeros((54, 128), F32)], axis=0).astype(BF)


def later(v, *others):
    return lax.optimization_barrier((v, *others))


def over_dp(v):
    return lax.all_to_all(v, "dp", split_axis=0, concat_axis=0, tiled=True)


def shards(tokens, counts, cotangent, w_qkv, w_out, w_up, w_down, norm_gain, norm_shift,
           bias_qv, bias_up, bias_branch):
    s, dp = lax.axis_index("seq"), lax.axis_index("dp")
    ids = jnp.stack([s // 2, s % 2, dp % 4, dp // 4]).astype(jnp.int32)

    def compact(blocks):
        own, give = run(pick_kernel, [((ROWS, D), BF)] * 2, ids, counts, *blocks)
        return own, core_swap(give)

    token_blocks = x_gather(tokens[0])
    first, rest0, rest1 = run(
        pack_kernel, [((64, 512), BF), ((64, 1920), BF), ((64, 1536), BF)], ids,
        away(w_qkv), away(w_out), away(w_up), away(w_down), away(norm_gain), away(norm_shift), away(bias_branch),
        away(bias_qv), away(bias_up),
        scratch=[pltpu.VMEM((64, 384), BF), pltpu.VMEM((2, 8, 64, 128), BF), pltpu.VMEM((3, 2, 2, 64), BF),
                 pltpu.VMEM((2, 128), BF), pltpu.VMEM((2, 256), BF), pltpu.SemaphoreType.DMA((31,))])
    rest0 = lax.all_gather(rest0, "dp", axis=0, tiled=True)
    rest1 = lax.all_gather(rest1, "dp", axis=0, tiled=True)
    source = list(compact(token_blocks))
    first, = run(order_kernel, [((4, 64, 512), BF)], ids, *dp_gather(first, 1), after=[source[0]])
    first, vec, qkv_bias, up_bias = run(
        unpack_kernel, [((D, 512), BF), ((16, D), F32), ((8, 384), F32), ((8, 512), F32)], ids, *dp_gather(first, 4),
        scratch=[pltpu.VMEM((16, 64, 512), BF)])
    first_far = core_swap(first)

    own, far = compact(x_gather(cotangent[0]))
    dz, dh, mark = run(join_kernel, in_hbm([((ROWS, D), BF), ((BLOCK, D), F32)]) + [MARK], own, far)
    dh = saved(dh)

    full = lambda *dtypes: [((ROWS, D), t) for t in dtypes]
    sent = [((BLOCK, D), BF)] * 4
    kept = []
    for l in range(2):
        outs = full(F32, BF) + [((ROWS, 256), BF), ((ROWS, 512), BF)]
        if l == 0:
            hidden, a, q, kv = run(functools.partial(qkv_kernel, l), outs, ids, vec, qkv_bias, *source, first, first_far,
                                   after=[mark], us=2)
        else:
            hidden, a, q, kv, middle0, g0, slope0 = run(
                functools.partial(qkv_kernel, l), outs + [((BLOCK, D), F32, "away")] + [((ROWS, D), BF, "away")] * 2,
                ids, vec, qkv_bias, *source, g, slope, *rests[0], scratch=held(2, D, 384) + [pltpu.SemaphoreType.DMA((3,))], us=3)
            kept[0][-3:] = [saved(v) for v in (middle0, g0, slope0)]
        kv_far = core_swap(kv)
        outs = [((ROWS, 256), BF), ((ROWS, 128), F32)]
        if l == 0:
            mixed, lse, q, kv, hidden, a, first, first_far = run(
                attend_kernel, outs + [(s, t, "away") for s, t in (
                    ((ROWS, 256), BF), ((2 * ROWS, 512), BF), ((ROWS, D), F32), ((ROWS, D), BF), ((D, 512), BF), ((D, 512), BF))],
                ids, q, kv, kv_far, hidden, a, first, first_far, scratch=[pltpu.SemaphoreType.DMA((7,))], us=4)
            rest0, lse = later(rest0, lse)
            rests = [[away(rest0), ("any", core_swap(rest0))]]
            hidden, a, q, kvs, lse = saved(hidden), saved(a), saved(q), [saved(kv)], saved(lse)
        else:
            mixed, lse = run(attend_kernel, outs, ids, q, kv, kv_far, us=3)
            kvs = [kv, kv_far]
            rest1, lse = later(rest1, lse)
            rests.append([away(rest1), ("any", core_swap(rest1))])
        mixes = x_gather(mixed)
        outs = [((ROWS, D), BF, "away")] * 2 if l == 0 else full(BF, BF)
        extra = [pltpu.VMEM((ROWS, D), BF)] * 2 + [pltpu.SemaphoreType.DMA((2,))] if l == 0 else []
        near, = load(ids, [(rests[l][0][1], (3, D, 512), lanes_of(512, 0, 1024))])
        room = held(3, D, 512)
        all_mixed, normed, middle, g, slope, *parts = run(
            functools.partial(mlp_kernel, l), outs + full(F32, BF, BF) + sent + ([((3, D, 512), BF)] if l else []),
            ids, vec, up_bias, *mixes, hidden, near, rests[l][1],
            scratch=[pltpu.VMEM((ROWS, 512), F32)] + (room[1:] if l else room) + extra, us=6)
        if l:
            *parts, near_far = parts
            near = [near, near_far]
        if l == 0:
            all_mixed, normed = saved(all_mixed), saved(normed)
            mlp, mark = run(sum_kernel, [((BLOCK, D), BF), LOOSE], *x_scatter(parts))
            source = [middle, *x_gather(mlp)]
        kept.append([hidden, a, q, kvs, lse, all_mixed, normed, middle, g, slope])

    dz = [(saved(dz), (BLOCK, D), (j, 0)) for j in range(4)]
    swapped = lambda v: v + [core_swap(b) for b in v]
    last_parts, last_rows = parts, (saved(middle), (BLOCK, D), (0, 0))
    rests[0][1] = away(rests[0][1][1])
    keep = lambda v: v if isinstance(v, tuple) else saved(v)
    tiny = []
    for l in (1, 0):
        hidden, a, q, kvs, lse, all_mixed, normed, middle, g, slope = kept[l]
        qkv = rests[0] if l else [away(first), away(first_far)]
        if l == 0:
            weights0 = lanes_of(0, 1024)
            *near, slope_v = load(ids, [(rests[0][0][1], (2, D, 512), weights0), (rests[0][1][1], (2, D, 512), weights0),
                                        (slope[1], (ROWS, D), None)], after=[mark_add, dh])
            slope = slope_v
        top = lambda v: (v, (BLOCK, D), (0, 0))
        dz_all, du, up_sum, *parts = run(
            mlp_back_kernel, full(BF, BF) + [((8, D), F32)] + sent, ids, *dz, slope, *near,
            after=[mark_add] if l == 0 else (), us=4)
        errs = x_scatter(parts)
        mlp_mine, mlp_other, sums_grad = run(mlp_grad_kernel, [((D, D), BF)] * 2 + [LOOSE], ids, normed, du, g, dz_all, us=4)
        dm, dmb, sums1 = run(functools.partial(norm_back_kernel, 2 * l + 1),
                             [((BLOCK, D), F32), ((BLOCK, D), BF), ((8, D), F32)], vec, top(middle), dh, *errs,
                             after=[sums_grad], us=1 if l else 8)
        mlp_came = core_swap(mlp_other)
        dmbs = x_gather(dmb)
        if l == 0:
            rows = lambda ids: [(pl.ds(pl.multiple_of(256 * ids[0], 256), 256), pl.ds(512, 512))]
            q, lse, kvs, w_near, w_far, *near = load(ids, [
                (q[1], (ROWS, 256), None), (lse[1], (ROWS, 128), None), (kvs[0][1], (2 * ROWS, 512), None),
                (first, (1, D, 384), lanes_of(0, width=384)), (first_far, (1, D, 384), lanes_of(0, width=384)),
                (rests[0][0][1], (1, 256, 512), rows), (rests[0][1][1], (1, 256, 512), rows)], after=[dm])
            kvs, qkv = [kvs], [w_near, w_far]
        before = []
        if l == 0:
            shares, mark = run(add_kernel, [((D, D), BF, "saved"), LOOSE], mlp_mine, mlp_came, us=3)
            got_mlp = over_dp(shares.reshape(16, 64, D))
            before = [mark]
        dmb_all, dq, dkv, give = run(
            attend_back_kernel, full(BF) + [((ROWS, 256), BF), ((ROWS, 512), F32), ((ROWS, 512), BF)],
            ids, *dmbs, *near, q, lse, *kvs, after=before, us=5 if l else 0.1)
        give = core_swap(give)
        out_mine, out_other, mark_out = run(out_grad_kernel, [((D, 128), BF)] * 2 + [LOOSE], ids, all_mixed, *dmbs, us=2 if l else 0.1)
        out_came = core_swap(out_other)
        high = BLOCK * (2 - l)
        gm, go, qv_sum, *parts = run(
            functools.partial(qkv_back_kernel, 1536 if l else None),
            [((ROWS, 384), BF)] * 2 + [((8, 512), F32)] + [((high, D), BF)] * 4,
            ids, dq, dkv, give, *qkv, *([] if l else map(keep, last_parts)), scratch=held(2, D, 384) if l else (), after=[mark_out], us=3 if l else 0.1)
        errs = x_scatter(parts)
        qkv_mine, qkv_other, sums0 = run(qkv_grad_kernel, [((D, 384), BF)] * 2 + [((8, D), F32)],
                                         keep(a), gm, go, keep(hidden), *parts, us=4 if l else 0.1)
        tiny = [sums1, sums0, up_sum, qv_sum] + tiny
        qkv_came = core_swap(qkv_other)
        qkv_pair = [qkv_mine, qkv_came]
        if l == 1:
            shares, mark_add = run(add_kernel, [((D, 1536), BF, "saved"), LOOSE], mlp_mine, mlp_came,
                                   out_mine, out_came, *qkv_pair, us=4)
            got1 = lax.psum_scatter(shares, "dp", scatter_dimension=0, tiled=True)
        else:
            rest, = run(rest_kernel, in_hbm([((16, 64, 640), BF)]), ids, out_mine, out_came, *qkv_pair, *tiny, us=0.1)
            got_rest = over_dp(rest)
        if l == 1:
            dh, dz = run(functools.partial(norm_back_kernel, 2), [((BLOCK, D), F32), ((BLOCK, D), BF)],
                         vec, top(hidden), dm, *errs)
            dz = x_gather(dz)
        else:
            dz, = run(functools.partial(norm_back_kernel, 0), [((2 * BLOCK + 64, D), BF)],
                      vec, top(hidden), saved(dm), *errs, last_rows, got_mlp, after=[rest], us=2)
    grad_tokens, output, g_up, g_down = finish(
        early_kernel, ids, swapped(x_gather(dz)),
        [((1, 128, D), BF, None, 0)] * 2 + [((2, 64, 4096), F32, 1, 0), ((2, 256, 1024), F32, 1, 0)], D, first=[counts])
    total_rest, = run(total_kernel, [((64, 2176), BF)], got_rest, got1)
    g_out, g_qkv, g_gain, g_shift, g_branch, g_qv, g_upb, g_up, g_down = finish(
        late_kernel, ids, swapped(x_gather(total_rest)),
        [((2, 64, 1024), F32, 2, 0), ((2, 64, 3072), F32, 2, 0)] + [((2, 2, 64), F32, None, 0)] * 3
        + [((2, 128), F32, None, 0), ((2, 256), F32, None, 0), ((2, 64, 4096), F32, 1, 1), ((2, 256, 1024), F32, 1, 1)],
        2176, before=(g_up, g_down), at=7)
    return (output, grad_tokens, g_qkv, g_out, g_up, g_down, g_gain, g_shift, g_qv, g_upb, g_branch)


def solution(mesh):
    rows = P("dp", "seq", None)
    mid = P(None, "dp", None)
    end = P(None, None, "dp")
    two = P(None, "dp")
    return jax.shard_map(
        shards,
        mesh=mesh,
        in_specs=(rows, P("dp", None), rows, mid, mid, mid, mid, end, end, two, two, end),
        out_specs=(rows, rows, mid, mid, mid, mid, end, end, two, two, end),
        check_vma=False,
    )
```

```python
import functools

import jax
import jax.numpy as jnp
from jax import lax
from jax.experimental import pallas as pl
from jax.experimental.pallas import tpu as pltpu
from jax.sharding import PartitionSpec as P

EPSILON = 1e-06
BF = jnp.bfloat16
F32 = jnp.float32
BLOCK = 80
SHARE = 73
TOTAL = 577
ROWS = 4 * BLOCK
D = 1024
LOOSE = ((8, 128), jnp.float32)
MARK = ((8, 128), jnp.float32, "saved")
LIMIT = 24

NEXT = [(i, (i + 2) % 8) for i in range(8)]
PREV = [(i, (i - 2) % 8) for i in range(8)]
FAR = [(i, (i + 4) % 8) for i in range(8)]
CORE = [(i, i ^ 1) for i in range(8)]


def x_gather(block):
    two = lax.ppermute(block, "seq", PREV)
    four = lax.ppermute(block, "seq", NEXT)
    return [block, two, lax.ppermute(block, "seq", FAR), four]


def x_scatter(blocks):
    three = lax.ppermute(blocks[2], "seq", FAR)
    return [blocks[0], lax.ppermute(blocks[1], "seq", NEXT), three, lax.ppermute(blocks[3], "seq", PREV)]


def core_swap(v):
    return lax.ppermute(v, "seq", CORE)


def dp_pairs(step, k):
    if step == 1:
        return [(i, i // 4 * 4 + (i + k) % 4) for i in range(16)]
    return [(i, (i + 4 * k) % 16) for i in range(16)]


def dp_scatter(blocks, step):
    return [blocks[0]] + [lax.ppermute(blocks[k], "dp", dp_pairs(step, k)) for k in (1, 2, 3)]


def dp_gather(block, step):
    return [block] + [lax.ppermute(block, "dp", dp_pairs(step, -k)) for k in (1, 2, 3)]


def dot(a, b):
    return jnp.dot(a, b, preferred_element_type=F32)


def dot_nt(a, b):
    return lax.dot_general(a, b, (((1,), (1,)), ((), ())), preferred_element_type=F32)


def dot_tn(a, b):
    return lax.dot_general(a, b, (((0,), (0,)), ((), ())), preferred_element_type=F32)


def cols(ref, at, width):
    return ref.at[:, pl.ds(pl.multiple_of(at, 128), width)]


def norm_parts(rows):
    mean = jnp.mean(rows, axis=-1, keepdims=True)
    centered = rows - mean
    rstd = lax.rsqrt(jnp.mean(centered * centered, axis=-1, keepdims=True) + EPSILON)
    return centered * rstd, rstd


def away(v):
    return ("away", v)


def saved(v):
    return ("saved", v)


def in_hbm(outs):
    return [o + ("saved",) for o in outs]


def run(kernel, outs, *ins, scratch=(), after=(), us=1.0):
    once = pl.Buffered(1)
    small = lambda v: v.size < 200000
    hbm = lambda v: pltpu.with_memory_space_constraint(v, pltpu.HBM)
    whole = lambda s: pl.BlockSpec(s, functools.partial(lambda n, _: (0,) * n, len(s)), pipeline_mode=once)
    specs, arrays = [], []
    for v in ins:
        if isinstance(v, tuple) and len(v) == 2:
            kind, v = v
            specs.append(whole(v.shape) if kind == "saved" else pl.BlockSpec(memory_space=pl.ANY if kind == "any" else pltpu.HBM))
            v = v if kind == "any" else hbm(v)
        elif isinstance(v, tuple):
            v, block, index = v
            specs.append(pl.BlockSpec(block, functools.partial(lambda at, _: at, index), pipeline_mode=once))
            if isinstance(v, tuple):
                v = hbm(v[1])
        elif v.dtype == jnp.int32:
            specs.append(pl.BlockSpec(memory_space=pltpu.SMEM))
        else:
            specs.append(whole(v.shape))
        arrays.append(v)
    specs += [pl.BlockSpec(memory_space=pl.ANY if small(v) else pltpu.HBM) for v in after]
    n = len(arrays)
    body = lambda *refs: kernel(*refs[:n], *refs[n + len(after):])
    kinds = [o[2] if len(o) > 2 else "" for o in outs]
    return pl.pallas_call(
        body,
        grid=(1,),
        in_specs=specs,
        out_specs=[pl.BlockSpec(memory_space=pltpu.HBM) if k == "away" else whole(o[0]) for k, o in zip(kinds, outs)],
        out_shape=[pltpu.HBM(o[0], o[1]) if k else jax.ShapeDtypeStruct(o[0], o[1]) for k, o in zip(kinds, outs)],
        scratch_shapes=list(scratch),
        compiler_params=pltpu.CompilerParams(vmem_limit_bytes=LIMIT << 20),
        cost_estimate=pl.CostEstimate(flops=int(us * 1.0 * 1.15e9), bytes_accessed=1, transcendentals=0),
    )(*arrays, *[v if small(v) else hbm(v) for v in after])


def fetch(parts, buf, sem):
    copies = [pltpu.make_async_copy(v, buf.at[i], sem.at[i]) for i, v in enumerate(parts)]
    for copy in copies:
        copy.start()
    return copies


def send(pairs, sem):
    copies = [pltpu.make_async_copy(v, out, sem.at[i]) for i, (v, out) in enumerate(pairs)]
    for copy in copies:
        copy.start()
    return copies


def held(count, rows, width):
    return [pltpu.VMEM((count, rows, width), BF), pltpu.SemaphoreType.DMA((count,))]


def load_kernel(slices, ids, *refs):
    n = len(slices)
    sources, outs, sem = refs[:n], refs[n:-1], refs[-1]
    copies = []
    for part, source, out in zip(slices, sources, outs):
        for i, at in enumerate(part(ids) if part else [None]):
            copies.append(pltpu.make_async_copy(source if at is None else source.at[at], out if at is None else out.at[i],
                                                sem.at[len(copies)]))
            copies[-1].start()
    for copy in copies:
        copy.wait()


def load(ids, parts, after=()):
    count = sum(s[0] if p else 1 for _, s, p in parts)
    return run(functools.partial(load_kernel, [p for _, _, p in parts]), [(s, BF if v.dtype == BF else F32) for v, s, _ in parts],
               ids, *[away(v) for v, _, _ in parts], scratch=[pltpu.SemaphoreType.DMA((count,))], after=after, us=2)


def store_kernel(*refs):
    n = (len(refs) - 2) // 2
    mark, sem = refs[-2], refs[-1]
    mark[...] = jnp.zeros_like(mark)
    pairs = [(v.at[pl.ds(0, out.shape[0]), :], out) for v, out in zip(refs[:n], refs[n:])]
    for copy in send(pairs, sem):
        copy.wait()


def store(parts, after):
    outs = [((rows, v.shape[1]), v.dtype, "away") for v, rows in parts]
    return run(store_kernel, outs + [LOOSE], *[v for v, _ in parts], scratch=[pltpu.SemaphoreType.DMA((len(parts),))],
               after=after, us=2)


def lanes_of(*at, width=512):
    return lambda ids: [(slice(None), pl.ds(i, width)) for i in at]


def half_ranks(shape, axis, x, core):
    at = lax.broadcasted_iota(jnp.int32, shape, axis)
    block = sum((at >= BLOCK * i).astype(jnp.int32) for i in (1, 2, 3))
    within = at - BLOCK * block
    chip = x + block
    chip = jnp.where(chip >= 4, chip - 4, chip)
    rank = (4 * core + chip) * SHARE + within
    return jnp.where((within < SHARE) & (rank < TOTAL), rank, -2)


def slot_ranks(shape, axis, counts, s):
    at = lax.broadcasted_iota(jnp.int32, shape, axis)
    start = sum(jnp.where(i < s, counts[0, i], 0) for i in range(8))
    return jnp.where(at < counts[0, s], start + at, -1)


def kept_keys(x, c):
    at = lax.broadcasted_iota(jnp.int32, (1, 2 * ROWS), 1)
    second = (at >= ROWS).astype(jnp.int32)
    at = at - ROWS * second
    block = sum((at >= BLOCK * i).astype(jnp.int32) for i in (1, 2, 3))
    chip = x + block
    chip = jnp.where(chip >= 4, chip - 4, chip)
    core = jnp.where(second > 0, 1 - c, c)
    within = at - BLOCK * block
    return (within < SHARE) & ((4 * core + chip) * SHARE + within < TOTAL)


def pick_kernel(ids, counts, t0, t1, t2, t3, own_ref, far_ref):
    x, c = ids[0], ids[1]
    rows = jnp.concatenate([t[...] for t in (t0, t1, t2, t3)], axis=0)
    slots = [slot_ranks((1, 128), 1, counts, 2 * lax.rem(x + j, 4) + c) for j in range(4)]
    for core, out in ((c, own_ref), (1 - c, far_ref)):
        rank = half_ranks((ROWS, 1), 0, x, core)
        pick = jnp.concatenate([jnp.where(rank == s, 1.0, 0.0) for s in slots], axis=1)
        out[...] = dot(pick.astype(BF), rows).astype(BF)


def join_kernel(own, far, dz_ref, dh_ref, mark):
    mark[...] = jnp.zeros_like(mark)
    dz = own[...] + far[...]
    dz_ref[...] = dz
    dh_ref[...] = dz[:BLOCK, :].astype(F32)


def pack_kernel(ids, w_qkv, w_out, w_up, w_down, gain, shift, branch, qv, up,
                first_ref, rest0_ref, rest1_ref, qkv_buf, up_buf, norm_buf, qv_buf, wide_buf, sem):
    x, c = ids[0], ids[1]
    lanes = lambda at, width: pl.ds(pl.multiple_of(at, 128), width)
    copies = []

    def copy(source, target):
        copies.append(pltpu.make_async_copy(source, target, sem.at[len(copies)]))
        copies[-1].start()

    rests = (rest0_ref, rest1_ref)
    for l in range(2):
        for m in range(3):
            target = qkv_buf.at[:, pl.ds(128 * m, 128)] if l == 0 else rest0_ref.at[:, pl.ds(1536 + 128 * m, 128)]
            copy(w_qkv.at[l, :, lanes(D * m + 256 * x + 128 * c, 128)], target)
        for d in range(8):
            copy(w_up.at[l, :, lanes(2048 * c + 256 * d + 128 * (x // 2), 128)], up_buf.at[l, d])
        copy(w_out.at[l, :, lanes(512 * c, 512)], rests[l].at[:, pl.ds(512, 512)])
        copy(w_down.at[l, pl.ds(pl.multiple_of(64 * x, 64), 64), lanes(512 * c, 512)], rests[l].at[:, pl.ds(1024, 512)])
    for i, v in enumerate((gain, shift, branch)):
        copy(v, norm_buf.at[i])
    copy(qv, qv_buf)
    copy(up, wide_buf)
    for each in copies:
        each.wait()
    pairs = lambda i: jnp.concatenate([norm_buf[i, 0], norm_buf[i, 1]], axis=0).astype(F32)
    wide = wide_buf[...].astype(F32)
    small = jnp.concatenate([
        jnp.concatenate([pairs(0), pairs(1)], axis=1),
        jnp.concatenate([pairs(2), jnp.zeros((4, 64), F32)], axis=1),
        qv_buf[...].astype(F32),
        wide[0:1, :128], wide[0:1, 128:], wide[1:2, :128], wide[1:2, 128:],
        jnp.zeros((50, 128), F32)], axis=0).astype(BF)
    block = jnp.concatenate([qkv_buf[...], small], axis=1)
    first_ref[...] = block
    odd = lax.rem(x, 2) == 1
    for l in range(2):
        got = []
        for d in range(8):
            piece = up_buf[l, d].astype(F32)
            got.append(jnp.where(odd, piece[:, 64:], piece[:, :64]))
        rests[l][:, :512] = jnp.concatenate(got, axis=1).astype(BF)


def order_kernel(ids, a, b, c, d, out):
    for i, v in enumerate((a, b, c, d)):
        out[lax.rem(ids[2] + i, 4)] = v[...]


def unpack_kernel(ids, a, b, c, d, first_ref, vec_ref, qkv_ref, up_ref, first):
    for i, v in enumerate((a, b, c, d)):
        for y in range(4):
            first[4 * lax.rem(ids[3] + i, 4) + y] = v[y]
    for i in range(16):
        first_ref[64 * i:64 * (i + 1), :] = first[i]
    x, c = ids[0], ids[1]
    rows = [first[d, 0:16, 384:].astype(F32) for d in range(16)]
    line = lambda at, lanes: jnp.concatenate([r[at:at + 4, lanes:lanes + 64] for r in rows], axis=1)
    vec_ref[...] = jnp.concatenate([line(0, 0), line(0, 64), line(4, 0), jnp.zeros((4, D), F32)], axis=0)
    qkv, up = [], []
    for l in range(2):
        for core in (c, 1 - c):
            q = first[2 * x + core, 0:16, 384:].astype(F32)[8 + l:9 + l]
            v = first[8 + 2 * x + core, 0:16, 384:].astype(F32)[8 + l:9 + l]
            qkv.append(jnp.concatenate([q, jnp.zeros((1, 128), F32), v], axis=1))
            got = []
            for d in range(8):
                r = first[8 * core + d, 0:16, 384:].astype(F32)
                r = jnp.where(x >= 2, r[11 + 2 * l:12 + 2 * l], r[10 + 2 * l:11 + 2 * l])
                got.append(jnp.where(lax.rem(x, 2) == 1, r[:, 64:], r[:, :64]))
            up.append(jnp.concatenate(got, axis=1))
    qkv_ref[...] = jnp.concatenate(qkv + [jnp.zeros((4, 384), F32)], axis=0)
    up_ref[...] = jnp.concatenate(up + [jnp.zeros((4, 512), F32)], axis=0)


def qkv_kernel(l, ids, vec, bias, *refs):
    gain, shift = vec[2 * l:2 * l + 1, :], vec[4 + 2 * l:5 + 2 * l, :]
    first = l == 0
    if first:
        own, far, wm, wo, h_ref, a_ref, q_ref, kv_ref = refs
        weight = lambda i: (wm, wo)[i][:, :384]
    else:
        m, d0, d1, d2, d3, wm, wo, h_ref, a_ref, q_ref, kv_ref, buf, sem = refs
        branch = vec[9:10, :]
        copies = fetch([w.at[:, pl.ds(1536, 384)] for w in (wm, wo)], buf, sem)

        def weight(i):
            copies[i].wait()
            return buf[i]

    c = ids[1]
    for r in range(0, ROWS, 16):
        rows = slice(r, r + 16)
        if first:
            h = own[rows, :].astype(F32) + far[rows, :].astype(F32)
        else:
            b, o = divmod(r, BLOCK)
            h = m[rows, :] + (d0, d1, d2, d3)[b][o:o + 16, :].astype(F32) + branch
        h_ref[rows, :] = h
        a_ref[rows, :] = (norm_parts(h)[0] * gain + shift).astype(BF)
    a = a_ref[...]
    for i in range(2):
        core = c if i == 0 else 1 - c
        packed = (dot(a, weight(i)) + bias[2 * l + i:2 * l + i + 1, :]).astype(BF)
        cols(q_ref, 128 * core, 128)[...] = packed[:, :128]
        cols(kv_ref, 128 * core, 128)[...] = packed[:, 128:256]
        cols(kv_ref, 256 + 128 * core, 128)[...] = packed[:, 256:]


def head_mask(rows, sub):
    lane = lax.broadcasted_iota(jnp.int32, (rows, 128), 1)
    return (lane < 64) if sub == 0 else (lane >= 64)


def attend_kernel(ids, q_ref, kv_ref, far_ref, *refs):
    keeps = []
    if len(refs) == 2:
        mixed_ref, lse_ref = refs
    else:
        n = (len(refs) - 5) // 2
        mixed_ref, lse_ref = refs[n:n + 2]
        outs, sem = refs[n + 2:-1], refs[-1]
        keeps = send([(q_ref, outs[0]), (kv_ref, outs[1].at[pl.ds(0, ROWS), :]),
                      (far_ref, outs[1].at[pl.ds(ROWS, ROWS), :])], sem)
        keeps += send(list(zip(refs[:n], outs[2:])), sem.at[pl.ds(3, n)])
    low = head_mask(ROWS, 0)
    keep = kept_keys(ids[0], ids[1])
    lane = lax.broadcasted_iota(jnp.int32, (ROWS, 128), 1)
    lses = jnp.zeros((ROWS, 128), F32)
    for pair in range(2):
        at = 128 * pair
        k = jnp.concatenate([kv_ref[:, at:at + 128], far_ref[:, at:at + 128]], axis=0)
        v = jnp.concatenate([kv_ref[:, 256 + at:384 + at], far_ref[:, 256 + at:384 + at]], axis=0)
        q = q_ref[:, at:at + 128]
        got = []
        for sub in range(2):
            qm = jnp.where(low if sub == 0 else ~low, q, jnp.zeros_like(q))
            s = dot_nt(qm, k) * 0.125
            s = jnp.where(keep, s, -1e9)
            top = jnp.max(s, axis=-1, keepdims=True)
            e = jnp.exp(s - top)
            total = jnp.sum(e, axis=-1, keepdims=True)
            got.append(dot((e * (1.0 / total)).astype(BF), v))
            lses = jnp.where(lane == 2 * pair + sub, top + jnp.log(total), lses)
        mixed_ref[:, at:at + 128] = jnp.where(low, got[0], got[1]).astype(BF)
    lse_ref[...] = lses
    for keep in keeps:
        keep.wait()


def mlp_kernel(l, ids, vec, up_bias, mx0, mx1, mx2, mx3, h, near, wo, *refs):
    x, c = ids[0], ids[1]
    all_ref, c_ref, m_ref, g_ref, slope_ref, p0, p1, p2, p3, *room, sem = refs
    u_ref, buf = room if l == 0 else room[::-1]
    copies = fetch([wo.at[:, pl.ds(at, 512)] for at in (512, 0, 1024)], buf, sem)

    def weight(i):
        if i % 2 == 0:
            return near[i // 2]
        copies[i // 2].wait()
        return buf[i // 2]

    gain, shift, branch = (vec[i + 2 * l:i + 1 + 2 * l, :] for i in (1, 5, 8))
    for j, mx in enumerate((mx0, mx1, mx2, mx3)):
        at = 256 * lax.rem(x + j, 4)
        for b in range(4):
            to = BLOCK * ((j + b) % 4)
            all_ref[to:to + BLOCK, pl.ds(pl.multiple_of(at, 128), 256)] = mx[BLOCK * b:BLOCK * (b + 1), :]
    mixed = all_ref[...]
    for i in range(2):
        core = c if i == 0 else 1 - c
        cols(m_ref, 512 * core, 512)[...] = dot(mixed, weight(i))
    for r in range(0, ROWS, 16):
        rows = slice(r, r + 16)
        m = h[rows, :] + m_ref[rows, :] + branch
        m_ref[rows, :] = m
        c_ref[rows, :] = (norm_parts(m)[0] * gain + shift).astype(BF)
    normed = c_ref[...]
    for i in range(2):
        core = c if i == 0 else 1 - c
        slope_part = cols(slope_ref, 512 * core, 512)
        g_part = cols(g_ref, 512 * core, 512)
        u_ref[...] = dot(normed, weight(2 + i)) + up_bias[2 * l + i:2 * l + i + 1, :]
        for r in range(0, ROWS, 32):
            rows = pl.ds(r, 32)
            u = u_ref[rows, :]
            half = 0.5 + 0.5 * lax.erf(u * 0.7071067811865476)
            g_part[rows, :] = (u * half).astype(BF)
            slope_part[rows, :] = (half + u * (0.3989422804014327 * jnp.exp(-0.5 * u * u))).astype(BF)
    g = g_ref[...]
    for i in range(2):
        core = c if i == 0 else 1 - c
        part = dot(g, weight(4 + i)).astype(BF)
        for j, out in enumerate((p0, p1, p2, p3)):
            cols(out, 512 * core, 512)[...] = part[BLOCK * j:BLOCK * (j + 1), :]


def sum_kernel(a, b, c, d, out, mark):
    mark[...] = jnp.zeros_like(mark)
    out[...] = (a[...].astype(F32) + b[...].astype(F32) + c[...].astype(F32) + d[...].astype(F32)).astype(BF)


def mlp_back_kernel(ids, z0, z1, z2, z3, slope, *refs):
    near, near_far, dz_ref, du_ref, sum_ref, p0, p1, p2, p3 = refs
    weight = lambda i: (near, near_far)[i % 2][near.shape[0] - 1 - i // 2]
    c = ids[1]
    for j, z in enumerate((z0, z1, z2, z3)):
        dz_ref[BLOCK * j:BLOCK * (j + 1), :] = z[...]
    dact = (dot_nt(cols(dz_ref, 512 * c, 512)[...], weight(0))
            + dot_nt(cols(dz_ref, 512 * (1 - c), 512)[...], weight(1)))
    du_ref[...] = (dact * slope[...].astype(F32)).astype(BF)
    part = (dot_nt(cols(du_ref, 512 * c, 512)[...], weight(2))
            + dot_nt(cols(du_ref, 512 * (1 - c), 512)[...], weight(3)))
    part = part.astype(BF)
    for j, out in enumerate((p0, p1, p2, p3)):
        out[...] = part[BLOCK * j:BLOCK * (j + 1), :]
    sums = jnp.sum(du_ref[...].astype(F32), axis=0, keepdims=True)
    sum_ref[...] = jnp.broadcast_to(sums, (8, D))


def norm_back_kernel(row, vec, base, above, e0, e1, e2, e3, *refs):
    final = len(refs) == 3 and refs[2].shape[0] > BLOCK
    if final:
        last, got, db_ref = refs
    else:
        d_ref, db_ref, sum_ref = refs if len(refs) == 3 else (*refs, None)
    gain = vec[row:row + 1, :]
    totals = [jnp.zeros((16, D), F32) for _ in range(4)]
    for r in range(0, BLOCK, 16):
        rows = slice(r, r + 16)
        e = e0[rows, :].astype(F32) + e1[rows, :].astype(F32) + e2[rows, :].astype(F32) + e3[rows, :].astype(F32)
        n, rstd = norm_parts(base[rows, :])
        eg = e * gain
        back = rstd * (eg - jnp.mean(eg, axis=-1, keepdims=True) - n * jnp.mean(eg * n, axis=-1, keepdims=True))
        up = above[rows, :]
        d = up + back
        db = d.astype(BF)
        db_ref[rows, :] = db
        if final:
            late = slice(BLOCK + r, BLOCK + r + 16)
            sums = sum(v[late, :].astype(F32) for v in (e0, e1, e2, e3))
            db_ref[late, :] = (last[rows, :] + sums + vec[11:12, :]).astype(BF)
            continue
        d_ref[rows, :] = d
        if sum_ref is not None:
            for i, t in enumerate((e * n, e, db.astype(F32), up.astype(BF).astype(F32))):
                totals[i] = totals[i] + t
    if final:
        total = got[0].astype(F32)
        for d in range(1, 16):
            total = total + got[d].astype(F32)
        db_ref[2 * BLOCK:, :] = total.astype(BF)
    elif sum_ref is not None:
        out = [jnp.sum(t, axis=0, keepdims=True) for t in totals]
        sum_ref[...] = jnp.concatenate(out + out, axis=0)


def attend_back_kernel(ids, z0, z1, z2, z3, *refs):
    near, near_far, q_ref, lse_ref, *kvs, dmb_ref, dq_ref, dkv_ref, give_ref = refs
    x, c = ids[0], ids[1]
    part = pl.ds(pl.multiple_of(256 * x, 256), 256)
    for j, z in enumerate((z0, z1, z2, z3)):
        dmb_ref[BLOCK * j:BLOCK * (j + 1), :] = z[:BLOCK, :]
    weight = lambda i: (near, near_far)[i][0] if near.shape[1] == 256 else (near, near_far)[i][0, part, :]
    dmixed = (dot_nt(cols(dmb_ref, 512 * c, 512)[...], weight(0))
              + dot_nt(cols(dmb_ref, 512 * (1 - c), 512)[...], weight(1))).astype(BF)
    low = head_mask(ROWS, 0)
    keep = kept_keys(ids[0], ids[1])
    lane = lax.broadcasted_iota(jnp.int32, (ROWS, 128), 1)
    for pair in range(2):
        at = 128 * pair
        k, v = (jnp.concatenate([ref[:, i + at:i + at + 128] for ref in kvs], axis=0) for i in (0, 256))
        q = q_ref[:, at:at + 128]
        dmp = dmixed[:, at:at + 128]
        dqs = []
        dk = jnp.zeros((2 * ROWS, 128), F32)
        dv = jnp.zeros((2 * ROWS, 128), F32)
        for sub in range(2):
            mask = low if sub == 0 else ~low
            qm = jnp.where(mask, q, jnp.zeros_like(q))
            dmm = jnp.where(mask, dmp, jnp.zeros_like(dmp))
            lse = jnp.sum(jnp.where(lane == 2 * pair + sub, lse_ref[...], 0.0), axis=-1, keepdims=True)
            s = dot_nt(qm, k) * 0.125
            p = jnp.exp(jnp.where(keep, s, -1e9) - lse)
            dp = dot_nt(dmm, v)
            inner = jnp.sum(dp * p, axis=-1, keepdims=True)
            ds = (p * (dp - inner)).astype(BF)
            dqs.append(dot(ds, k))
            dk = dk + dot_tn(ds, qm)
            dv = dv + dot_tn(p.astype(BF), dmm)
        dq_ref[:, at:at + 128] = (jnp.where(low, dqs[0], dqs[1]) * 0.125).astype(BF)
        dk = dk * 0.125
        dkv_ref[:, at:at + 128] = dk[:ROWS]
        dkv_ref[:, 256 + at:384 + at] = dv[:ROWS]
        give_ref[:, at:at + 128] = dk[ROWS:].astype(BF)
        give_ref[:, 256 + at:384 + at] = dv[ROWS:].astype(BF)


def qkv_back_kernel(at, ids, dq, dkv, far, wm, wo, *refs):
    if at is None:
        lasts, (gm_ref, go_ref, sum_ref, p0, p1, p2, p3) = refs[:-7], refs[-7:]
        weight = lambda i: (wm, wo)[i][0]
    else:
        lasts, (gm_ref, go_ref, sum_ref, p0, p1, p2, p3, buf, sem) = refs[:-9], refs[-9:]
        copies = fetch([w.at[:, pl.ds(at, 384)] for w in (wm, wo)], buf, sem)

        def weight(i):
            copies[i].wait()
            return buf[i]

    c = ids[1]
    part = None
    sum_ref[...] = jnp.zeros((8, 512), F32)
    for i, g in enumerate((gm_ref, go_ref)):
        core = c if i == 0 else 1 - c
        g[:, :128] = cols(dq, 128 * core, 128)[...]
        g[:, 128:256] = (cols(dkv, 128 * core, 128)[...] + cols(far, 128 * core, 128)[...].astype(F32)).astype(BF)
        g[:, 256:] = (cols(dkv, 256 + 128 * core, 128)[...]
                      + cols(far, 256 + 128 * core, 128)[...].astype(F32)).astype(BF)
        got = dot_nt(g[...], weight(i))
        part = got if part is None else part + got
        total = jnp.sum(g[...].astype(F32), axis=0, keepdims=True)
        cols(sum_ref, 128 * core, 128)[0:1, :] = total[:, :128]
        cols(sum_ref, 256 + 128 * core, 128)[0:1, :] = total[:, 256:]
    part = part.astype(BF)
    for j, out in enumerate((p0, p1, p2, p3)):
        out[:BLOCK, :] = part[BLOCK * j:BLOCK * (j + 1), :]
        if lasts:
            out[BLOCK:, :] = lasts[j][...]


def mlp_grad_kernel(ids, normed, du, g, dz, mine_ref, other_ref, mark):
    mark[...] = jnp.zeros_like(mark)
    c = ids[1]
    for at, left, right in ((0, normed, du), (512, g, dz)):
        turned = left[...].T
        for i, out in enumerate((mine_ref, other_ref)):
            core = c if i == 0 else 1 - c
            out[:, at:at + 512] = dot(turned, cols(right, 512 * core, 512)[...]).astype(BF)


def out_grad_kernel(ids, mixed, z0, z1, z2, z3, mine_ref, other_ref, mark):
    mark[...] = jnp.zeros_like(mark)
    x, c = ids[0], ids[1]
    turned = mixed[...].T
    for i, out in enumerate((mine_ref, other_ref)):
        core = c if i == 0 else 1 - c
        dmb = jnp.concatenate([cols(z, 256 * x + 128 * core, 128)[:BLOCK, :] for z in (z0, z1, z2, z3)], axis=0)
        out[...] = dot(turned, dmb).astype(BF)


def qkv_grad_kernel(a, gm, go, h, p0, p1, p2, p3, mine_ref, other_ref, sum_ref):
    turned = a[...].T
    mine_ref[...] = dot(turned, gm[...]).astype(BF)
    other_ref[...] = dot(turned, go[...]).astype(BF)
    gain = jnp.zeros((16, D), F32)
    shift = jnp.zeros((16, D), F32)
    for j, p in enumerate((p0, p1, p2, p3)):
        for r in range(0, BLOCK, 16):
            e = p[r:r + 16, :].astype(F32)
            gain = gain + e * norm_parts(h[BLOCK * j + r:BLOCK * j + r + 16, :])[0]
            shift = shift + e
    out = [jnp.sum(t, axis=0, keepdims=True) for t in (gain, shift)]
    sum_ref[...] = jnp.concatenate(out * 4, axis=0)


def add_kernel(*refs):
    out, mark, at = refs[-2], refs[-1], 0
    mark[...] = jnp.zeros_like(mark)
    for mine, came in zip(refs[:-2:2], refs[1:-2:2]):
        width = mine.shape[1]
        out[:, at:at + width] = (mine[...].astype(F32) + came[...].astype(F32)).astype(BF)
        at += width


def total_kernel(got, more, out):
    total = got[0].astype(F32)
    for d in range(1, 16):
        total = total + got[d].astype(F32)
    width = got.shape[2]
    out[:, :width] = total.astype(BF)
    out[:, width:] = more[...]


def write_gradient(name, layer, ref, all_ref, at):
    for core in range(2):
        if name == "up":
            for d in range(8):
                to = 256 * (8 * core + d)
                ref[layer, :, to:to + 256] = jnp.concatenate(
                    [all_ref[chip, core, :, at + 64 * d:at + 64 * (d + 1)] for chip in range(4)], axis=1).astype(F32)
        for chip in range(4):
            to = 256 * chip + 128 * core
            block = lambda i, width: all_ref[chip, core, :, at + i:at + i + width].astype(F32)
            if name == "down":
                ref[layer, 64 * chip:64 * (chip + 1), 512 * core:512 * (core + 1)] = block(0, 512)
            if name == "out":
                ref[layer, :, to:to + 128] = block(0, 128)
            if name == "qkv":
                for m in range(3):
                    ref[layer, :, D * m + to:D * m + to + 128] = block(128 * m, 128)


def arrange(ids, blocks, all_ref, at):
    x, c = ids[0], ids[1]
    for i in range(2):
        for j in range(4):
            all_ref[lax.rem(x + j, 4), c if i == 0 else 1 - c] = blocks[4 * i + j][at:, :]


def early_kernel(ids, counts, *refs):
    blocks, (tokens_ref, output_ref, up, down), all_ref = refs[:8], refs[8:12], refs[12]
    x, c = ids[0], ids[1]
    ranks = jnp.concatenate([half_ranks((1, ROWS), 1, x, core) for core in (c, 1 - c)], axis=1)
    put = jnp.where(slot_ranks((128, 1), 0, counts, 2 * x + c) == ranks, 1.0, 0.0).astype(BF)
    for i, ref in enumerate((tokens_ref, output_ref)):
        rows = jnp.concatenate([t[BLOCK * i:BLOCK * (i + 1), :] for t in blocks], axis=0)
        ref[0] = dot(put, rows).astype(BF)
    arrange(ids, blocks, all_ref, 2 * BLOCK)
    write_gradient("up", 0, up, all_ref, 0)
    write_gradient("down", 0, down, all_ref, 512)


def late_kernel(ids, *refs):
    blocks = refs[:8]
    (out, qkv, gain_ref, shift_ref, branch_ref, qv_ref, up_ref, up, down), all_ref = refs[-10:-1], refs[-1]
    arrange(ids, blocks, all_ref, 0)
    for name, layer, ref, at in (("out", 0, out, 0), ("qkv", 0, qkv, 128), ("up", 0, up, 640), ("down", 0, down, 1152),
                                 ("out", 1, out, 1664), ("qkv", 1, qkv, 1792)):
        write_gradient(name, layer, ref, all_ref, at)
    part = [sum(all_ref[chip, core, 0:16, 512:640].astype(F32) for core in range(2)) for chip in range(4)]
    total = part[0] + part[1] + part[2] + part[3]
    for l in range(2):
        for i, small in enumerate((gain_ref, shift_ref, branch_ref)):
            row = total[5 * l + i:5 * l + i + 1]
            small[l] = jnp.concatenate([row[:, :64], row[:, 64:]], axis=0)
        qv_ref[l:l + 1, :] = total[5 * l + 4:5 * l + 5]
        up_ref[l:l + 1, :] = jnp.concatenate([p[5 * l + 3:5 * l + 4, :64] for p in part], axis=1)


def finish(kernel, ids, blocks, outs, width, before=(), at=0, first=()):
    once = pl.Buffered(1)
    whole = lambda s: pl.BlockSpec(s, functools.partial(lambda n, _: (0,) * n, len(s)), pipeline_mode=once)
    out_specs = [whole(s) if n is None else pl.BlockSpec((n,) + s[1:], functools.partial(lambda at, _: (at, 0, 0), at),
                                                         pipeline_mode=once) for s, _, n, at in outs]
    n = 1 + len(first) + len(blocks)
    return pl.pallas_call(
        kernel,
        grid=(1,),
        in_specs=[pl.BlockSpec(memory_space=pltpu.SMEM)] * (1 + len(first)) + [whole(b.shape) for b in blocks]
        + [pl.BlockSpec(memory_space=pl.ANY)] * len(before),
        out_specs=out_specs,
        out_shape=[pltpu.HBM(s, t) for s, t, _, _ in outs],
        scratch_shapes=[pltpu.VMEM((4, 2, 64, width), BF)],
        input_output_aliases={n + i: at + i for i in range(len(before))},
        compiler_params=pltpu.CompilerParams(vmem_limit_bytes=LIMIT << 20),
        cost_estimate=pl.CostEstimate(flops=int(4e9), bytes_accessed=1, transcendentals=0),
    )(ids, *first, *blocks, *before)


def rest_kernel(ids, out_mine, out_came, qkv_mine, qkv_came, *refs):
    x, out = ids[0], refs[-1]
    for d in range(16):
        at = slice(64 * d, 64 * (d + 1))
        out[d, :, :128] = (out_mine[at, :].astype(F32) + out_came[at, :].astype(F32)).astype(BF)
        out[d, :, 128:512] = (qkv_mine[at, :].astype(F32) + qkv_came[at, :].astype(F32)).astype(BF)
        rows = []
        for l in range(2):
            one, zero, up, qv = refs[4 * l:4 * l + 4]
            pair = lambda u, v: jnp.concatenate([u, v], axis=1)
            rows += [pair(zero[0:1, at], one[0:1, at]), pair(zero[1:2, at], one[1:2, at]),
                     pair(one[2:3, at], one[3:4, at]), pair(up[0:1, at], jnp.zeros((1, 64), F32))]
            lanes = 256 * (d // 8) + 128 * (d % 2)
            rows.append(jnp.where(x == d % 8 // 2, qv[0:1, lanes:lanes + 128], 0.0))
        out[d, :, 512:] = jnp.concatenate(rows + [jnp.zeros((54, 128), F32)], axis=0).astype(BF)


def later(v, *others):
    return lax.optimization_barrier((v, *others))


def over_dp(v):
    return lax.all_to_all(v, "dp", split_axis=0, concat_axis=0, tiled=True)


def shards(tokens, counts, cotangent, w_qkv, w_out, w_up, w_down, norm_gain, norm_shift,
           bias_qv, bias_up, bias_branch):
    s, dp = lax.axis_index("seq"), lax.axis_index("dp")
    ids = jnp.stack([s // 2, s % 2, dp % 4, dp // 4]).astype(jnp.int32)

    def compact(blocks):
        own, give = run(pick_kernel, [((ROWS, D), BF)] * 2, ids, counts, *blocks)
        return own, core_swap(give)

    token_blocks = x_gather(tokens[0])
    first, rest0, rest1 = run(
        pack_kernel, [((64, 512), BF), ((64, 1920), BF), ((64, 1536), BF)], ids,
        away(w_qkv), away(w_out), away(w_up), away(w_down), away(norm_gain), away(norm_shift), away(bias_branch),
        away(bias_qv), away(bias_up),
        scratch=[pltpu.VMEM((64, 384), BF), pltpu.VMEM((2, 8, 64, 128), BF), pltpu.VMEM((3, 2, 2, 64), BF),
                 pltpu.VMEM((2, 128), BF), pltpu.VMEM((2, 256), BF), pltpu.SemaphoreType.DMA((31,))])
    rest0 = lax.all_gather(rest0, "dp", axis=0, tiled=True)
    rest1 = lax.all_gather(rest1, "dp", axis=0, tiled=True)
    source = list(compact(token_blocks))
    first, = run(order_kernel, [((4, 64, 512), BF)], ids, *dp_gather(first, 1), after=[source[0]])
    first, vec, qkv_bias, up_bias = run(
        unpack_kernel, [((D, 512), BF), ((16, D), F32), ((8, 384), F32), ((8, 512), F32)], ids, *dp_gather(first, 4),
        scratch=[pltpu.VMEM((16, 64, 512), BF)])
    first_far = core_swap(first)

    own, far = compact(x_gather(cotangent[0]))
    dz, dh, mark = run(join_kernel, in_hbm([((ROWS, D), BF), ((BLOCK, D), F32)]) + [MARK], own, far)
    dh = saved(dh)

    full = lambda *dtypes: [((ROWS, D), t) for t in dtypes]
    sent = [((BLOCK, D), BF)] * 4
    kept = []
    for l in range(2):
        outs = full(F32, BF) + [((ROWS, 256), BF), ((ROWS, 512), BF)]
        if l == 0:
            hidden, a, q, kv = run(functools.partial(qkv_kernel, l), outs, ids, vec, qkv_bias, *source, first, first_far,
                                   after=[mark], us=2)
        else:
            hidden, a, q, kv = run(functools.partial(qkv_kernel, l), outs, ids, vec, qkv_bias, *source, *rests[0],
                                   scratch=held(2, D, 384), after=[mark], us=3)
        kv_far = core_swap(kv)
        outs = [((ROWS, 256), BF), ((ROWS, 128), F32)]
        if l == 0:
            mixed, lse, q, kv, hidden, a, first, first_far = run(
                attend_kernel, outs + [(s, t, "away") for s, t in (
                    ((ROWS, 256), BF), ((2 * ROWS, 512), BF), ((ROWS, D), F32), ((ROWS, D), BF), ((D, 512), BF), ((D, 512), BF))],
                ids, q, kv, kv_far, hidden, a, first, first_far, scratch=[pltpu.SemaphoreType.DMA((7,))], us=4)
            rest0, lse = later(rest0, lse)
            rests = [[away(rest0), ("any", core_swap(rest0))]]
            hidden, a, q, kvs, lse = saved(hidden), saved(a), saved(q), [saved(kv)], saved(lse)
        else:
            mixed, lse = run(attend_kernel, outs, ids, q, kv, kv_far, us=3)
            kvs = [kv, kv_far]
            rest1, lse = later(rest1, lse)
            rests.append([away(rest1), ("any", core_swap(rest1))])
        mixes = x_gather(mixed)
        parts = [(rests[l][0][1], (3, D, 512), lanes_of(512, 0, 1024))]
        if l == 0:
            near, = load(ids, parts)
        else:
            near, a, hidden = load(ids, parts + [(a, (ROWS, D), None), (hidden, (ROWS, D), None)])
        room = held(3, D, 512)
        all_mixed, normed, middle, g, slope, *parts = run(
            functools.partial(mlp_kernel, l), full(BF, BF, F32, BF, BF) + sent + ([((3, D, 512), BF)] if l else []),
            ids, vec, up_bias, *mixes, hidden, near, rests[l][1],
            scratch=[pltpu.VMEM((ROWS, 512), F32)] + (room[1:] if l else room), us=6)
        if l:
            *parts, near_far = parts
            near = [near, near_far]
        if l == 0:
            mlp, mark = run(sum_kernel, [((BLOCK, D), BF), LOOSE], *x_scatter(parts))
            source = [middle, *x_gather(mlp)]
            *stored, mark = store([(all_mixed, ROWS), (normed, ROWS), (middle, BLOCK), (g, ROWS), (slope, ROWS)], [mark])
            all_mixed, normed, middle, g, slope = map(saved, stored)
        kept.append([hidden, a, q, kvs, lse, all_mixed, normed, middle, g, slope])

    dz = [(saved(dz), (BLOCK, D), (j, 0)) for j in range(4)]
    swapped = lambda v: v + [core_swap(b) for b in v]
    last_parts, last_rows = parts, (saved(middle), (BLOCK, D), (0, 0))
    rests[0][1] = away(rests[0][1][1])
    keep = lambda v: v if isinstance(v, tuple) else saved(v)
    tiny = []
    for l in (1, 0):
        hidden, a, q, kvs, lse, all_mixed, normed, middle, g, slope = kept[l]
        qkv = rests[0] if l else [away(first), away(first_far)]
        if l == 0:
            weights0 = lanes_of(0, 1024)
            *near, slope, normed, g = load(ids, [(rests[0][0][1], (2, D, 512), weights0), (rests[0][1][1], (2, D, 512), weights0),
                                        (slope[1], (ROWS, D), None), (normed[1], (ROWS, D), None),
                                        (g[1], (ROWS, D), None)], after=[mark_add, dh])
        top = lambda v: (v, (BLOCK, D), (0, 0))
        dz_all, du, up_sum, *parts = run(
            mlp_back_kernel, full(BF, BF) + [((8, D), F32)] + sent, ids, *dz, slope, *near,
            after=[mark_add] if l == 0 else (), us=4)
        errs = x_scatter(parts)
        mlp_mine, mlp_other, sums_grad = run(mlp_grad_kernel, [((D, D), BF)] * 2 + [LOOSE], ids, normed, du, g, dz_all, us=4)
        dm, dmb, sums1 = run(functools.partial(norm_back_kernel, 2 * l + 1),
                             [((BLOCK, D), F32), ((BLOCK, D), BF), ((8, D), F32)], vec, top(middle), dh, *errs,
                             after=[sums_grad], us=1 if l else 8)
        mlp_came = core_swap(mlp_other)
        dmbs = x_gather(dmb)
        if l == 0:
            rows = lambda ids: [(pl.ds(pl.multiple_of(256 * ids[0], 256), 256), pl.ds(512, 512))]
            q, lse, kvs, w_near, w_far, *near = load(ids, [
                (q[1], (ROWS, 256), None), (lse[1], (ROWS, 128), None), (kvs[0][1], (2 * ROWS, 512), None),
                (first, (1, D, 384), lanes_of(0, width=384)), (first_far, (1, D, 384), lanes_of(0, width=384)),
                (rests[0][0][1], (1, 256, 512), rows), (rests[0][1][1], (1, 256, 512), rows)], after=[dm])
            kvs, qkv = [kvs], [w_near, w_far]
        before = []
        if l == 0:
            shares, mark = run(add_kernel, [((D, D), BF, "saved"), LOOSE], mlp_mine, mlp_came, us=3)
            got_mlp = over_dp(shares.reshape(16, 64, D))
            before = [mark]
        dmb_all, dq, dkv, give = run(
            attend_back_kernel, full(BF) + [((ROWS, 256), BF), ((ROWS, 512), F32), ((ROWS, 512), BF)],
            ids, *dmbs, *near, q, lse, *kvs, after=before, us=5 if l else 0.1)
        give = core_swap(give)
        out_mine, out_other, mark_out = run(out_grad_kernel, [((D, 128), BF)] * 2 + [LOOSE], ids, all_mixed, *dmbs, us=2 if l else 0.1)
        out_came = core_swap(out_other)
        high = BLOCK * (2 - l)
        gm, go, qv_sum, *parts = run(
            functools.partial(qkv_back_kernel, 1536 if l else None),
            [((ROWS, 384), BF)] * 2 + [((8, 512), F32)] + [((high, D), BF)] * 4,
            ids, dq, dkv, give, *qkv, *([] if l else map(keep, last_parts)), scratch=held(2, D, 384) if l else (), after=[mark_out], us=3 if l else 0.1)
        errs = x_scatter(parts)
        qkv_mine, qkv_other, sums0 = run(qkv_grad_kernel, [((D, 384), BF)] * 2 + [((8, D), F32)],
                                         a, gm, go, hidden, *parts, us=4 if l else 0.1)
        tiny = [sums1, sums0, up_sum, qv_sum] + tiny
        qkv_came = core_swap(qkv_other)
        qkv_pair = [qkv_mine, qkv_came]
        if l == 1:
            shares, mark_add = run(add_kernel, [((D, 1536), BF, "saved"), LOOSE], mlp_mine, mlp_came,
                                   out_mine, out_came, *qkv_pair, us=4)
            got1 = lax.psum_scatter(shares, "dp", scatter_dimension=0, tiled=True)
        else:
            rest, = run(rest_kernel, in_hbm([((16, 64, 640), BF)]), ids, out_mine, out_came, *qkv_pair, *tiny, us=0.1)
            got_rest = over_dp(rest)
        if l == 1:
            dh, dz = run(functools.partial(norm_back_kernel, 2), [((BLOCK, D), F32), ((BLOCK, D), BF)],
                         vec, top(hidden), dm, *errs, after=[mark_add])
            dz = x_gather(dz)
        else:
            dz, = run(functools.partial(norm_back_kernel, 0), [((2 * BLOCK + 64, D), BF)],
                      vec, top(hidden), saved(dm), *errs, last_rows, got_mlp, after=[rest], us=2)
    grad_tokens, output, g_up, g_down = finish(
        early_kernel, ids, swapped(x_gather(dz)),
        [((1, 128, D), BF, None, 0)] * 2 + [((2, 64, 4096), F32, 1, 0), ((2, 256, 1024), F32, 1, 0)], D, first=[counts])
    total_rest, = run(total_kernel, [((64, 2176), BF)], got_rest, saved(got1))
    g_out, g_qkv, g_gain, g_shift, g_branch, g_qv, g_upb, g_up, g_down = finish(
        late_kernel, ids, swapped(x_gather(total_rest)),
        [((2, 64, 1024), F32, 2, 0), ((2, 64, 3072), F32, 2, 0)] + [((2, 2, 64), F32, None, 0)] * 3
        + [((2, 128), F32, None, 0), ((2, 256), F32, None, 0), ((2, 64, 4096), F32, 1, 1), ((2, 256, 1024), F32, 1, 1)],
        2176, before=(g_up, g_down), at=7)
    return (output, grad_tokens, g_qkv, g_out, g_up, g_down, g_gain, g_shift, g_qv, g_upb, g_branch)


def solution(mesh):
    rows = P("dp", "seq", None)
    mid = P(None, "dp", None)
    end = P(None, None, "dp")
    two = P(None, "dp")
    return jax.shard_map(
        shards,
        mesh=mesh,
        in_specs=(rows, P("dp", None), rows, mid, mid, mid, mid, end, end, two, two, end),
        out_specs=(rows, rows, mid, mid, mid, mid, end, end, two, two, end),
        check_vma=False,
    )
```

```python
import functools

import jax
import jax.numpy as jnp
from jax import lax
from jax.experimental import pallas as pl
from jax.experimental.pallas import tpu as pltpu
from jax.sharding import PartitionSpec as P

EPSILON = 1e-06
BF = jnp.bfloat16
F32 = jnp.float32
BLOCK = 80
SHARE = 73
TOTAL = 577
ROWS = 4 * BLOCK
D = 1024
LOOSE = ((8, 128), jnp.float32)
MARK = ((8, 128), jnp.float32, "saved")
LIMIT = 24

NEXT = [(i, (i + 2) % 8) for i in range(8)]
PREV = [(i, (i - 2) % 8) for i in range(8)]
FAR = [(i, (i + 4) % 8) for i in range(8)]
CORE = [(i, i ^ 1) for i in range(8)]


def x_gather(block):
    two = lax.ppermute(block, "seq", PREV)
    four = lax.ppermute(block, "seq", NEXT)
    return [block, two, lax.ppermute(block, "seq", FAR), four]


def x_scatter(blocks):
    three = lax.ppermute(blocks[2], "seq", FAR)
    return [blocks[0], lax.ppermute(blocks[1], "seq", NEXT), three, lax.ppermute(blocks[3], "seq", PREV)]


def core_swap(v):
    return lax.ppermute(v, "seq", CORE)


def dp_pairs(step, k):
    if step == 1:
        return [(i, i // 4 * 4 + (i + k) % 4) for i in range(16)]
    return [(i, (i + 4 * k) % 16) for i in range(16)]


def dp_scatter(blocks, step):
    return [blocks[0]] + [lax.ppermute(blocks[k], "dp", dp_pairs(step, k)) for k in (1, 2, 3)]


def dp_gather(block, step):
    return [block] + [lax.ppermute(block, "dp", dp_pairs(step, -k)) for k in (1, 2, 3)]


def dot(a, b):
    return jnp.dot(a, b, preferred_element_type=F32)


def dot_nt(a, b):
    return lax.dot_general(a, b, (((1,), (1,)), ((), ())), preferred_element_type=F32)


def dot_tn(a, b):
    return lax.dot_general(a, b, (((0,), (0,)), ((), ())), preferred_element_type=F32)


def cols(ref, at, width):
    return ref.at[:, pl.ds(pl.multiple_of(at, 128), width)]


def norm_parts(rows):
    mean = jnp.mean(rows, axis=-1, keepdims=True)
    centered = rows - mean
    rstd = lax.rsqrt(jnp.mean(centered * centered, axis=-1, keepdims=True) + EPSILON)
    return centered * rstd, rstd


def away(v):
    return ("away", v)


def saved(v):
    return ("saved", v)


def in_hbm(outs):
    return [o + ("saved",) for o in outs]


def run(kernel, outs, *ins, scratch=(), after=(), us=1.0):
    once = pl.Buffered(1)
    small = lambda v: v.size < 200000
    hbm = lambda v: pltpu.with_memory_space_constraint(v, pltpu.HBM)
    whole = lambda s: pl.BlockSpec(s, functools.partial(lambda n, _: (0,) * n, len(s)), pipeline_mode=once)
    specs, arrays = [], []
    for v in ins:
        if isinstance(v, tuple) and len(v) == 2:
            kind, v = v
            specs.append(whole(v.shape) if kind == "saved" else pl.BlockSpec(memory_space=pl.ANY if kind == "any" else pltpu.HBM))
            v = v if kind == "any" else hbm(v)
        elif isinstance(v, tuple):
            v, block, index = v
            specs.append(pl.BlockSpec(block, functools.partial(lambda at, _: at, index), pipeline_mode=once))
            if isinstance(v, tuple):
                v = hbm(v[1])
        elif v.dtype == jnp.int32:
            specs.append(pl.BlockSpec(memory_space=pltpu.SMEM))
        else:
            specs.append(whole(v.shape))
        arrays.append(v)
    specs += [pl.BlockSpec(memory_space=pl.ANY if small(v) else pltpu.HBM) for v in after]
    n = len(arrays)
    body = lambda *refs: kernel(*refs[:n], *refs[n + len(after):])
    kinds = [o[2] if len(o) > 2 else "" for o in outs]
    return pl.pallas_call(
        body,
        grid=(1,),
        in_specs=specs,
        out_specs=[pl.BlockSpec(memory_space=pltpu.HBM) if k == "away" else whole(o[0]) for k, o in zip(kinds, outs)],
        out_shape=[pltpu.HBM(o[0], o[1]) if k else jax.ShapeDtypeStruct(o[0], o[1]) for k, o in zip(kinds, outs)],
        scratch_shapes=list(scratch),
        compiler_params=pltpu.CompilerParams(vmem_limit_bytes=LIMIT << 20),
        cost_estimate=pl.CostEstimate(flops=int(us * 1.0 * 1.15e9), bytes_accessed=1, transcendentals=0),
    )(*arrays, *[v if small(v) else hbm(v) for v in after])


def fetch(parts, buf, sem):
    copies = [pltpu.make_async_copy(v, buf.at[i], sem.at[i]) for i, v in enumerate(parts)]
    for copy in copies:
        copy.start()
    return copies


def send(pairs, sem):
    copies = [pltpu.make_async_copy(v, out, sem.at[i]) for i, (v, out) in enumerate(pairs)]
    for copy in copies:
        copy.start()
    return copies


def held(count, rows, width):
    return [pltpu.VMEM((count, rows, width), BF), pltpu.SemaphoreType.DMA((count,))]


def load_kernel(slices, ids, *refs):
    n = len(slices)
    sources, outs, sem = refs[:n], refs[n:-1], refs[-1]
    copies = []
    for part, source, out in zip(slices, sources, outs):
        for i, at in enumerate(part(ids) if part else [None]):
            copies.append(pltpu.make_async_copy(source if at is None else source.at[at], out if at is None else out.at[i],
                                                sem.at[len(copies)]))
            copies[-1].start()
    for copy in copies:
        copy.wait()


def load(ids, parts, after=()):
    count = sum(s[0] if p else 1 for _, s, p in parts)
    return run(functools.partial(load_kernel, [p for _, _, p in parts]), [(s, BF if v.dtype == BF else F32) for v, s, _ in parts],
               ids, *[away(v) for v, _, _ in parts], scratch=[pltpu.SemaphoreType.DMA((count,))], after=after, us=2)


def store_kernel(*refs):
    n = (len(refs) - 2) // 2
    mark, sem = refs[-2], refs[-1]
    mark[...] = jnp.zeros_like(mark)
    pairs = [(v.at[pl.ds(0, out.shape[0]), :], out) for v, out in zip(refs[:n], refs[n:])]
    for copy in send(pairs, sem):
        copy.wait()


def store(parts, after):
    outs = [((rows, v.shape[1]), v.dtype, "away") for v, rows in parts]
    return run(store_kernel, outs + [LOOSE], *[v for v, _ in parts], scratch=[pltpu.SemaphoreType.DMA((len(parts),))],
               after=after, us=2)


def lanes_of(*at, width=512):
    return lambda ids: [(slice(None), pl.ds(i, width)) for i in at]


def half_ranks(shape, axis, x, core):
    at = lax.broadcasted_iota(jnp.int32, shape, axis)
    block = sum((at >= BLOCK * i).astype(jnp.int32) for i in (1, 2, 3))
    within = at - BLOCK * block
    chip = x + block
    chip = jnp.where(chip >= 4, chip - 4, chip)
    rank = (4 * core + chip) * SHARE + within
    return jnp.where((within < SHARE) & (rank < TOTAL), rank, -2)


def slot_ranks(shape, axis, counts, s):
    at = lax.broadcasted_iota(jnp.int32, shape, axis)
    start = sum(jnp.where(i < s, counts[0, i], 0) for i in range(8))
    return jnp.where(at < counts[0, s], start + at, -1)


def kept_keys(x, c):
    at = lax.broadcasted_iota(jnp.int32, (1, 2 * ROWS), 1)
    second = (at >= ROWS).astype(jnp.int32)
    at = at - ROWS * second
    block = sum((at >= BLOCK * i).astype(jnp.int32) for i in (1, 2, 3))
    chip = x + block
    chip = jnp.where(chip >= 4, chip - 4, chip)
    core = jnp.where(second > 0, 1 - c, c)
    within = at - BLOCK * block
    return (within < SHARE) & ((4 * core + chip) * SHARE + within < TOTAL)


def pick_kernel(ids, counts, t0, t1, t2, t3, own_ref, far_ref):
    x, c = ids[0], ids[1]
    rows = jnp.concatenate([t[...] for t in (t0, t1, t2, t3)], axis=0)
    slots = [slot_ranks((1, 128), 1, counts, 2 * lax.rem(x + j, 4) + c) for j in range(4)]
    for core, out in ((c, own_ref), (1 - c, far_ref)):
        rank = half_ranks((ROWS, 1), 0, x, core)
        pick = jnp.concatenate([jnp.where(rank == s, 1.0, 0.0) for s in slots], axis=1)
        out[...] = dot(pick.astype(BF), rows).astype(BF)


def join_kernel(own, far, dz_ref, dh_ref, mark):
    mark[...] = jnp.zeros_like(mark)
    dz = own[...] + far[...]
    dz_ref[...] = dz
    dh_ref[...] = dz[:BLOCK, :].astype(F32)


def pack_kernel(ids, w_qkv, w_out, w_up, w_down, gain, shift, branch, qv, up,
                first_ref, rest0_ref, rest1_ref, qkv_buf, up_buf, norm_buf, qv_buf, wide_buf, sem):
    x, c = ids[0], ids[1]
    lanes = lambda at, width: pl.ds(pl.multiple_of(at, 128), width)
    copies = []

    def copy(source, target):
        copies.append(pltpu.make_async_copy(source, target, sem.at[len(copies)]))
        copies[-1].start()

    rests = (rest0_ref, rest1_ref)
    for l in range(2):
        for m in range(3):
            target = qkv_buf.at[:, pl.ds(128 * m, 128)] if l == 0 else rest0_ref.at[:, pl.ds(1536 + 128 * m, 128)]
            copy(w_qkv.at[l, :, lanes(D * m + 256 * x + 128 * c, 128)], target)
        for d in range(8):
            copy(w_up.at[l, :, lanes(2048 * c + 256 * d + 128 * (x // 2), 128)], up_buf.at[l, d])
        copy(w_out.at[l, :, lanes(512 * c, 512)], rests[l].at[:, pl.ds(512, 512)])
        copy(w_down.at[l, pl.ds(pl.multiple_of(64 * x, 64), 64), lanes(512 * c, 512)], rests[l].at[:, pl.ds(1024, 512)])
    for i, v in enumerate((gain, shift, branch)):
        copy(v, norm_buf.at[i])
    copy(qv, qv_buf)
    copy(up, wide_buf)
    for each in copies:
        each.wait()
    pairs = lambda i: jnp.concatenate([norm_buf[i, 0], norm_buf[i, 1]], axis=0).astype(F32)
    wide = wide_buf[...].astype(F32)
    small = jnp.concatenate([
        jnp.concatenate([pairs(0), pairs(1)], axis=1),
        jnp.concatenate([pairs(2), jnp.zeros((4, 64), F32)], axis=1),
        qv_buf[...].astype(F32),
        wide[0:1, :128], wide[0:1, 128:], wide[1:2, :128], wide[1:2, 128:],
        jnp.zeros((50, 128), F32)], axis=0).astype(BF)
    block = jnp.concatenate([qkv_buf[...], small], axis=1)
    first_ref[...] = block
    odd = lax.rem(x, 2) == 1
    for l in range(2):
        got = []
        for d in range(8):
            piece = up_buf[l, d].astype(F32)
            got.append(jnp.where(odd, piece[:, 64:], piece[:, :64]))
        rests[l][:, :512] = jnp.concatenate(got, axis=1).astype(BF)


def order_kernel(ids, a, b, c, d, out):
    for i, v in enumerate((a, b, c, d)):
        out[lax.rem(ids[2] + i, 4)] = v[...]


def unpack_kernel(ids, a, b, c, d, first_ref, vec_ref, qkv_ref, up_ref, first):
    for i, v in enumerate((a, b, c, d)):
        for y in range(4):
            first[4 * lax.rem(ids[3] + i, 4) + y] = v[y]
    for i in range(16):
        first_ref[64 * i:64 * (i + 1), :] = first[i]
    x, c = ids[0], ids[1]
    rows = [first[d, 0:16, 384:].astype(F32) for d in range(16)]
    line = lambda at, lanes: jnp.concatenate([r[at:at + 4, lanes:lanes + 64] for r in rows], axis=1)
    vec_ref[...] = jnp.concatenate([line(0, 0), line(0, 64), line(4, 0), jnp.zeros((4, D), F32)], axis=0)
    qkv, up = [], []
    for l in range(2):
        for core in (c, 1 - c):
            q = first[2 * x + core, 0:16, 384:].astype(F32)[8 + l:9 + l]
            v = first[8 + 2 * x + core, 0:16, 384:].astype(F32)[8 + l:9 + l]
            qkv.append(jnp.concatenate([q, jnp.zeros((1, 128), F32), v], axis=1))
            got = []
            for d in range(8):
                r = first[8 * core + d, 0:16, 384:].astype(F32)
                r = jnp.where(x >= 2, r[11 + 2 * l:12 + 2 * l], r[10 + 2 * l:11 + 2 * l])
                got.append(jnp.where(lax.rem(x, 2) == 1, r[:, 64:], r[:, :64]))
            up.append(jnp.concatenate(got, axis=1))
    qkv_ref[...] = jnp.concatenate(qkv + [jnp.zeros((4, 384), F32)], axis=0)
    up_ref[...] = jnp.concatenate(up + [jnp.zeros((4, 512), F32)], axis=0)


def qkv_kernel(l, ids, vec, bias, *refs):
    gain, shift = vec[2 * l:2 * l + 1, :], vec[4 + 2 * l:5 + 2 * l, :]
    first = l == 0
    if first:
        own, far, wm, wo, h_ref, a_ref, q_ref, kv_ref = refs
        weight = lambda i: (wm, wo)[i][:, :384]
    else:
        m, d0, d1, d2, d3, wm, wo, h_ref, a_ref, q_ref, kv_ref, buf, sem = refs
        branch = vec[9:10, :]
        copies = fetch([w.at[:, pl.ds(1536, 384)] for w in (wm, wo)], buf, sem)

        def weight(i):
            copies[i].wait()
            return buf[i]

    c = ids[1]
    for r in range(0, ROWS, 16):
        rows = slice(r, r + 16)
        if first:
            h = own[rows, :].astype(F32) + far[rows, :].astype(F32)
        else:
            b, o = divmod(r, BLOCK)
            h = m[rows, :] + (d0, d1, d2, d3)[b][o:o + 16, :].astype(F32) + branch
        h_ref[rows, :] = h
        a_ref[rows, :] = (norm_parts(h)[0] * gain + shift).astype(BF)
    a = a_ref[...]
    for i in range(2):
        core = c if i == 0 else 1 - c
        packed = (dot(a, weight(i)) + bias[2 * l + i:2 * l + i + 1, :]).astype(BF)
        cols(q_ref, 128 * core, 128)[...] = packed[:, :128]
        cols(kv_ref, 128 * core, 128)[...] = packed[:, 128:256]
        cols(kv_ref, 256 + 128 * core, 128)[...] = packed[:, 256:]


def head_mask(rows, sub):
    lane = lax.broadcasted_iota(jnp.int32, (rows, 128), 1)
    return (lane < 64) if sub == 0 else (lane >= 64)


def attend_kernel(ids, q_ref, kv_ref, far_ref, *refs):
    keeps = []
    if len(refs) == 2:
        mixed_ref, lse_ref = refs
    else:
        n = (len(refs) - 5) // 2
        mixed_ref, lse_ref = refs[n:n + 2]
        outs, sem = refs[n + 2:-1], refs[-1]
        keeps = send([(q_ref, outs[0]), (kv_ref, outs[1].at[pl.ds(0, ROWS), :]),
                      (far_ref, outs[1].at[pl.ds(ROWS, ROWS), :])], sem)
        keeps += send(list(zip(refs[:n], outs[2:])), sem.at[pl.ds(3, n)])
    low = head_mask(ROWS, 0)
    keep = kept_keys(ids[0], ids[1])
    lane = lax.broadcasted_iota(jnp.int32, (ROWS, 128), 1)
    lses = jnp.zeros((ROWS, 128), F32)
    for pair in range(2):
        at = 128 * pair
        k = jnp.concatenate([kv_ref[:, at:at + 128], far_ref[:, at:at + 128]], axis=0)
        v = jnp.concatenate([kv_ref[:, 256 + at:384 + at], far_ref[:, 256 + at:384 + at]], axis=0)
        q = q_ref[:, at:at + 128]
        got = []
        for sub in range(2):
            qm = jnp.where(low if sub == 0 else ~low, q, jnp.zeros_like(q))
            s = dot_nt(qm, k) * 0.125
            s = jnp.where(keep, s, -1e9)
            top = jnp.max(s, axis=-1, keepdims=True)
            e = jnp.exp(s - top)
            total = jnp.sum(e, axis=-1, keepdims=True)
            got.append(dot((e * (1.0 / total)).astype(BF), v))
            lses = jnp.where(lane == 2 * pair + sub, top + jnp.log(total), lses)
        mixed_ref[:, at:at + 128] = jnp.where(low, got[0], got[1]).astype(BF)
    lse_ref[...] = lses
    for keep in keeps:
        keep.wait()


def mlp_kernel(l, ids, vec, up_bias, mx0, mx1, mx2, mx3, h, near, wo, *refs):
    x, c = ids[0], ids[1]
    all_ref, c_ref, m_ref, g_ref, slope_ref, p0, p1, p2, p3, *room, sem = refs
    u_ref, buf = room if l == 0 else room[::-1]
    copies = fetch([wo.at[:, pl.ds(at, 512)] for at in (512, 0, 1024)], buf, sem)

    def weight(i):
        if i % 2 == 0:
            return near[i // 2]
        copies[i // 2].wait()
        return buf[i // 2]

    gain, shift, branch = (vec[i + 2 * l:i + 1 + 2 * l, :] for i in (1, 5, 8))
    for j, mx in enumerate((mx0, mx1, mx2, mx3)):
        at = 256 * lax.rem(x + j, 4)
        for b in range(4):
            to = BLOCK * ((j + b) % 4)
            all_ref[to:to + BLOCK, pl.ds(pl.multiple_of(at, 128), 256)] = mx[BLOCK * b:BLOCK * (b + 1), :]
    mixed = all_ref[...]
    for i in range(2):
        core = c if i == 0 else 1 - c
        cols(m_ref, 512 * core, 512)[...] = dot(mixed, weight(i))
    for r in range(0, ROWS, 16):
        rows = slice(r, r + 16)
        m = h[rows, :] + m_ref[rows, :] + branch
        m_ref[rows, :] = m
        c_ref[rows, :] = (norm_parts(m)[0] * gain + shift).astype(BF)
    normed = c_ref[...]
    for i in range(2):
        core = c if i == 0 else 1 - c
        slope_part = cols(slope_ref, 512 * core, 512)
        g_part = cols(g_ref, 512 * core, 512)
        u_ref[...] = dot(normed, weight(2 + i)) + up_bias[2 * l + i:2 * l + i + 1, :]
        for r in range(0, ROWS, 32):
            rows = pl.ds(r, 32)
            u = u_ref[rows, :]
            half = 0.5 + 0.5 * lax.erf(u * 0.7071067811865476)
            g_part[rows, :] = (u * half).astype(BF)
            slope_part[rows, :] = (half + u * (0.3989422804014327 * jnp.exp(-0.5 * u * u))).astype(BF)
    g = g_ref[...]
    for i in range(2):
        core = c if i == 0 else 1 - c
        part = dot(g, weight(4 + i)).astype(BF)
        for j, out in enumerate((p0, p1, p2, p3)):
            cols(out, 512 * core, 512)[...] = part[BLOCK * j:BLOCK * (j + 1), :]


def sum_kernel(a, b, c, d, out, mark):
    mark[...] = jnp.zeros_like(mark)
    out[...] = (a[...].astype(F32) + b[...].astype(F32) + c[...].astype(F32) + d[...].astype(F32)).astype(BF)


def mlp_back_kernel(ids, z0, z1, z2, z3, slope, *refs):
    near, near_far, dz_ref, du_ref, sum_ref, p0, p1, p2, p3 = refs
    weight = lambda i: (near, near_far)[i % 2][near.shape[0] - 1 - i // 2]
    c = ids[1]
    for j, z in enumerate((z0, z1, z2, z3)):
        dz_ref[BLOCK * j:BLOCK * (j + 1), :] = z[...]
    dact = (dot_nt(cols(dz_ref, 512 * c, 512)[...], weight(0))
            + dot_nt(cols(dz_ref, 512 * (1 - c), 512)[...], weight(1)))
    du_ref[...] = (dact * slope[...].astype(F32)).astype(BF)
    part = (dot_nt(cols(du_ref, 512 * c, 512)[...], weight(2))
            + dot_nt(cols(du_ref, 512 * (1 - c), 512)[...], weight(3)))
    part = part.astype(BF)
    for j, out in enumerate((p0, p1, p2, p3)):
        out[...] = part[BLOCK * j:BLOCK * (j + 1), :]
    sums = jnp.sum(du_ref[...].astype(F32), axis=0, keepdims=True)
    sum_ref[...] = jnp.broadcast_to(sums, (8, D))


def norm_back_kernel(row, vec, base, above, e0, e1, e2, e3, *refs):
    final = len(refs) == 3 and refs[2].shape[0] > BLOCK
    if final:
        last, got, db_ref = refs
    else:
        d_ref, db_ref, sum_ref = refs if len(refs) == 3 else (*refs, None)
    gain = vec[row:row + 1, :]
    totals = [jnp.zeros((16, D), F32) for _ in range(4)]
    for r in range(0, BLOCK, 16):
        rows = slice(r, r + 16)
        e = e0[rows, :].astype(F32) + e1[rows, :].astype(F32) + e2[rows, :].astype(F32) + e3[rows, :].astype(F32)
        n, rstd = norm_parts(base[rows, :])
        eg = e * gain
        back = rstd * (eg - jnp.mean(eg, axis=-1, keepdims=True) - n * jnp.mean(eg * n, axis=-1, keepdims=True))
        up = above[rows, :]
        d = up + back
        db = d.astype(BF)
        db_ref[rows, :] = db
        if final:
            late = slice(BLOCK + r, BLOCK + r + 16)
            sums = sum(v[late, :].astype(F32) for v in (e0, e1, e2, e3))
            db_ref[late, :] = (last[rows, :] + sums + vec[11:12, :]).astype(BF)
            continue
        d_ref[rows, :] = d
        if sum_ref is not None:
            for i, t in enumerate((e * n, e, db.astype(F32), up.astype(BF).astype(F32))):
                totals[i] = totals[i] + t
    if final:
        total = got[0].astype(F32)
        for d in range(1, 16):
            total = total + got[d].astype(F32)
        db_ref[2 * BLOCK:, :] = total.astype(BF)
    elif sum_ref is not None:
        out = [jnp.sum(t, axis=0, keepdims=True) for t in totals]
        sum_ref[...] = jnp.concatenate(out + out, axis=0)


def attend_back_kernel(ids, z0, z1, z2, z3, *refs):
    near, near_far, q_ref, lse_ref, *kvs, dmb_ref, dq_ref, dkv_ref, give_ref = refs
    x, c = ids[0], ids[1]
    part = pl.ds(pl.multiple_of(256 * x, 256), 256)
    for j, z in enumerate((z0, z1, z2, z3)):
        dmb_ref[BLOCK * j:BLOCK * (j + 1), :] = z[:BLOCK, :]
    weight = lambda i: (near, near_far)[i][0] if near.shape[1] == 256 else (near, near_far)[i][0, part, :]
    dmixed = (dot_nt(cols(dmb_ref, 512 * c, 512)[...], weight(0))
              + dot_nt(cols(dmb_ref, 512 * (1 - c), 512)[...], weight(1))).astype(BF)
    low = head_mask(ROWS, 0)
    keep = kept_keys(ids[0], ids[1])
    lane = lax.broadcasted_iota(jnp.int32, (ROWS, 128), 1)
    for pair in range(2):
        at = 128 * pair
        k, v = (jnp.concatenate([ref[:, i + at:i + at + 128] for ref in kvs], axis=0) for i in (0, 256))
        q = q_ref[:, at:at + 128]
        dmp = dmixed[:, at:at + 128]
        dqs = []
        dk = jnp.zeros((2 * ROWS, 128), F32)
        dv = jnp.zeros((2 * ROWS, 128), F32)
        for sub in range(2):
            mask = low if sub == 0 else ~low
            qm = jnp.where(mask, q, jnp.zeros_like(q))
            dmm = jnp.where(mask, dmp, jnp.zeros_like(dmp))
            lse = jnp.sum(jnp.where(lane == 2 * pair + sub, lse_ref[...], 0.0), axis=-1, keepdims=True)
            s = dot_nt(qm, k) * 0.125
            p = jnp.exp(jnp.where(keep, s, -1e9) - lse)
            dp = dot_nt(dmm, v)
            inner = jnp.sum(dp * p, axis=-1, keepdims=True)
            ds = (p * (dp - inner)).astype(BF)
            dqs.append(dot(ds, k))
            dk = dk + dot_tn(ds, qm)
            dv = dv + dot_tn(p.astype(BF), dmm)
        dq_ref[:, at:at + 128] = (jnp.where(low, dqs[0], dqs[1]) * 0.125).astype(BF)
        dk = dk * 0.125
        dkv_ref[:, at:at + 128] = dk[:ROWS]
        dkv_ref[:, 256 + at:384 + at] = dv[:ROWS]
        give_ref[:, at:at + 128] = dk[ROWS:].astype(BF)
        give_ref[:, 256 + at:384 + at] = dv[ROWS:].astype(BF)


def qkv_back_kernel(at, ids, dq, dkv, far, wm, wo, *refs):
    if at is None:
        lasts, (gm_ref, go_ref, sum_ref, p0, p1, p2, p3) = refs[:-7], refs[-7:]
        weight = lambda i: (wm, wo)[i][0]
    else:
        lasts, (gm_ref, go_ref, sum_ref, p0, p1, p2, p3, buf, sem) = refs[:-9], refs[-9:]
        copies = fetch([w.at[:, pl.ds(at, 384)] for w in (wm, wo)], buf, sem)

        def weight(i):
            copies[i].wait()
            return buf[i]

    c = ids[1]
    part = None
    sum_ref[...] = jnp.zeros((8, 512), F32)
    for i, g in enumerate((gm_ref, go_ref)):
        core = c if i == 0 else 1 - c
        g[:, :128] = cols(dq, 128 * core, 128)[...]
        g[:, 128:256] = (cols(dkv, 128 * core, 128)[...] + cols(far, 128 * core, 128)[...].astype(F32)).astype(BF)
        g[:, 256:] = (cols(dkv, 256 + 128 * core, 128)[...]
                      + cols(far, 256 + 128 * core, 128)[...].astype(F32)).astype(BF)
        got = dot_nt(g[...], weight(i))
        part = got if part is None else part + got
        total = jnp.sum(g[...].astype(F32), axis=0, keepdims=True)
        cols(sum_ref, 128 * core, 128)[0:1, :] = total[:, :128]
        cols(sum_ref, 256 + 128 * core, 128)[0:1, :] = total[:, 256:]
    part = part.astype(BF)
    for j, out in enumerate((p0, p1, p2, p3)):
        out[:BLOCK, :] = part[BLOCK * j:BLOCK * (j + 1), :]
        if lasts:
            out[BLOCK:, :] = lasts[j][...]


def mlp_grad_kernel(ids, normed, du, g, dz, mine_ref, other_ref, mark):
    mark[...] = jnp.zeros_like(mark)
    c = ids[1]
    for at, left, right in ((0, normed, du), (512, g, dz)):
        turned = left[...].T
        for i, out in enumerate((mine_ref, other_ref)):
            core = c if i == 0 else 1 - c
            out[:, at:at + 512] = dot(turned, cols(right, 512 * core, 512)[...]).astype(BF)


def out_grad_kernel(ids, mixed, z0, z1, z2, z3, mine_ref, other_ref, mark):
    mark[...] = jnp.zeros_like(mark)
    x, c = ids[0], ids[1]
    turned = mixed[...].T
    for i, out in enumerate((mine_ref, other_ref)):
        core = c if i == 0 else 1 - c
        dmb = jnp.concatenate([cols(z, 256 * x + 128 * core, 128)[:BLOCK, :] for z in (z0, z1, z2, z3)], axis=0)
        out[...] = dot(turned, dmb).astype(BF)


def qkv_grad_kernel(a, gm, go, h, p0, p1, p2, p3, mine_ref, other_ref, sum_ref):
    turned = a[...].T
    mine_ref[...] = dot(turned, gm[...]).astype(BF)
    other_ref[...] = dot(turned, go[...]).astype(BF)
    gain = jnp.zeros((16, D), F32)
    shift = jnp.zeros((16, D), F32)
    for j, p in enumerate((p0, p1, p2, p3)):
        for r in range(0, BLOCK, 16):
            e = p[r:r + 16, :].astype(F32)
            gain = gain + e * norm_parts(h[BLOCK * j + r:BLOCK * j + r + 16, :])[0]
            shift = shift + e
    out = [jnp.sum(t, axis=0, keepdims=True) for t in (gain, shift)]
    sum_ref[...] = jnp.concatenate(out * 4, axis=0)


def add_kernel(*refs):
    out, mark, at = refs[-2], refs[-1], 0
    mark[...] = jnp.zeros_like(mark)
    for mine, came in zip(refs[:-2:2], refs[1:-2:2]):
        width = mine.shape[1]
        out[:, at:at + width] = (mine[...].astype(F32) + came[...].astype(F32)).astype(BF)
        at += width


def total_kernel(got, more, out):
    total = got[0].astype(F32)
    for d in range(1, 16):
        total = total + got[d].astype(F32)
    width = got.shape[2]
    out[:, :width] = total.astype(BF)
    out[:, width:] = more[...]


def write_gradient(name, layer, ref, all_ref, at):
    for core in range(2):
        if name == "up":
            for d in range(8):
                to = 256 * (8 * core + d)
                ref[layer, :, to:to + 256] = jnp.concatenate(
                    [all_ref[chip, core, :, at + 64 * d:at + 64 * (d + 1)] for chip in range(4)], axis=1).astype(F32)
        for chip in range(4):
            to = 256 * chip + 128 * core
            block = lambda i, width: all_ref[chip, core, :, at + i:at + i + width].astype(F32)
            if name == "down":
                ref[layer, 64 * chip:64 * (chip + 1), 512 * core:512 * (core + 1)] = block(0, 512)
            if name == "out":
                ref[layer, :, to:to + 128] = block(0, 128)
            if name == "qkv":
                for m in range(3):
                    ref[layer, :, D * m + to:D * m + to + 128] = block(128 * m, 128)


def arrange(ids, blocks, all_ref, at):
    x, c = ids[0], ids[1]
    for i in range(2):
        for j in range(4):
            all_ref[lax.rem(x + j, 4), c if i == 0 else 1 - c] = blocks[4 * i + j][at:, :]


def early_kernel(ids, counts, *refs):
    blocks, (tokens_ref, output_ref, up, down), all_ref = refs[:8], refs[8:12], refs[12]
    x, c = ids[0], ids[1]
    ranks = jnp.concatenate([half_ranks((1, ROWS), 1, x, core) for core in (c, 1 - c)], axis=1)
    put = jnp.where(slot_ranks((128, 1), 0, counts, 2 * x + c) == ranks, 1.0, 0.0).astype(BF)
    for i, ref in enumerate((tokens_ref, output_ref)):
        rows = jnp.concatenate([t[BLOCK * i:BLOCK * (i + 1), :] for t in blocks], axis=0)
        ref[0] = dot(put, rows).astype(BF)
    arrange(ids, blocks, all_ref, 2 * BLOCK)
    write_gradient("up", 0, up, all_ref, 0)
    write_gradient("down", 0, down, all_ref, 512)


def late_kernel(ids, *refs):
    blocks = refs[:8]
    (out, qkv, gain_ref, shift_ref, branch_ref, qv_ref, up_ref, up, down), all_ref = refs[-10:-1], refs[-1]
    arrange(ids, blocks, all_ref, 0)
    for name, layer, ref, at in (("out", 0, out, 0), ("qkv", 0, qkv, 128), ("up", 0, up, 640), ("down", 0, down, 1152),
                                 ("out", 1, out, 1664), ("qkv", 1, qkv, 1792)):
        write_gradient(name, layer, ref, all_ref, at)
    part = [sum(all_ref[chip, core, 0:16, 512:640].astype(F32) for core in range(2)) for chip in range(4)]
    total = part[0] + part[1] + part[2] + part[3]
    for l in range(2):
        for i, small in enumerate((gain_ref, shift_ref, branch_ref)):
            row = total[5 * l + i:5 * l + i + 1]
            small[l] = jnp.concatenate([row[:, :64], row[:, 64:]], axis=0)
        qv_ref[l:l + 1, :] = total[5 * l + 4:5 * l + 5]
        up_ref[l:l + 1, :] = jnp.concatenate([p[5 * l + 3:5 * l + 4, :64] for p in part], axis=1)


def finish(kernel, ids, blocks, outs, width, before=(), at=0, first=()):
    once = pl.Buffered(1)
    whole = lambda s: pl.BlockSpec(s, functools.partial(lambda n, _: (0,) * n, len(s)), pipeline_mode=once)
    out_specs = [whole(s) if n is None else pl.BlockSpec((n,) + s[1:], functools.partial(lambda at, _: (at, 0, 0), at),
                                                         pipeline_mode=once) for s, _, n, at in outs]
    n = 1 + len(first) + len(blocks)
    return pl.pallas_call(
        kernel,
        grid=(1,),
        in_specs=[pl.BlockSpec(memory_space=pltpu.SMEM)] * (1 + len(first)) + [whole(b.shape) for b in blocks]
        + [pl.BlockSpec(memory_space=pl.ANY)] * len(before),
        out_specs=out_specs,
        out_shape=[pltpu.HBM(s, t) for s, t, _, _ in outs],
        scratch_shapes=[pltpu.VMEM((4, 2, 64, width), BF)],
        input_output_aliases={n + i: at + i for i in range(len(before))},
        compiler_params=pltpu.CompilerParams(vmem_limit_bytes=LIMIT << 20),
        cost_estimate=pl.CostEstimate(flops=int(4e9), bytes_accessed=1, transcendentals=0),
    )(ids, *first, *blocks, *before)


def rest_kernel(ids, out_mine, out_came, qkv_mine, qkv_came, *refs):
    x, out = ids[0], refs[-1]
    for d in range(16):
        at = slice(64 * d, 64 * (d + 1))
        out[d, :, :128] = (out_mine[at, :].astype(F32) + out_came[at, :].astype(F32)).astype(BF)
        out[d, :, 128:512] = (qkv_mine[at, :].astype(F32) + qkv_came[at, :].astype(F32)).astype(BF)
        rows = []
        for l in range(2):
            one, zero, up, qv = refs[4 * l:4 * l + 4]
            pair = lambda u, v: jnp.concatenate([u, v], axis=1)
            rows += [pair(zero[0:1, at], one[0:1, at]), pair(zero[1:2, at], one[1:2, at]),
                     pair(one[2:3, at], one[3:4, at]), pair(up[0:1, at], jnp.zeros((1, 64), F32))]
            lanes = 256 * (d // 8) + 128 * (d % 2)
            rows.append(jnp.where(x == d % 8 // 2, qv[0:1, lanes:lanes + 128], 0.0))
        out[d, :, 512:] = jnp.concatenate(rows + [jnp.zeros((54, 128), F32)], axis=0).astype(BF)


def later(v, *others):
    return lax.optimization_barrier((v, *others))


def over_dp(v):
    return lax.all_to_all(v, "dp", split_axis=0, concat_axis=0, tiled=True)


def shards(tokens, counts, cotangent, w_qkv, w_out, w_up, w_down, norm_gain, norm_shift,
           bias_qv, bias_up, bias_branch):
    s, dp = lax.axis_index("seq"), lax.axis_index("dp")
    ids = jnp.stack([s // 2, s % 2, dp % 4, dp // 4]).astype(jnp.int32)

    def compact(blocks):
        own, give = run(pick_kernel, [((ROWS, D), BF)] * 2, ids, counts, *blocks)
        return own, core_swap(give)

    token_blocks = x_gather(tokens[0])
    first, rest0, rest1 = run(
        pack_kernel, [((64, 512), BF), ((64, 1920), BF), ((64, 1536), BF)], ids,
        away(w_qkv), away(w_out), away(w_up), away(w_down), away(norm_gain), away(norm_shift), away(bias_branch),
        away(bias_qv), away(bias_up),
        scratch=[pltpu.VMEM((64, 384), BF), pltpu.VMEM((2, 8, 64, 128), BF), pltpu.VMEM((3, 2, 2, 64), BF),
                 pltpu.VMEM((2, 128), BF), pltpu.VMEM((2, 256), BF), pltpu.SemaphoreType.DMA((31,))])
    rest0 = lax.all_gather(rest0, "dp", axis=0, tiled=True)
    rest1 = lax.all_gather(rest1, "dp", axis=0, tiled=True)
    source = list(compact(token_blocks))
    first, = run(order_kernel, [((4, 64, 512), BF)], ids, *dp_gather(first, 1), after=[source[0]])
    first, vec, qkv_bias, up_bias = run(
        unpack_kernel, [((D, 512), BF), ((16, D), F32), ((8, 384), F32), ((8, 512), F32)], ids, *dp_gather(first, 4),
        scratch=[pltpu.VMEM((16, 64, 512), BF)])
    first_far = core_swap(first)

    own, far = compact(x_gather(cotangent[0]))
    dz, dh, mark = run(join_kernel, in_hbm([((ROWS, D), BF), ((BLOCK, D), F32)]) + [MARK], own, far)
    dh = saved(dh)

    full = lambda *dtypes: [((ROWS, D), t) for t in dtypes]
    sent = [((BLOCK, D), BF)] * 4
    kept = []
    for l in range(2):
        outs = full(F32, BF) + [((ROWS, 256), BF), ((ROWS, 512), BF)]
        if l == 0:
            hidden, a, q, kv = run(functools.partial(qkv_kernel, l), outs, ids, vec, qkv_bias, *source, first, first_far,
                                   after=[mark], us=2)
        else:
            hidden, a, q, kv = run(functools.partial(qkv_kernel, l), outs, ids, vec, qkv_bias, *source, *rests[0],
                                   scratch=held(2, D, 384), after=[mark], us=3)
        kv_far = core_swap(kv)
        outs = [((ROWS, 256), BF), ((ROWS, 128), F32)]
        if l == 0:
            mixed, lse, q, kv, hidden, a, first, first_far = run(
                attend_kernel, outs + [(s, t, "away") for s, t in (
                    ((ROWS, 256), BF), ((2 * ROWS, 512), BF), ((ROWS, D), F32), ((ROWS, D), BF), ((D, 512), BF), ((D, 512), BF))],
                ids, q, kv, kv_far, hidden, a, first, first_far, scratch=[pltpu.SemaphoreType.DMA((7,))], us=4)
            rest0, lse = later(rest0, lse)
            rests = [[away(rest0), ("any", core_swap(rest0))]]
            hidden, a, q, kvs, lse = saved(hidden), saved(a), saved(q), [saved(kv)], saved(lse)
        else:
            mixed, lse = run(attend_kernel, outs, ids, q, kv, kv_far, us=3)
            kvs = [kv, kv_far]
            rest1, lse = later(rest1, lse)
            rests.append([away(rest1), ("any", core_swap(rest1))])
        mixes = x_gather(mixed)
        parts = [(rests[l][0][1], (3, D, 512), lanes_of(512, 0, 1024))]
        if l == 0:
            near, = load(ids, parts)
        else:
            near, a, hidden = load(ids, parts + [(a, (ROWS, D), None), (hidden, (ROWS, D), None)])
        room = held(3, D, 512)
        all_mixed, normed, middle, g, slope, *parts = run(
            functools.partial(mlp_kernel, l), full(BF, BF, F32, BF, BF) + sent + ([((3, D, 512), BF)] if l else []),
            ids, vec, up_bias, *mixes, hidden, near, rests[l][1],
            scratch=[pltpu.VMEM((ROWS, 512), F32)] + (room[1:] if l else room), us=6)
        if l:
            *parts, near_far = parts
            near = [near, near_far]
        if l == 0:
            mlp, mark = run(sum_kernel, [((BLOCK, D), BF), LOOSE], *x_scatter(parts))
            source = [middle, *x_gather(mlp)]
            *stored, mark = store([(all_mixed, ROWS), (normed, ROWS), (middle, BLOCK), (g, ROWS), (slope, ROWS)], [mark])
            all_mixed, normed, middle, g, slope = map(saved, stored)
        kept.append([hidden, a, q, kvs, lse, all_mixed, normed, middle, g, slope])

    dz = [(saved(dz), (BLOCK, D), (j, 0)) for j in range(4)]
    swapped = lambda v: v + [core_swap(b) for b in v]
    last_parts, last_rows = parts, (saved(middle), (BLOCK, D), (0, 0))
    rests[0][1] = away(rests[0][1][1])
    keep = lambda v: v if isinstance(v, tuple) else saved(v)
    tiny = []
    for l in (1, 0):
        hidden, a, q, kvs, lse, all_mixed, normed, middle, g, slope = kept[l]
        qkv = rests[0] if l else [away(first), away(first_far)]
        if l == 0:
            weights0 = lanes_of(0, 1024)
            *near, slope, normed, g = load(ids, [(rests[0][0][1], (2, D, 512), weights0), (rests[0][1][1], (2, D, 512), weights0),
                                        (slope[1], (ROWS, D), None), (normed[1], (ROWS, D), None),
                                        (g[1], (ROWS, D), None)], after=[mark_add, dh])
        top = lambda v: (v, (BLOCK, D), (0, 0))
        dz_all, du, up_sum, *parts = run(
            mlp_back_kernel, full(BF, BF) + [((8, D), F32)] + sent, ids, *dz, slope, *near,
            after=[mark_add] if l == 0 else (), us=4)
        errs = x_scatter(parts)
        mlp_mine, mlp_other, sums_grad = run(mlp_grad_kernel, [((D, D), BF)] * 2 + [LOOSE], ids, normed, du, g, dz_all, us=4)
        dm, dmb, sums1 = run(functools.partial(norm_back_kernel, 2 * l + 1),
                             [((BLOCK, D), F32), ((BLOCK, D), BF), ((8, D), F32)], vec, top(middle), dh,
                             errs[0] if l else saved(errs[0]), *errs[1:],
                             after=[sums_grad], us=1 if l else 8)
        mlp_came = core_swap(mlp_other)
        dmbs = x_gather(dmb)
        if l == 0:
            rows = lambda ids: [(pl.ds(pl.multiple_of(256 * ids[0], 256), 256), pl.ds(512, 512))]
            q, lse, kvs, w_near, w_far, *near = load(ids, [
                (q[1], (ROWS, 256), None), (lse[1], (ROWS, 128), None), (kvs[0][1], (2 * ROWS, 512), None),
                (first, (1, D, 384), lanes_of(0, width=384)), (first_far, (1, D, 384), lanes_of(0, width=384)),
                (rests[0][0][1], (1, 256, 512), rows), (rests[0][1][1], (1, 256, 512), rows)], after=[dm])
            kvs, qkv = [kvs], [w_near, w_far]
        before = []
        if l == 0:
            shares, mark = run(add_kernel, [((D, D), BF, "saved"), LOOSE], mlp_mine, mlp_came, us=3)
            got_mlp = over_dp(shares.reshape(16, 64, D))
            before = [mark]
        dmb_all, dq, dkv, give = run(
            attend_back_kernel, full(BF) + [((ROWS, 256), BF), ((ROWS, 512), F32), ((ROWS, 512), BF)],
            ids, *dmbs, *near, q, lse, *kvs, after=before, us=5 if l else 0.1)
        give = core_swap(give)
        out_mine, out_other, mark_out = run(out_grad_kernel, [((D, 128), BF)] * 2 + [LOOSE], ids, all_mixed, *dmbs, us=2 if l else 0.1)
        out_came = core_swap(out_other)
        high = BLOCK * (2 - l)
        gm, go, qv_sum, *parts = run(
            functools.partial(qkv_back_kernel, 1536 if l else None),
            [((ROWS, 384), BF)] * 2 + [((8, 512), F32)] + [((high, D), BF)] * 4,
            ids, dq, dkv, give, *qkv, *([] if l else map(keep, last_parts)), scratch=held(2, D, 384) if l else (), after=[mark_out], us=3 if l else 0.1)
        errs = x_scatter(parts)
        qkv_mine, qkv_other, sums0 = run(qkv_grad_kernel, [((D, 384), BF)] * 2 + [((8, D), F32)],
                                         a, gm, go, hidden, *parts, us=4 if l else 0.1)
        tiny = [sums1, sums0, up_sum, qv_sum] + tiny
        qkv_came = core_swap(qkv_other)
        qkv_pair = [qkv_mine, qkv_came]
        if l == 1:
            shares, mark_add = run(add_kernel, [((D, 1536), BF, "saved"), LOOSE], mlp_mine, mlp_came,
                                   out_mine, out_came, *qkv_pair, us=4)
            got1 = lax.psum_scatter(shares, "dp", scatter_dimension=0, tiled=True)
        else:
            rest, = run(rest_kernel, in_hbm([((16, 64, 640), BF)]), ids, out_mine, out_came, *qkv_pair, *tiny, us=0.1)
            got_rest = over_dp(rest)
        if l == 1:
            dh, dz = run(functools.partial(norm_back_kernel, 2), [((BLOCK, D), F32), ((BLOCK, D), BF)],
                         vec, top(hidden), dm, *errs, after=[mark_add])
            dz = x_gather(dz)
        else:
            dz, = run(functools.partial(norm_back_kernel, 0), [((2 * BLOCK + 64, D), BF)],
                      vec, top(hidden), saved(dm), saved(errs[0]), *errs[1:], last_rows, got_mlp, after=[rest], us=2)
    grad_tokens, output, g_up, g_down = finish(
        early_kernel, ids, swapped(x_gather(dz)),
        [((1, 128, D), BF, None, 0)] * 2 + [((2, 64, 4096), F32, 1, 0), ((2, 256, 1024), F32, 1, 0)], D, first=[counts])
    total_rest, = run(total_kernel, [((64, 2176), BF)], got_rest, saved(got1))
    g_out, g_qkv, g_gain, g_shift, g_branch, g_qv, g_upb, g_up, g_down = finish(
        late_kernel, ids, swapped(x_gather(total_rest)),
        [((2, 64, 1024), F32, 2, 0), ((2, 64, 3072), F32, 2, 0)] + [((2, 2, 64), F32, None, 0)] * 3
        + [((2, 128), F32, None, 0), ((2, 256), F32, None, 0), ((2, 64, 4096), F32, 1, 1), ((2, 256, 1024), F32, 1, 1)],
        2176, before=(g_up, g_down), at=7)
    return (output, grad_tokens, g_qkv, g_out, g_up, g_down, g_gain, g_shift, g_qv, g_upb, g_branch)


def solution(mesh):
    rows = P("dp", "seq", None)
    mid = P(None, "dp", None)
    end = P(None, None, "dp")
    two = P(None, "dp")
    return jax.shard_map(
        shards,
        mesh=mesh,
        in_specs=(rows, P("dp", None), rows, mid, mid, mid, mid, end, end, two, two, end),
        out_specs=(rows, rows, mid, mid, mid, mid, end, end, two, two, end),
        check_vma=False,
    )
```

```python
import functools

import jax
import jax.numpy as jnp
from jax import lax
from jax.experimental import pallas as pl
from jax.experimental.pallas import tpu as pltpu
from jax.sharding import PartitionSpec as P

EPSILON = 1e-06
BF = jnp.bfloat16
F32 = jnp.float32
BLOCK = 80
SHARE = 73
TOTAL = 577
ROWS = 4 * BLOCK
D = 1024
LOOSE = ((8, 128), jnp.float32)
MARK = ((8, 128), jnp.float32, "saved")
LIMIT = 24

NEXT = [(i, (i + 2) % 8) for i in range(8)]
PREV = [(i, (i - 2) % 8) for i in range(8)]
FAR = [(i, (i + 4) % 8) for i in range(8)]
CORE = [(i, i ^ 1) for i in range(8)]


def x_gather(block):
    two = lax.ppermute(block, "seq", PREV)
    four = lax.ppermute(block, "seq", NEXT)
    return [block, two, lax.ppermute(block, "seq", FAR), four]


def x_scatter(blocks):
    three = lax.ppermute(blocks[2], "seq", FAR)
    return [blocks[0], lax.ppermute(blocks[1], "seq", NEXT), three, lax.ppermute(blocks[3], "seq", PREV)]


def core_swap(v):
    return lax.ppermute(v, "seq", CORE)


def dp_pairs(step, k):
    if step == 1:
        return [(i, i // 4 * 4 + (i + k) % 4) for i in range(16)]
    return [(i, (i + 4 * k) % 16) for i in range(16)]


def dp_scatter(blocks, step):
    return [blocks[0]] + [lax.ppermute(blocks[k], "dp", dp_pairs(step, k)) for k in (1, 2, 3)]


def dp_gather(block, step):
    return [block] + [lax.ppermute(block, "dp", dp_pairs(step, -k)) for k in (1, 2, 3)]


def dot(a, b):
    return jnp.dot(a, b, preferred_element_type=F32)


def dot_nt(a, b):
    return lax.dot_general(a, b, (((1,), (1,)), ((), ())), preferred_element_type=F32)


def dot_tn(a, b):
    return lax.dot_general(a, b, (((0,), (0,)), ((), ())), preferred_element_type=F32)


def cols(ref, at, width):
    return ref.at[:, pl.ds(pl.multiple_of(at, 128), width)]


def norm_parts(rows):
    mean = jnp.mean(rows, axis=-1, keepdims=True)
    centered = rows - mean
    rstd = lax.rsqrt(jnp.mean(centered * centered, axis=-1, keepdims=True) + EPSILON)
    return centered * rstd, rstd


def away(v):
    return ("away", v)


def saved(v):
    return ("saved", v)


def in_hbm(outs):
    return [o + ("saved",) for o in outs]


def run(kernel, outs, *ins, scratch=(), after=(), us=1.0):
    once = pl.Buffered(1)
    small = lambda v: v.size < 200000
    hbm = lambda v: pltpu.with_memory_space_constraint(v, pltpu.HBM)
    whole = lambda s: pl.BlockSpec(s, functools.partial(lambda n, _: (0,) * n, len(s)), pipeline_mode=once)
    specs, arrays = [], []
    for v in ins:
        if isinstance(v, tuple) and len(v) == 2:
            kind, v = v
            specs.append(whole(v.shape) if kind == "saved" else pl.BlockSpec(memory_space=pl.ANY if kind == "any" else pltpu.HBM))
            v = v if kind == "any" else hbm(v)
        elif isinstance(v, tuple):
            v, block, index = v
            specs.append(pl.BlockSpec(block, functools.partial(lambda at, _: at, index), pipeline_mode=once))
            if isinstance(v, tuple):
                v = hbm(v[1])
        elif v.dtype == jnp.int32:
            specs.append(pl.BlockSpec(memory_space=pltpu.SMEM))
        else:
            specs.append(whole(v.shape))
        arrays.append(v)
    specs += [pl.BlockSpec(memory_space=pl.ANY if small(v) else pltpu.HBM) for v in after]
    n = len(arrays)
    body = lambda *refs: kernel(*refs[:n], *refs[n + len(after):])
    kinds = [o[2] if len(o) > 2 else "" for o in outs]
    return pl.pallas_call(
        body,
        grid=(1,),
        in_specs=specs,
        out_specs=[pl.BlockSpec(memory_space=pltpu.HBM) if k == "away" else whole(o[0]) for k, o in zip(kinds, outs)],
        out_shape=[pltpu.HBM(o[0], o[1]) if k else jax.ShapeDtypeStruct(o[0], o[1]) for k, o in zip(kinds, outs)],
        scratch_shapes=list(scratch),
        compiler_params=pltpu.CompilerParams(vmem_limit_bytes=LIMIT << 20),
        cost_estimate=pl.CostEstimate(flops=int(us * 1.0 * 1.15e9), bytes_accessed=1, transcendentals=0),
    )(*arrays, *[v if small(v) else hbm(v) for v in after])


def fetch(parts, buf, sem):
    copies = [pltpu.make_async_copy(v, buf.at[i], sem.at[i]) for i, v in enumerate(parts)]
    for copy in copies:
        copy.start()
    return copies


def send(pairs, sem):
    copies = [pltpu.make_async_copy(v, out, sem.at[i]) for i, (v, out) in enumerate(pairs)]
    for copy in copies:
        copy.start()
    return copies


def held(count, rows, width):
    return [pltpu.VMEM((count, rows, width), BF), pltpu.SemaphoreType.DMA((count,))]


def load_kernel(slices, ids, *refs):
    n = len(slices)
    sources, outs, sem = refs[:n], refs[n:-1], refs[-1]
    copies = []
    for part, source, out in zip(slices, sources, outs):
        for i, at in enumerate(part(ids) if part else [None]):
            copies.append(pltpu.make_async_copy(source if at is None else source.at[at], out if at is None else out.at[i],
                                                sem.at[len(copies)]))
            copies[-1].start()
    for copy in copies:
        copy.wait()


def load(ids, parts, after=()):
    count = sum(s[0] if p else 1 for _, s, p in parts)
    return run(functools.partial(load_kernel, [p for _, _, p in parts]), [(s, BF if v.dtype == BF else F32) for v, s, _ in parts],
               ids, *[away(v) for v, _, _ in parts], scratch=[pltpu.SemaphoreType.DMA((count,))], after=after, us=2)


def store_kernel(*refs):
    n = (len(refs) - 2) // 2
    mark, sem = refs[-2], refs[-1]
    mark[...] = jnp.zeros_like(mark)
    pairs = [(v.at[pl.ds(0, out.shape[0]), :], out) for v, out in zip(refs[:n], refs[n:])]
    for copy in send(pairs, sem):
        copy.wait()


def store(parts, after):
    outs = [((rows, v.shape[1]), v.dtype, "away") for v, rows in parts]
    return run(store_kernel, outs + [LOOSE], *[v for v, _ in parts], scratch=[pltpu.SemaphoreType.DMA((len(parts),))],
               after=after, us=2)


def lanes_of(*at, width=512):
    return lambda ids: [(slice(None), pl.ds(i, width)) for i in at]


def half_ranks(shape, axis, x, core):
    at = lax.broadcasted_iota(jnp.int32, shape, axis)
    block = sum((at >= BLOCK * i).astype(jnp.int32) for i in (1, 2, 3))
    within = at - BLOCK * block
    chip = x + block
    chip = jnp.where(chip >= 4, chip - 4, chip)
    rank = (4 * core + chip) * SHARE + within
    return jnp.where((within < SHARE) & (rank < TOTAL), rank, -2)


def slot_ranks(shape, axis, counts, s):
    at = lax.broadcasted_iota(jnp.int32, shape, axis)
    start = sum(jnp.where(i < s, counts[0, i], 0) for i in range(8))
    return jnp.where(at < counts[0, s], start + at, -1)


def kept_keys(x, c):
    at = lax.broadcasted_iota(jnp.int32, (1, 2 * ROWS), 1)
    second = (at >= ROWS).astype(jnp.int32)
    at = at - ROWS * second
    block = sum((at >= BLOCK * i).astype(jnp.int32) for i in (1, 2, 3))
    chip = x + block
    chip = jnp.where(chip >= 4, chip - 4, chip)
    core = jnp.where(second > 0, 1 - c, c)
    within = at - BLOCK * block
    return (within < SHARE) & ((4 * core + chip) * SHARE + within < TOTAL)


def pick_kernel(ids, counts, t0, t1, t2, t3, own_ref, far_ref):
    x, c = ids[0], ids[1]
    rows = jnp.concatenate([t[...] for t in (t0, t1, t2, t3)], axis=0)
    slots = [slot_ranks((1, 128), 1, counts, 2 * lax.rem(x + j, 4) + c) for j in range(4)]
    for core, out in ((c, own_ref), (1 - c, far_ref)):
        rank = half_ranks((ROWS, 1), 0, x, core)
        pick = jnp.concatenate([jnp.where(rank == s, 1.0, 0.0) for s in slots], axis=1)
        out[...] = dot(pick.astype(BF), rows).astype(BF)


def join_kernel(own, far, dz_ref, dh_ref, mark):
    mark[...] = jnp.zeros_like(mark)
    dz = own[...] + far[...]
    dz_ref[...] = dz
    dh_ref[...] = dz[:BLOCK, :].astype(F32)


def pack_kernel(ids, w_qkv, w_out, w_up, w_down, gain, shift, branch, qv, up,
                first_ref, rest0_ref, rest1_ref, qkv_buf, up_buf, norm_buf, qv_buf, wide_buf, sem):
    x, c = ids[0], ids[1]
    lanes = lambda at, width: pl.ds(pl.multiple_of(at, 128), width)
    copies = []

    def copy(source, target):
        copies.append(pltpu.make_async_copy(source, target, sem.at[len(copies)]))
        copies[-1].start()

    rests = (rest0_ref, rest1_ref)
    for l in range(2):
        for m in range(3):
            target = qkv_buf.at[:, pl.ds(128 * m, 128)] if l == 0 else rest0_ref.at[:, pl.ds(1536 + 128 * m, 128)]
            copy(w_qkv.at[l, :, lanes(D * m + 256 * x + 128 * c, 128)], target)
        for d in range(8):
            copy(w_up.at[l, :, lanes(2048 * c + 256 * d + 128 * (x // 2), 128)], up_buf.at[l, d])
        copy(w_out.at[l, :, lanes(512 * c, 512)], rests[l].at[:, pl.ds(512, 512)])
        copy(w_down.at[l, pl.ds(pl.multiple_of(64 * x, 64), 64), lanes(512 * c, 512)], rests[l].at[:, pl.ds(1024, 512)])
    for i, v in enumerate((gain, shift, branch)):
        copy(v, norm_buf.at[i])
    copy(qv, qv_buf)
    copy(up, wide_buf)
    for each in copies:
        each.wait()
    pairs = lambda i: jnp.concatenate([norm_buf[i, 0], norm_buf[i, 1]], axis=0).astype(F32)
    wide = wide_buf[...].astype(F32)
    small = jnp.concatenate([
        jnp.concatenate([pairs(0), pairs(1)], axis=1),
        jnp.concatenate([pairs(2), jnp.zeros((4, 64), F32)], axis=1),
        qv_buf[...].astype(F32),
        wide[0:1, :128], wide[0:1, 128:], wide[1:2, :128], wide[1:2, 128:],
        jnp.zeros((50, 128), F32)], axis=0).astype(BF)
    block = jnp.concatenate([qkv_buf[...], small], axis=1)
    first_ref[...] = block
    odd = lax.rem(x, 2) == 1
    for l in range(2):
        got = []
        for d in range(8):
            piece = up_buf[l, d].astype(F32)
            got.append(jnp.where(odd, piece[:, 64:], piece[:, :64]))
        rests[l][:, :512] = jnp.concatenate(got, axis=1).astype(BF)


def order_kernel(ids, a, b, c, d, out):
    for i, v in enumerate((a, b, c, d)):
        out[lax.rem(ids[2] + i, 4)] = v[...]


def unpack_kernel(ids, a, b, c, d, first_ref, vec_ref, qkv_ref, up_ref, first):
    for i, v in enumerate((a, b, c, d)):
        for y in range(4):
            first[4 * lax.rem(ids[3] + i, 4) + y] = v[y]
    for i in range(16):
        first_ref[64 * i:64 * (i + 1), :] = first[i]
    x, c = ids[0], ids[1]
    rows = [first[d, 0:16, 384:].astype(F32) for d in range(16)]
    line = lambda at, lanes: jnp.concatenate([r[at:at + 4, lanes:lanes + 64] for r in rows], axis=1)
    vec_ref[...] = jnp.concatenate([line(0, 0), line(0, 64), line(4, 0), jnp.zeros((4, D), F32)], axis=0)
    qkv, up = [], []
    for l in range(2):
        for core in (c, 1 - c):
            q = first[2 * x + core, 0:16, 384:].astype(F32)[8 + l:9 + l]
            v = first[8 + 2 * x + core, 0:16, 384:].astype(F32)[8 + l:9 + l]
            qkv.append(jnp.concatenate([q, jnp.zeros((1, 128), F32), v], axis=1))
            got = []
            for d in range(8):
                r = first[8 * core + d, 0:16, 384:].astype(F32)
                r = jnp.where(x >= 2, r[11 + 2 * l:12 + 2 * l], r[10 + 2 * l:11 + 2 * l])
                got.append(jnp.where(lax.rem(x, 2) == 1, r[:, 64:], r[:, :64]))
            up.append(jnp.concatenate(got, axis=1))
    qkv_ref[...] = jnp.concatenate(qkv + [jnp.zeros((4, 384), F32)], axis=0)
    up_ref[...] = jnp.concatenate(up + [jnp.zeros((4, 512), F32)], axis=0)


def qkv_kernel(l, ids, vec, bias, *refs):
    gain, shift = vec[2 * l:2 * l + 1, :], vec[4 + 2 * l:5 + 2 * l, :]
    first = l == 0
    if first:
        own, far, wm, wo, h_ref, a_ref, q_ref, kv_ref = refs
        weight = lambda i: (wm, wo)[i][:, :384]
    else:
        m, d0, d1, d2, d3, wm, wo, h_ref, a_ref, q_ref, kv_ref, buf, sem = refs
        branch = vec[9:10, :]
        copies = fetch([w.at[:, pl.ds(1536, 384)] for w in (wm, wo)], buf, sem)

        def weight(i):
            copies[i].wait()
            return buf[i]

    c = ids[1]
    for r in range(0, ROWS, 16):
        rows = slice(r, r + 16)
        if first:
            h = own[rows, :].astype(F32) + far[rows, :].astype(F32)
        else:
            b, o = divmod(r, BLOCK)
            h = m[rows, :] + (d0, d1, d2, d3)[b][o:o + 16, :].astype(F32) + branch
        h_ref[rows, :] = h
        a_ref[rows, :] = (norm_parts(h)[0] * gain + shift).astype(BF)
    a = a_ref[...]
    for i in range(2):
        core = c if i == 0 else 1 - c
        packed = (dot(a, weight(i)) + bias[2 * l + i:2 * l + i + 1, :]).astype(BF)
        cols(q_ref, 128 * core, 128)[...] = packed[:, :128]
        cols(kv_ref, 128 * core, 128)[...] = packed[:, 128:256]
        cols(kv_ref, 256 + 128 * core, 128)[...] = packed[:, 256:]


def head_mask(rows, sub):
    lane = lax.broadcasted_iota(jnp.int32, (rows, 128), 1)
    return (lane < 64) if sub == 0 else (lane >= 64)


def attend_kernel(ids, q_ref, kv_ref, far_ref, *refs):
    keeps = []
    if len(refs) == 2:
        mixed_ref, lse_ref = refs
    else:
        n = (len(refs) - 5) // 2
        mixed_ref, lse_ref = refs[n:n + 2]
        outs, sem = refs[n + 2:-1], refs[-1]
        keeps = send([(q_ref, outs[0]), (kv_ref, outs[1].at[pl.ds(0, ROWS), :]),
                      (far_ref, outs[1].at[pl.ds(ROWS, ROWS), :])], sem)
        keeps += send(list(zip(refs[:n], outs[2:])), sem.at[pl.ds(3, n)])
    low = head_mask(ROWS, 0)
    keep = kept_keys(ids[0], ids[1])
    lane = lax.broadcasted_iota(jnp.int32, (ROWS, 128), 1)
    lses = jnp.zeros((ROWS, 128), F32)
    for pair in range(2):
        at = 128 * pair
        k = jnp.concatenate([kv_ref[:, at:at + 128], far_ref[:, at:at + 128]], axis=0)
        v = jnp.concatenate([kv_ref[:, 256 + at:384 + at], far_ref[:, 256 + at:384 + at]], axis=0)
        q = q_ref[:, at:at + 128]
        got = []
        for sub in range(2):
            qm = jnp.where(low if sub == 0 else ~low, q, jnp.zeros_like(q))
            s = dot_nt(qm, k) * 0.125
            s = jnp.where(keep, s, -1e9)
            top = jnp.max(s, axis=-1, keepdims=True)
            e = jnp.exp(s - top)
            total = jnp.sum(e, axis=-1, keepdims=True)
            got.append(dot((e * (1.0 / total)).astype(BF), v))
            lses = jnp.where(lane == 2 * pair + sub, top + jnp.log(total), lses)
        mixed_ref[:, at:at + 128] = jnp.where(low, got[0], got[1]).astype(BF)
    lse_ref[...] = lses
    for keep in keeps:
        keep.wait()


def mlp_kernel(l, ids, vec, up_bias, mx0, mx1, mx2, mx3, h, near, wo, *refs):
    x, c = ids[0], ids[1]
    all_ref, c_ref, m_ref, g_ref, slope_ref, p0, p1, p2, p3, *room, sem = refs
    u_ref, buf = room if l == 0 else room[::-1]
    copies = fetch([wo.at[:, pl.ds(at, 512)] for at in (512, 0, 1024)], buf, sem)

    def weight(i):
        if i % 2 == 0:
            return near[i // 2]
        copies[i // 2].wait()
        return buf[i // 2]

    gain, shift, branch = (vec[i + 2 * l:i + 1 + 2 * l, :] for i in (1, 5, 8))
    for j, mx in enumerate((mx0, mx1, mx2, mx3)):
        at = 256 * lax.rem(x + j, 4)
        for b in range(4):
            to = BLOCK * ((j + b) % 4)
            all_ref[to:to + BLOCK, pl.ds(pl.multiple_of(at, 128), 256)] = mx[BLOCK * b:BLOCK * (b + 1), :]
    mixed = all_ref[...]
    for i in range(2):
        core = c if i == 0 else 1 - c
        cols(m_ref, 512 * core, 512)[...] = dot(mixed, weight(i))
    for r in range(0, ROWS, 16):
        rows = slice(r, r + 16)
        m = h[rows, :] + m_ref[rows, :] + branch
        m_ref[rows, :] = m
        c_ref[rows, :] = (norm_parts(m)[0] * gain + shift).astype(BF)
    normed = c_ref[...]
    for i in range(2):
        core = c if i == 0 else 1 - c
        slope_part = cols(slope_ref, 512 * core, 512)
        g_part = cols(g_ref, 512 * core, 512)
        u_ref[...] = dot(normed, weight(2 + i)) + up_bias[2 * l + i:2 * l + i + 1, :]
        for r in range(0, ROWS, 32):
            rows = pl.ds(r, 32)
            u = u_ref[rows, :]
            half = 0.5 + 0.5 * lax.erf(u * 0.7071067811865476)
            g_part[rows, :] = (u * half).astype(BF)
            slope_part[rows, :] = (half + u * (0.3989422804014327 * jnp.exp(-0.5 * u * u))).astype(BF)
    g = g_ref[...]
    for i in range(2):
        core = c if i == 0 else 1 - c
        part = dot(g, weight(4 + i)).astype(BF)
        for j, out in enumerate((p0, p1, p2, p3)):
            cols(out, 512 * core, 512)[...] = part[BLOCK * j:BLOCK * (j + 1), :]


def sum_kernel(a, b, c, d, out, mark):
    mark[...] = jnp.zeros_like(mark)
    out[...] = (a[...].astype(F32) + b[...].astype(F32) + c[...].astype(F32) + d[...].astype(F32)).astype(BF)


def mlp_back_kernel(ids, z0, z1, z2, z3, slope, *refs):
    near, near_far, dz_ref, du_ref, sum_ref, p0, p1, p2, p3 = refs
    weight = lambda i: (near, near_far)[i % 2][near.shape[0] - 1 - i // 2]
    c = ids[1]
    for j, z in enumerate((z0, z1, z2, z3)):
        dz_ref[BLOCK * j:BLOCK * (j + 1), :] = z[...]
    dact = (dot_nt(cols(dz_ref, 512 * c, 512)[...], weight(0))
            + dot_nt(cols(dz_ref, 512 * (1 - c), 512)[...], weight(1)))
    du_ref[...] = (dact * slope[...].astype(F32)).astype(BF)
    part = (dot_nt(cols(du_ref, 512 * c, 512)[...], weight(2))
            + dot_nt(cols(du_ref, 512 * (1 - c), 512)[...], weight(3)))
    part = part.astype(BF)
    for j, out in enumerate((p0, p1, p2, p3)):
        out[...] = part[BLOCK * j:BLOCK * (j + 1), :]
    sums = jnp.sum(du_ref[...].astype(F32), axis=0, keepdims=True)
    sum_ref[...] = jnp.broadcast_to(sums, (8, D))


def norm_back_kernel(row, vec, base, above, e0, e1, e2, e3, *refs):
    final = len(refs) == 3 and refs[2].shape[0] > BLOCK
    if final:
        last, got, db_ref = refs
    else:
        d_ref, db_ref, sum_ref = refs if len(refs) == 3 else (*refs, None)
    gain = vec[row:row + 1, :]
    totals = [jnp.zeros((16, D), F32) for _ in range(4)]
    for r in range(0, BLOCK, 16):
        rows = slice(r, r + 16)
        e = e0[rows, :].astype(F32) + e1[rows, :].astype(F32) + e2[rows, :].astype(F32) + e3[rows, :].astype(F32)
        n, rstd = norm_parts(base[rows, :])
        eg = e * gain
        back = rstd * (eg - jnp.mean(eg, axis=-1, keepdims=True) - n * jnp.mean(eg * n, axis=-1, keepdims=True))
        up = above[rows, :]
        d = up + back
        db = d.astype(BF)
        db_ref[rows, :] = db
        if final:
            late = slice(BLOCK + r, BLOCK + r + 16)
            sums = sum(v[late, :].astype(F32) for v in (e0, e1, e2, e3))
            db_ref[late, :] = (last[rows, :] + sums + vec[11:12, :]).astype(BF)
            continue
        d_ref[rows, :] = d
        if sum_ref is not None:
            for i, t in enumerate((e * n, e, db.astype(F32), up.astype(BF).astype(F32))):
                totals[i] = totals[i] + t
    if final:
        total = got[0].astype(F32)
        for d in range(1, 16):
            total = total + got[d].astype(F32)
        db_ref[2 * BLOCK:, :] = total.astype(BF)
    elif sum_ref is not None:
        out = [jnp.sum(t, axis=0, keepdims=True) for t in totals]
        sum_ref[...] = jnp.concatenate(out + out, axis=0)


def attend_back_kernel(ids, z0, z1, z2, z3, *refs):
    near, near_far, q_ref, lse_ref, *kvs, dmb_ref, dq_ref, dkv_ref, give_ref = refs
    x, c = ids[0], ids[1]
    part = pl.ds(pl.multiple_of(256 * x, 256), 256)
    for j, z in enumerate((z0, z1, z2, z3)):
        dmb_ref[BLOCK * j:BLOCK * (j + 1), :] = z[:BLOCK, :]
    weight = lambda i: (near, near_far)[i][0] if near.shape[1] == 256 else (near, near_far)[i][0, part, :]
    dmixed = (dot_nt(cols(dmb_ref, 512 * c, 512)[...], weight(0))
              + dot_nt(cols(dmb_ref, 512 * (1 - c), 512)[...], weight(1))).astype(BF)
    low = head_mask(ROWS, 0)
    keep = kept_keys(ids[0], ids[1])
    lane = lax.broadcasted_iota(jnp.int32, (ROWS, 128), 1)
    for pair in range(2):
        at = 128 * pair
        k, v = (jnp.concatenate([ref[:, i + at:i + at + 128] for ref in kvs], axis=0) for i in (0, 256))
        q = q_ref[:, at:at + 128]
        dmp = dmixed[:, at:at + 128]
        dqs = []
        dk = jnp.zeros((2 * ROWS, 128), F32)
        dv = jnp.zeros((2 * ROWS, 128), F32)
        for sub in range(2):
            mask = low if sub == 0 else ~low
            qm = jnp.where(mask, q, jnp.zeros_like(q))
            dmm = jnp.where(mask, dmp, jnp.zeros_like(dmp))
            lse = jnp.sum(jnp.where(lane == 2 * pair + sub, lse_ref[...], 0.0), axis=-1, keepdims=True)
            s = dot_nt(qm, k) * 0.125
            p = jnp.exp(jnp.where(keep, s, -1e9) - lse)
            dp = dot_nt(dmm, v)
            inner = jnp.sum(dp * p, axis=-1, keepdims=True)
            ds = (p * (dp - inner)).astype(BF)
            dqs.append(dot(ds, k))
            dk = dk + dot_tn(ds, qm)
            dv = dv + dot_tn(p.astype(BF), dmm)
        dq_ref[:, at:at + 128] = (jnp.where(low, dqs[0], dqs[1]) * 0.125).astype(BF)
        dk = dk * 0.125
        dkv_ref[:, at:at + 128] = dk[:ROWS]
        dkv_ref[:, 256 + at:384 + at] = dv[:ROWS]
        give_ref[:, at:at + 128] = dk[ROWS:].astype(BF)
        give_ref[:, 256 + at:384 + at] = dv[ROWS:].astype(BF)


def qkv_back_kernel(at, ids, dq, dkv, far, wm, wo, *refs):
    if at is None:
        lasts, (gm_ref, go_ref, sum_ref, p0, p1, p2, p3) = refs[:-7], refs[-7:]
        weight = lambda i: (wm, wo)[i][0]
    else:
        lasts, (gm_ref, go_ref, sum_ref, p0, p1, p2, p3, buf, sem) = refs[:-9], refs[-9:]
        copies = fetch([w.at[:, pl.ds(at, 384)] for w in (wm, wo)], buf, sem)

        def weight(i):
            copies[i].wait()
            return buf[i]

    c = ids[1]
    part = None
    sum_ref[...] = jnp.zeros((8, 512), F32)
    for i, g in enumerate((gm_ref, go_ref)):
        core = c if i == 0 else 1 - c
        g[:, :128] = cols(dq, 128 * core, 128)[...]
        g[:, 128:256] = (cols(dkv, 128 * core, 128)[...] + cols(far, 128 * core, 128)[...].astype(F32)).astype(BF)
        g[:, 256:] = (cols(dkv, 256 + 128 * core, 128)[...]
                      + cols(far, 256 + 128 * core, 128)[...].astype(F32)).astype(BF)
        got = dot_nt(g[...], weight(i))
        part = got if part is None else part + got
        total = jnp.sum(g[...].astype(F32), axis=0, keepdims=True)
        cols(sum_ref, 128 * core, 128)[0:1, :] = total[:, :128]
        cols(sum_ref, 256 + 128 * core, 128)[0:1, :] = total[:, 256:]
    part = part.astype(BF)
    for j, out in enumerate((p0, p1, p2, p3)):
        out[:BLOCK, :] = part[BLOCK * j:BLOCK * (j + 1), :]
        if lasts:
            out[BLOCK:, :] = lasts[j][...]


def mlp_grad_kernel(ids, normed, du, g, dz, mine_ref, other_ref, mark):
    mark[...] = jnp.zeros_like(mark)
    c = ids[1]
    for at, left, right in ((0, normed, du), (512, g, dz)):
        turned = left[...].T
        for i, out in enumerate((mine_ref, other_ref)):
            core = c if i == 0 else 1 - c
            out[:, at:at + 512] = dot(turned, cols(right, 512 * core, 512)[...]).astype(BF)


def out_grad_kernel(ids, mixed, z0, z1, z2, z3, mine_ref, other_ref, mark):
    mark[...] = jnp.zeros_like(mark)
    x, c = ids[0], ids[1]
    turned = mixed[...].T
    for i, out in enumerate((mine_ref, other_ref)):
        core = c if i == 0 else 1 - c
        dmb = jnp.concatenate([cols(z, 256 * x + 128 * core, 128)[:BLOCK, :] for z in (z0, z1, z2, z3)], axis=0)
        out[...] = dot(turned, dmb).astype(BF)


def qkv_grad_kernel(a, gm, go, h, p0, p1, p2, p3, mine_ref, other_ref, sum_ref):
    turned = a[...].T
    mine_ref[...] = dot(turned, gm[...]).astype(BF)
    other_ref[...] = dot(turned, go[...]).astype(BF)
    gain = jnp.zeros((16, D), F32)
    shift = jnp.zeros((16, D), F32)
    for j, p in enumerate((p0, p1, p2, p3)):
        for r in range(0, BLOCK, 16):
            e = p[r:r + 16, :].astype(F32)
            gain = gain + e * norm_parts(h[BLOCK * j + r:BLOCK * j + r + 16, :])[0]
            shift = shift + e
    out = [jnp.sum(t, axis=0, keepdims=True) for t in (gain, shift)]
    sum_ref[...] = jnp.concatenate(out * 4, axis=0)


def add_kernel(*refs):
    out, mark, at = refs[-2], refs[-1], 0
    mark[...] = jnp.zeros_like(mark)
    for mine, came in zip(refs[:-2:2], refs[1:-2:2]):
        width = mine.shape[1]
        out[:, at:at + width] = (mine[...].astype(F32) + came[...].astype(F32)).astype(BF)
        at += width


def total_kernel(got, more, out):
    total = got[0].astype(F32)
    for d in range(1, 16):
        total = total + got[d].astype(F32)
    width = got.shape[2]
    out[:, :width] = total.astype(BF)
    out[:, width:] = more[...]


def write_gradient(name, layer, ref, all_ref, at):
    for core in range(2):
        if name == "up":
            for d in range(8):
                to = 256 * (8 * core + d)
                ref[layer, :, to:to + 256] = jnp.concatenate(
                    [all_ref[chip, core, :, at + 64 * d:at + 64 * (d + 1)] for chip in range(4)], axis=1).astype(F32)
        for chip in range(4):
            to = 256 * chip + 128 * core
            block = lambda i, width: all_ref[chip, core, :, at + i:at + i + width].astype(F32)
            if name == "down":
                ref[layer, 64 * chip:64 * (chip + 1), 512 * core:512 * (core + 1)] = block(0, 512)
            if name == "out":
                ref[layer, :, to:to + 128] = block(0, 128)
            if name == "qkv":
                for m in range(3):
                    ref[layer, :, D * m + to:D * m + to + 128] = block(128 * m, 128)


def arrange(ids, blocks, all_ref, at):
    x, c = ids[0], ids[1]
    for i in range(2):
        for j in range(4):
            all_ref[lax.rem(x + j, 4), c if i == 0 else 1 - c] = blocks[4 * i + j][at:, :]


def early_kernel(ids, counts, *refs):
    blocks, (tokens_ref, output_ref, up, down), all_ref = refs[:8], refs[8:12], refs[12]
    x, c = ids[0], ids[1]
    ranks = jnp.concatenate([half_ranks((1, ROWS), 1, x, core) for core in (c, 1 - c)], axis=1)
    put = jnp.where(slot_ranks((128, 1), 0, counts, 2 * x + c) == ranks, 1.0, 0.0).astype(BF)
    for i, ref in enumerate((tokens_ref, output_ref)):
        rows = jnp.concatenate([t[BLOCK * i:BLOCK * (i + 1), :] for t in blocks], axis=0)
        ref[0] = dot(put, rows).astype(BF)
    arrange(ids, blocks, all_ref, 2 * BLOCK)
    write_gradient("up", 0, up, all_ref, 0)
    write_gradient("down", 0, down, all_ref, 512)


def late_kernel(ids, *refs):
    blocks = refs[:8]
    (out, qkv, gain_ref, shift_ref, branch_ref, qv_ref, up_ref, up, down), all_ref = refs[-10:-1], refs[-1]
    arrange(ids, blocks, all_ref, 0)
    for name, layer, ref, at in (("out", 0, out, 0), ("qkv", 0, qkv, 128), ("up", 0, up, 640), ("down", 0, down, 1152),
                                 ("out", 1, out, 1664), ("qkv", 1, qkv, 1792)):
        write_gradient(name, layer, ref, all_ref, at)
    part = [sum(all_ref[chip, core, 0:16, 512:640].astype(F32) for core in range(2)) for chip in range(4)]
    total = part[0] + part[1] + part[2] + part[3]
    for l in range(2):
        for i, small in enumerate((gain_ref, shift_ref, branch_ref)):
            row = total[5 * l + i:5 * l + i + 1]
            small[l] = jnp.concatenate([row[:, :64], row[:, 64:]], axis=0)
        qv_ref[l:l + 1, :] = total[5 * l + 4:5 * l + 5]
        up_ref[l:l + 1, :] = jnp.concatenate([p[5 * l + 3:5 * l + 4, :64] for p in part], axis=1)


def finish(kernel, ids, blocks, outs, width, before=(), at=0, first=()):
    once = pl.Buffered(1)
    whole = lambda s: pl.BlockSpec(s, functools.partial(lambda n, _: (0,) * n, len(s)), pipeline_mode=once)
    out_specs = [whole(s) if n is None else pl.BlockSpec((n,) + s[1:], functools.partial(lambda at, _: (at, 0, 0), at),
                                                         pipeline_mode=once) for s, _, n, at in outs]
    n = 1 + len(first) + len(blocks)
    return pl.pallas_call(
        kernel,
        grid=(1,),
        in_specs=[pl.BlockSpec(memory_space=pltpu.SMEM)] * (1 + len(first)) + [whole(b.shape) for b in blocks]
        + [pl.BlockSpec(memory_space=pl.ANY)] * len(before),
        out_specs=out_specs,
        out_shape=[pltpu.HBM(s, t) for s, t, _, _ in outs],
        scratch_shapes=[pltpu.VMEM((4, 2, 64, width), BF)],
        input_output_aliases={n + i: at + i for i in range(len(before))},
        compiler_params=pltpu.CompilerParams(vmem_limit_bytes=LIMIT << 20),
        cost_estimate=pl.CostEstimate(flops=int(4e9), bytes_accessed=1, transcendentals=0),
    )(ids, *first, *blocks, *before)


def rest_kernel(ids, out_mine, out_came, qkv_mine, qkv_came, *refs):
    x, out = ids[0], refs[-1]
    for d in range(16):
        at = slice(64 * d, 64 * (d + 1))
        out[d, :, :128] = (out_mine[at, :].astype(F32) + out_came[at, :].astype(F32)).astype(BF)
        out[d, :, 128:512] = (qkv_mine[at, :].astype(F32) + qkv_came[at, :].astype(F32)).astype(BF)
        rows = []
        for l in range(2):
            one, zero, up, qv = refs[4 * l:4 * l + 4]
            pair = lambda u, v: jnp.concatenate([u, v], axis=1)
            rows += [pair(zero[0:1, at], one[0:1, at]), pair(zero[1:2, at], one[1:2, at]),
                     pair(one[2:3, at], one[3:4, at]), pair(up[0:1, at], jnp.zeros((1, 64), F32))]
            lanes = 256 * (d // 8) + 128 * (d % 2)
            rows.append(jnp.where(x == d % 8 // 2, qv[0:1, lanes:lanes + 128], 0.0))
        out[d, :, 512:] = jnp.concatenate(rows + [jnp.zeros((54, 128), F32)], axis=0).astype(BF)


def later(v, *others):
    return lax.optimization_barrier((v, *others))


def over_dp(v):
    return lax.all_to_all(v, "dp", split_axis=0, concat_axis=0, tiled=True)


def shards(tokens, counts, cotangent, w_qkv, w_out, w_up, w_down, norm_gain, norm_shift,
           bias_qv, bias_up, bias_branch):
    s, dp = lax.axis_index("seq"), lax.axis_index("dp")
    ids = jnp.stack([s // 2, s % 2, dp % 4, dp // 4]).astype(jnp.int32)

    def compact(blocks):
        own, give = run(pick_kernel, [((ROWS, D), BF)] * 2, ids, counts, *blocks)
        return own, core_swap(give)

    token_blocks = x_gather(tokens[0])
    first, rest0, rest1 = run(
        pack_kernel, [((64, 512), BF), ((64, 1920), BF), ((64, 1536), BF)], ids,
        away(w_qkv), away(w_out), away(w_up), away(w_down), away(norm_gain), away(norm_shift), away(bias_branch),
        away(bias_qv), away(bias_up),
        scratch=[pltpu.VMEM((64, 384), BF), pltpu.VMEM((2, 8, 64, 128), BF), pltpu.VMEM((3, 2, 2, 64), BF),
                 pltpu.VMEM((2, 128), BF), pltpu.VMEM((2, 256), BF), pltpu.SemaphoreType.DMA((31,))])
    rest0 = lax.all_gather(rest0, "dp", axis=0, tiled=True)
    rest1 = lax.all_gather(rest1, "dp", axis=0, tiled=True)
    source = list(compact(token_blocks))
    first, = run(order_kernel, [((4, 64, 512), BF)], ids, *dp_gather(first, 1), after=[source[0]])
    first, vec, qkv_bias, up_bias = run(
        unpack_kernel, [((D, 512), BF), ((16, D), F32), ((8, 384), F32), ((8, 512), F32)], ids, *dp_gather(first, 4),
        scratch=[pltpu.VMEM((16, 64, 512), BF)])
    first_far = core_swap(first)

    own, far = compact(x_gather(cotangent[0]))
    dz, dh, mark = run(join_kernel, in_hbm([((ROWS, D), BF), ((BLOCK, D), F32)]) + [MARK], own, far)
    dh = saved(dh)

    full = lambda *dtypes: [((ROWS, D), t) for t in dtypes]
    sent = [((BLOCK, D), BF)] * 4
    kept = []
    for l in range(2):
        outs = in_hbm(full(F32, BF)) if l else full(F32, BF)
        outs += [((ROWS, 256), BF), ((ROWS, 512), BF)]
        if l == 0:
            hidden, a, q, kv = run(functools.partial(qkv_kernel, l), outs, ids, vec, qkv_bias, *source, first, first_far,
                                   after=[mark], us=2)
        else:
            hidden, a, q, kv = run(functools.partial(qkv_kernel, l), outs, ids, vec, qkv_bias, *source, *rests[0],
                                   scratch=held(2, D, 384), after=[mark], us=3)
        kv_far = core_swap(kv)
        outs = [((ROWS, 256), BF), ((ROWS, 128), F32)]
        if l == 0:
            mixed, lse, q, kv, hidden, a, first, first_far = run(
                attend_kernel, outs + [(s, t, "away") for s, t in (
                    ((ROWS, 256), BF), ((2 * ROWS, 512), BF), ((ROWS, D), F32), ((ROWS, D), BF), ((D, 512), BF), ((D, 512), BF))],
                ids, q, kv, kv_far, hidden, a, first, first_far, scratch=[pltpu.SemaphoreType.DMA((7,))], us=4)
            rest0, lse = later(rest0, lse)
            rests = [[away(rest0), ("any", core_swap(rest0))]]
            hidden, a, q, kvs, lse = saved(hidden), saved(a), saved(q), [saved(kv)], saved(lse)
        else:
            mixed, lse = run(attend_kernel, outs, ids, q, kv, kv_far, us=3)
            kvs = [kv, kv_far]
            rest1, lse = later(rest1, lse)
            rests.append([away(rest1), ("any", core_swap(rest1))])
        mixes = x_gather(mixed)
        parts = [(rests[l][0][1], (3, D, 512), lanes_of(512, 0, 1024))]
        if l == 0:
            near, = load(ids, parts)
        else:
            near, a, hidden = load(ids, parts + [(a, (ROWS, D), None), (hidden, (ROWS, D), None)])
        room = held(3, D, 512)
        all_mixed, normed, middle, g, slope, *parts = run(
            functools.partial(mlp_kernel, l), full(BF, BF, F32, BF, BF) + sent + ([((3, D, 512), BF)] if l else []),
            ids, vec, up_bias, *mixes, hidden, near, rests[l][1],
            scratch=[pltpu.VMEM((ROWS, 512), F32)] + (room[1:] if l else room), us=6)
        if l:
            *parts, near_far = parts
            near = [near, near_far]
        if l == 0:
            mlp, mark = run(sum_kernel, [((BLOCK, D), BF), LOOSE], *x_scatter(parts))
            source = [middle, *x_gather(mlp)]
            *stored, mark = store([(all_mixed, ROWS), (normed, ROWS), (middle, BLOCK), (g, ROWS), (slope, ROWS)], [mark])
            all_mixed, normed, middle, g, slope = map(saved, stored)
        kept.append([hidden, a, q, kvs, lse, all_mixed, normed, middle, g, slope])

    dz = [(saved(dz), (BLOCK, D), (j, 0)) for j in range(4)]
    swapped = lambda v: v + [core_swap(b) for b in v]
    last_parts, last_rows = parts, (saved(middle), (BLOCK, D), (0, 0))
    rests[0][1] = away(rests[0][1][1])
    keep = lambda v: v if isinstance(v, tuple) else saved(v)
    tiny = []
    for l in (1, 0):
        hidden, a, q, kvs, lse, all_mixed, normed, middle, g, slope = kept[l]
        qkv = rests[0] if l else [away(first), away(first_far)]
        if l == 0:
            weights0 = lanes_of(0, 1024)
            *near, slope, normed, g = load(ids, [(rests[0][0][1], (2, D, 512), weights0), (rests[0][1][1], (2, D, 512), weights0),
                                        (slope[1], (ROWS, D), None), (normed[1], (ROWS, D), None),
                                        (g[1], (ROWS, D), None)], after=[mark_add, dh])
        top = lambda v: (v, (BLOCK, D), (0, 0))
        dz_all, du, up_sum, *parts = run(
            mlp_back_kernel, full(BF, BF) + [((8, D), F32)] + sent, ids, *dz, slope, *near,
            after=[mark_add] if l == 0 else (), us=4)
        errs = x_scatter(parts)
        mlp_mine, mlp_other, sums_grad = run(mlp_grad_kernel, [((D, D), BF)] * 2 + [LOOSE], ids, normed, du, g, dz_all, us=4)
        dm, dmb, sums1 = run(functools.partial(norm_back_kernel, 2 * l + 1),
                             [((BLOCK, D), F32), ((BLOCK, D), BF), ((8, D), F32)], vec, top(middle), dh,
                             errs[0] if l else saved(errs[0]), *errs[1:],
                             after=[sums_grad], us=1 if l else 8)
        mlp_came = core_swap(mlp_other)
        dmbs = x_gather(dmb)
        if l == 0:
            rows = lambda ids: [(pl.ds(pl.multiple_of(256 * ids[0], 256), 256), pl.ds(512, 512))]
            q, lse, kvs, w_near, w_far, *near = load(ids, [
                (q[1], (ROWS, 256), None), (lse[1], (ROWS, 128), None), (kvs[0][1], (2 * ROWS, 512), None),
                (first, (1, D, 384), lanes_of(0, width=384)), (first_far, (1, D, 384), lanes_of(0, width=384)),
                (rests[0][0][1], (1, 256, 512), rows), (rests[0][1][1], (1, 256, 512), rows)], after=[dm])
            kvs, qkv = [kvs], [w_near, w_far]
        before = []
        if l == 0:
            shares, mark = run(add_kernel, [((D, D), BF, "saved"), LOOSE], mlp_mine, mlp_came, us=3)
            got_mlp = over_dp(shares.reshape(16, 64, D))
            before = [mark]
        dmb_all, dq, dkv, give = run(
            attend_back_kernel, full(BF) + [((ROWS, 256), BF), ((ROWS, 512), F32), ((ROWS, 512), BF)],
            ids, *dmbs, *near, q, lse, *kvs, after=before, us=5 if l else 0.1)
        give = core_swap(give)
        out_mine, out_other, mark_out = run(out_grad_kernel, [((D, 128), BF)] * 2 + [LOOSE], ids, all_mixed, *dmbs, us=2 if l else 0.1)
        out_came = core_swap(out_other)
        high = BLOCK * (2 - l)
        gm, go, qv_sum, *parts = run(
            functools.partial(qkv_back_kernel, 1536 if l else None),
            [((ROWS, 384), BF)] * 2 + [((8, 512), F32)] + [((high, D), BF)] * 4,
            ids, dq, dkv, give, *qkv, *([] if l else map(keep, last_parts)), scratch=held(2, D, 384) if l else (), after=[mark_out], us=3 if l else 0.1)
        errs = x_scatter(parts)
        qkv_mine, qkv_other, sums0 = run(qkv_grad_kernel, [((D, 384), BF)] * 2 + [((8, D), F32)],
                                         a, gm, go, hidden, *parts, us=4 if l else 0.1)
        tiny = [sums1, sums0, up_sum, qv_sum] + tiny
        qkv_came = core_swap(qkv_other)
        qkv_pair = [qkv_mine, qkv_came]
        if l == 1:
            shares, mark_add = run(add_kernel, [((D, 1536), BF, "saved"), LOOSE], mlp_mine, mlp_came,
                                   out_mine, out_came, *qkv_pair, us=4)
            got1 = lax.psum_scatter(shares, "dp", scatter_dimension=0, tiled=True)
        else:
            rest, = run(rest_kernel, in_hbm([((16, 64, 640), BF)]), ids, out_mine, out_came, *qkv_pair, *tiny, us=0.1)
            got_rest = over_dp(rest)
        if l == 1:
            dh, dz = run(functools.partial(norm_back_kernel, 2), [((BLOCK, D), F32), ((BLOCK, D), BF)],
                         vec, top(hidden), dm, *errs, after=[mark_add])
            dz = x_gather(dz)
        else:
            dz, = run(functools.partial(norm_back_kernel, 0), [((2 * BLOCK + 64, D), BF)],
                      vec, top(hidden), saved(dm), saved(errs[0]), *errs[1:], last_rows, got_mlp, after=[rest], us=2)
    grad_tokens, output, g_up, g_down = finish(
        early_kernel, ids, swapped(x_gather(dz)),
        [((1, 128, D), BF, None, 0)] * 2 + [((2, 64, 4096), F32, 1, 0), ((2, 256, 1024), F32, 1, 0)], D, first=[counts])
    total_rest, = run(total_kernel, [((64, 2176), BF)], got_rest, saved(got1))
    g_out, g_qkv, g_gain, g_shift, g_branch, g_qv, g_upb, g_up, g_down = finish(
        late_kernel, ids, swapped(x_gather(total_rest)),
        [((2, 64, 1024), F32, 2, 0), ((2, 64, 3072), F32, 2, 0)] + [((2, 2, 64), F32, None, 0)] * 3
        + [((2, 128), F32, None, 0), ((2, 256), F32, None, 0), ((2, 64, 4096), F32, 1, 1), ((2, 256, 1024), F32, 1, 1)],
        2176, before=(g_up, g_down), at=7)
    return (output, grad_tokens, g_qkv, g_out, g_up, g_down, g_gain, g_shift, g_qv, g_upb, g_branch)


def solution(mesh):
    rows = P("dp", "seq", None)
    mid = P(None, "dp", None)
    end = P(None, None, "dp")
    two = P(None, "dp")
    return jax.shard_map(
        shards,
        mesh=mesh,
        in_specs=(rows, P("dp", None), rows, mid, mid, mid, mid, end, end, two, two, end),
        out_specs=(rows, rows, mid, mid, mid, mid, end, end, two, two, end),
        check_vma=False,
    )
```
